32 devices in a mesh: section: 4 (over x, core), px: 4 (over z), py: 2 (over y).
Axes of the slice: x: 2, y: 2, z: 4, core: 2. Of those that a mesh axis runs over, the one named last changes fastest.
Arguments:
- psi: float32 [2, 32, 512, 256], P(None, None, 'px', 'py'), may hold values from -3.5 to 3.5
- disorder: int32 [32, 512, 256], P(None, 'px', 'py'), may hold values from 0 to 15
Outputs:
- psi_next: float32 [2, 32, 512, 256], P(None, 'section', 'px', 'py')
The draws below stay inside these ranges and needn't reach their ends.
All inputs are finite; a program needn't handle non-finite values.
Results may differ from the reference program's by a relative error of at most 0.00005.
Values sent between devices are 32-bit elements; how exact they have to be, the bound alone decides.
No kernel may reach another device: no remote copies, remote signals or barrier semaphores. Data moves between devices by JAX's collectives and lax.ppermute only.
A program may use at most 128 MiB of HBM per device.

```python
import math
import jax
import jax.numpy as jnp

NZ = 32
SECTIONS = 4
ITERS = 2
LEVELS = 16
NX = 512
NY = 256


def draw_psi(key, part):
    key = jax.random.fold_in(key, 11)
    sign_key, size_key = jax.random.split(key)
    shape = (2, NZ, NX, NY)
    flips = jax.random.bernoulli(sign_key, 0.5, shape)
    sign_flip = jnp.where(flips, 1.0, -1.0).astype(jnp.float32)
    low_end = 2.5
    magnitude = jax.random.uniform(size_key, shape, jnp.float32, low_end, 3.5)
    return (sign_flip * magnitude).astype(jnp.float32)


def plant(entries, key, smallest, largest):
    longest = entries.shape.index(max(entries.shape))
    spots = []
    for shift in (0, 1):
        where = [jax.random.randint(jax.random.fold_in(key, axis), (), 0, length) for axis, length in enumerate(entries.shape)]
        where[longest] = (where[longest] + shift) % entries.shape[longest]
        spots.append(tuple(where))
    return entries.at[spots[0]].set(smallest).at[spots[1]].set(largest)


def setup_inputs(seed: int = 0) -> dict:
    key_of = jax.random.split(jax.random.key(seed), 3)
    return {
        "psi": draw_psi(jax.random.fold_in(key_of[2], 71), 0),
        "disorder": plant(jax.random.randint(key_of[1], (NZ, NX, NY), 0, LEVELS), jax.random.fold_in(key_of[1], 1), 0, LEVELS - 1).astype(jnp.int32),
    }


time_step = 0.05
rotation_rate = 0.8
coupling = 0.25

def poly_integral(coeffs, point):
    total = 0.0
    for power in range(len(coeffs)):
        total = total + coeffs[power] * point ** (power + 1) / (power + 1)
    return total

def gauss_table():
    outer = math.sqrt((3.0 + 2.0 * math.sqrt(1.2)) / 7.0)
    inner = math.sqrt((3.0 - 2.0 * math.sqrt(1.2)) / 7.0)
    points = [(1.0 - outer) / 2.0, (1.0 - inner) / 2.0, (1.0 + inner) / 2.0, (1.0 + outer) / 2.0]
    matrix = [[0.0] * 4 for row_idx in range(4)]
    weights = [0.0] * 4
    for j in range(4):
        coeffs = [1.0]
        for m in range(4):
            if m != j:
                factor = 1.0 / (points[j] - points[m])
                longer = [0.0] * (len(coeffs) + 1)
                for power in range(len(coeffs)):
                    longer[power + 1] = longer[power + 1] + coeffs[power] * factor
                    longer[power] = longer[power] - points[m] * coeffs[power] * factor
                coeffs = longer
        for i in range(4):
            matrix[i][j] = poly_integral(coeffs, points[i])
        weights[j] = poly_integral(coeffs, 1.0)
    return (matrix, weights)

def slope(padded, potential, xs, ys):
    center = padded[..., 1:-1, 1:-1, 1:-1]
    laplace = padded[..., 2:, 1:-1, 1:-1] + padded[..., :-2, 1:-1, 1:-1] + padded[..., 1:-1, 2:, 1:-1] + padded[..., 1:-1, :-2, 1:-1] + padded[..., 1:-1, 1:-1, 2:] + padded[..., 1:-1, 1:-1, :-2] - 6.0 * center
    grad_x = 0.5 * (padded[..., 1:-1, 2:, 1:-1] - padded[..., 1:-1, :-2, 1:-1])
    grad_y = 0.5 * (padded[..., 1:-1, 1:-1, 2:] - padded[..., 1:-1, 1:-1, :-2])
    rotation = xs[:, None] * grad_y - ys[None, :] * grad_x
    real_part = center[..., 0, :, :, :]
    imag_part = center[..., 1, :, :, :]
    weight_pot = potential + coupling * (real_part * real_part + imag_part * imag_part)
    new_real = -0.5 * laplace[..., 0, :, :, :] + weight_pot * imag_part + rotation_rate * rotation[..., 0, :, :, :]
    new_imag = 0.5 * laplace[..., 1, :, :, :] - weight_pot * real_part + rotation_rate * rotation[..., 1, :, :, :]
    return jnp.stack([new_real, new_imag], axis=-4)

def coords(count):
    return (jnp.arange(count, dtype=jnp.float32) - (count - 1) / 2.0) / (count / 2.0)

def reference(psi, disorder):
    xs = coords(NX)
    ys = coords(NY)
    zs = coords(NZ)
    levels = jnp.arange(LEVELS, dtype=jnp.float32)
    table = 1.5 * jnp.sin(2.3 * levels + 0.4)
    trap = zs[:, None, None] ** 2 + xs[None, :, None] ** 2 + ys[None, None, :] ** 2
    potential = trap + jnp.take(table, disorder, axis=0)
    matrix, weights = gauss_table()

    def evaluate(field):
        return slope(jnp.pad(field, ((0, 0), (1, 1), (1, 1), (1, 1))), potential, xs, ys)
    first = evaluate(psi)
    slopes = [first] * SECTIONS
    for sweep in range(ITERS):
        sections_new = []
        for i in range(SECTIONS):
            accum = psi
            for j in range(SECTIONS):
                accum = accum + time_step * matrix[i][j] * slopes[j]
            sections_new.append(evaluate(accum))
        slopes = sections_new
    total = jnp.zeros_like(psi)
    for i in range(SECTIONS):
        total = total + time_step * weights[i] * slopes[i]
    return psi + total
```

```python
import functools
import math

import jax
import jax.numpy as jnp
from jax import lax
from jax.experimental import pallas as pl
from jax.experimental.pallas import tpu as pltpu
from jax.sharding import PartitionSpec as P

LEVELS = 16
STEP = 0.05
ROTATION = 0.8
COUPLING = 0.25

ROOT_OUT = math.sqrt((3.0 + 2.0 * math.sqrt(1.2)) / 7.0)
ROOT_IN = math.sqrt((3.0 - 2.0 * math.sqrt(1.2)) / 7.0)
PAIRS = (
    (0.25 * ROOT_OUT * ROOT_OUT, (18.0 - math.sqrt(30.0)) / 36.0),
    (0.25 * ROOT_IN * ROOT_IN, (18.0 + math.sqrt(30.0)) / 36.0),
)
KAPPA = STEP * COUPLING
HALF = 0.5 * STEP
SPIN = 0.5 * STEP * ROTATION

DEEP = 3
LANES = 128
ROWS = 8
F32 = jnp.float32


def iota(dim):
    return lax.broadcasted_iota(jnp.int32, (ROWS, LANES), dim)


def roll(value, shift, axis):
    return pltpu.roll(value, shift % value.shape[axis] if isinstance(shift, int) else shift, axis)


def level_table():
    lane = iota(1)
    table = jnp.zeros((ROWS, LANES), F32)
    for level in range(LEVELS):
        table = jnp.where(lane == level, F32(STEP * 1.5 * math.sin(2.3 * level + 0.4)), table)
    return table


def look_up(table, level):
    return jnp.take_along_axis(table, level, axis=1, mode="promise_in_bounds")


def linear(c, xp, xm, yp, ym, zp, zm, cx, cy):
    diag = [HALF * (zp[i] + zm[i]) - (6.0 * HALF) * c[i] for i in range(2)]
    real = cx[1] * yp[0] - cx[0] * ym[0] - cy[0] * xp[0] + cy[1] * xm[0] - diag[0]
    imag = cx[0] * yp[1] - cx[1] * ym[1] - cy[1] * xp[1] + cy[0] * xm[1] + diag[1]
    return real, imag


def first_slope(w, lin, pot):
    g = pot + KAPPA * (w[0] * w[0] + w[1] * w[1])
    return lin[0] + g * w[1], lin[1] - g * w[0]


def second_stage(w, k, lin_w, lin_k, pot, full):
    m = [w[i] + 0.5 * k[i] for i in range(2)]
    p0 = pot + KAPPA * (m[0] * m[0] + m[1] * m[1])
    p1 = (2.0 * KAPPA) * (m[0] * k[0] + m[1] * k[1])
    p2 = KAPPA * (k[0] * k[0] + k[1] * k[1])
    n0 = [p0 * m[i] for i in range(2)]
    n1 = [p0 * k[i] + p1 * m[i] for i in range(2)]
    n2 = [p1 * k[i] + p2 * m[i] for i in range(2)]
    n3 = [p2 * k[i] for i in range(2)]
    turn = lambda n: (n[1], -n[0])
    f0 = [lin_w[i] + 0.5 * lin_k[i] + turn(n0)[i] for i in range(2)]
    f1 = [lin_k[i] + turn(n1)[i] for i in range(2)]
    f2 = turn(n2)
    f3 = turn(n3)
    base = [w[i] + 0.5 * f0[i] + (1.0 / 24.0) * f2[i] for i in range(2)]
    z = [base[i] - (1.0 / 12.0) * f1[i] - (1.0 / 80.0) * f3[i] for i in range(2)]
    if not full:
        return z, None
    total = [pot * z[i] for i in range(2)]
    for sq, weight in PAIRS:
        even = [base[i] + (0.5 * sq - 0.125) * f1[i] + (0.25 * sq * sq - 1.0 / 64.0) * f3[i] for i in range(2)]
        odd = [f0[i] + (sq / 3.0) * f2[i] for i in range(2)]
        scale = weight * KAPPA
        p = scale * (even[0] * even[0] + even[1] * even[1]) + (scale * sq) * (odd[0] * odd[0] + odd[1] * odd[1])
        q = (2.0 * scale * sq) * (even[0] * odd[0] + even[1] * odd[1])
        total = [total[i] + p * even[i] + q * odd[i] for i in range(2)]
    return z, (w[0] + total[1], w[1] - total[0])


def pack_kernel(dims, psi, dis, *refs):
    planes, share, two, npy = dims
    n_sides = 1 if two else 2
    xup, xdn = refs[0], refs[1]
    ymsg = refs[2 : 2 + n_sides]
    corner = refs[2 + n_sides : 2 + 3 * n_sides]
    vpsi, vdis, psem, dsem = refs[2 + 3 * n_sides :]
    slots = share + 2 * DEEP
    z0 = lax.axis_index("section") * share - DEEP
    py = lax.axis_index("py")
    rows = psi.shape[2]
    tiles = rows // ROWS

    def psi_copy(p):
        return pltpu.make_async_copy(psi.at[:, z0 + p], vpsi.at[:, p - 1], psem.at[p])

    def dis_copy(p):
        return pltpu.make_async_copy(dis.at[z0 + p], vdis.at[p - 2], dsem.at[p])

    def valid(p):
        return (z0 + p >= 0) & (z0 + p < planes)

    for p in range(1, slots - 1):
        @pl.when(valid(p))
        def _():
            psi_copy(p).start()

        @pl.when(jnp.logical_not(valid(p)))
        def _():
            vpsi[:, p - 1] = jnp.zeros(vpsi.shape[:1] + vpsi.shape[2:], F32)

        if 2 <= p < slots - 2:
            @pl.when(valid(p))
            def _():
                dis_copy(p).start()

            @pl.when(jnp.logical_not(valid(p)))
            def _():
                vdis[p - 2] = jnp.zeros(vdis.shape[1:], jnp.int32)

    for p in range(1, slots - 1):
        @pl.when(valid(p))
        def _():
            psi_copy(p).wait()

        if 2 <= p < slots - 2:
            @pl.when(valid(p))
            def _():
                dis_copy(p).wait()

    sub = iota(0)
    lane = iota(1)
    off = lane % 8
    slot = lane // 8

    def dis_tile(p, base):
        if 2 <= p < slots - 2:
            return vdis[p - 2, pl.ds(base, ROWS), :].astype(F32)
        return jnp.zeros((ROWS, LANES), F32)

    for p in range(1, slots - 1):
        last, first = rows - ROWS, 0
        xup[p - 1] = jnp.where(
            sub >= 5,
            vpsi[0, p - 1, last:, :],
            jnp.where(sub >= 2, roll(vpsi[1, p - 1, last:, :], -3, 0), roll(dis_tile(p, last), 2, 0)),
        )
        xdn[p - 1] = jnp.where(
            sub < 3,
            vpsi[0, p - 1, :ROWS, :],
            jnp.where(sub < 6, roll(vpsi[1, p - 1, :ROWS, :], 3, 0), roll(dis_tile(p, first), -2, 0)),
        )

    for side in range(n_sides):
        if two:
            upper = py == 0
            low = jnp.where(upper, off, (off + 5) % 8)
            start_a = jnp.where(upper, 3, 3)
            start_b = jnp.where(upper, 6, 0)
            start_d = jnp.where(upper, 8, 6)
        else:
            upper = side == 1
            low = off if upper else (off + 5) % 8
            start_a = 3
            start_b = 6 if upper else 0
            start_d = 8 if upper else 6
        is_a = low < 3
        is_d = off >= 6

        def tile_body(j, carry):
            base = pl.multiple_of(j * ROWS, ROWS)
            acc = jnp.zeros((ROWS, LANES), F32)
            for p in range(1, slots - 1):
                a = roll(vpsi[0, p - 1, pl.ds(base, ROWS), :], (start_a + 8 * p) % LANES, 1)
                b = roll(vpsi[1, p - 1, pl.ds(base, ROWS), :], (start_b + 8 * p) % LANES, 1)
                t = jnp.where(is_a, a, b)
                if 2 <= p < slots - 2:
                    t = jnp.where(is_d, roll(dis_tile(p, base), (start_d + 8 * p) % LANES, 1), t)
                acc = jnp.where(slot == p, t, acc)
            ymsg[side][pl.ds(base, ROWS), :] = acc
            return carry

        lax.fori_loop(0, tiles, tile_body, 0)
        xup[slots - 2 + side] = ymsg[side][rows - ROWS :, :]
        xdn[slots - 2 + side] = ymsg[side][:ROWS, :]
        corner[2 * side][...] = ymsg[side][rows - ROWS :, :]
        corner[2 * side + 1][...] = ymsg[side][:ROWS, :]


def main_kernel(dims, psi, dis, *refs):
    planes, share, two, npx, npy = dims
    n_sides = 1 if two else 2
    refs = list(refs)
    take = lambda n: [refs.pop(0) for _ in range(n)]
    xup, xdn = take(2)
    own_y = take(n_sides)
    got_y = take(n_sides)
    got_up = take(n_sides)
    got_dn = take(n_sides)
    (out,) = take(1)
    w, d, k, lw, pot, zf, part, sw, sk, sl, sp, sz, cw, ck, cz, coef, dist, psem, dsem, osem = refs

    slots = share + 2 * DEEP
    z0 = lax.axis_index("section") * share - DEEP
    px = lax.axis_index("px")
    py = lax.axis_index("py")
    rows, cols = psi.shape[2], psi.shape[3]
    tiles = rows // ROWS
    low_row, end_row = ROWS, ROWS + rows
    whole_x, whole_y = rows * npx, cols * npy

    def psi_copy(p):
        return pltpu.make_async_copy(psi.at[:, z0 + p], w.at[:, p, pl.ds(low_row, rows)], psem.at[p])

    def dis_copy(p):
        return pltpu.make_async_copy(dis.at[z0 + p], d.at[p - 1, pl.ds(0, rows)], dsem.at[p])

    def out_copy(p):
        return pltpu.make_async_copy(part.at[:, p - DEEP], out.at[:, p - DEEP], osem.at[p - DEEP])

    def valid(p):
        return (z0 + p >= 0) & (z0 + p < planes)

    zero_plane = jnp.zeros((2, rows + 2 * ROWS, LANES), F32)
    for p in range(slots):
        @pl.when(valid(p))
        def _():
            psi_copy(p).start()

        @pl.when(jnp.logical_not(valid(p)))
        def _():
            w[:, p] = zero_plane

        if 1 <= p < slots - 1:
            @pl.when(valid(p))
            def _():
                dis_copy(p).start()

            @pl.when(jnp.logical_not(valid(p)))
            def _():
                k[:, p - 1] = zero_plane

        if 2 <= p < slots - 2:
            @pl.when(jnp.logical_not(valid(p)))
            def _():
                zf[:, p - 2] = zero_plane

    sub = iota(0)
    lane = iota(1)
    off = lane % 8
    slot = lane // 8
    table = level_table()
    zero = jnp.zeros((ROWS, LANES), F32)

    def xcoord(row):
        return ((px * rows + row).astype(F32) - (whole_x - 1) / 2.0) / (whole_x / 2.0)

    def ycoord(col):
        return ((py * cols + col).astype(F32) - (whole_y - 1) / 2.0) / (whole_y / 2.0)

    def zcoord(z):
        return (z.astype(F32) - (planes - 1) / 2.0) / (planes / 2.0)

    outer_row = jnp.where(sub >= 4, sub - ROWS, rows + sub)
    inside = lambda at, whole: (at >= 0) & (at < whole)
    row_ok = inside(px * rows + outer_row, whole_x)

    ys = ycoord(lane)
    cy = (SPIN * ys + HALF, SPIN * ys - HALF)
    for j in range(tiles + 1):
        xs = xcoord(outer_row if j == 0 else sub + (j - 1) * ROWS)
        coef[0, j * ROWS : (j + 1) * ROWS] = SPIN * xs + HALF
        coef[1, j * ROWS : (j + 1) * ROWS] = SPIN * xs - HALF
        dist[j * ROWS : (j + 1) * ROWS] = STEP * (xs * xs + ys * ys)

    def put(ref, lead, value, base):
        ref[lead + (pl.ds(base, ROWS), slice(None))] = value

    def get(ref, lead, base):
        return ref[lead + (pl.ds(base, ROWS), slice(None))]

    def tile_of(ref, lead, base):
        return [get(ref, (i,) + lead, base) for i in range(2)]

    def x_pair(ref, lead, base, outer):
        if outer:
            return tile_of(ref, lead, 1), tile_of(ref, lead, end_row - 1)
        return tile_of(ref, lead, base + 1), tile_of(ref, lead, base - 1)

    def put_field(ref, lead, values, base, outer):
        for i in range(2):
            put(ref, (i,) + lead, values[i], base)
            if outer:
                put(ref, (i,) + lead, values[i], end_row)

    def outer_body(p, carry):
        up, dn = xup[p - 1], xdn[p - 1]
        a = jnp.where(sub >= 4, up, dn)
        b = jnp.where(sub >= 4, roll(up, 3, 0), roll(dn, -3, 0))
        level = jnp.where(sub >= 4, roll(up, -2, 0), roll(dn, 2, 0))
        put_field(w, (p,), (a, b), 0, True)
        level = jnp.clip(level, 0.0, LEVELS - 1.0).astype(jnp.int32)
        d[p - 1, rows : rows + ROWS, :] = level
        return carry

    lax.fori_loop(1, slots - 1, outer_body, 0)
    for p in (0, slots - 1):
        put_field(w, (p,), (zero, zero), 0, True)

    zs = zcoord(z0 + slot)
    for side in range(n_sides):
        if two:
            is_left = py == npy - 1
            pick = lambda x, y: jnp.where(is_left, x, y)
            col = jnp.where(is_left, off - DEEP, off + cols - DEEP)
        else:
            pick = (lambda x, y: x) if side == 0 else (lambda x, y: y)
            col = off - DEEP if side == 0 else off + cols - DEEP
        ok = inside(z0 + slot, planes) & inside(py * cols + col, whole_y)
        ys_strip = ycoord(col)
        cy_strip = (SPIN * ys_strip + HALF, SPIN * ys_strip - HALF)
        far = STEP * (zs * zs + ys_strip * ys_strip)

        def strip_load(j, base, outer):
            if outer:
                got = jnp.where(sub >= 4, got_up[side][...], got_dn[side][...])
                own = jnp.where(sub >= 4, xup[slots - 2 + side], xdn[slots - 2 + side])
            else:
                at = pl.ds(base - ROWS, ROWS)
                got, own = got_y[side][at, :], own_y[side][at, :]
            lo, hi = pick(got, own), pick(own, got)
            a = jnp.where(off < 3, lo, hi)
            b = jnp.where(off < 3, roll(lo, -3, 1), roll(hi, 3, 1))
            level = jnp.where(off < 3, roll(lo, -5, 1), roll(hi, -3, 1))
            level = jnp.clip(level, 0.0, LEVELS - 1.0).astype(jnp.int32)
            put_field(sw, (side,), (a, b), base, outer)
            xs = (get(coef, (0,), base) - HALF) * (1.0 / SPIN)
            put(sp, (side,), look_up(table, level) + (far + STEP * (xs * xs)), base)

        def strip_linear(ref, base, outer):
            c = tile_of(ref, (side,), base)
            xp, xm = x_pair(ref, (side,), base, outer)
            rolled = [[roll(c[i], s, 1) for i in range(2)] for s in (-1, 1, -8, 8)]
            return c, linear(c, xp, xm, *rolled, tile_of(coef, (), base), cy_strip)

        def strip_one(j, base, outer):
            c, lin = strip_linear(sw, base, outer)
            slope = first_slope(c, lin, get(sp, (side,), base))
            good = (ok & row_ok) if outer else ok
            put_field(sk, (side,), [jnp.where(good, s, 0.0) for s in slope], base, outer)
            put_field(sl, (side,), lin, base, False)

        def strip_two(j, base, outer):
            c, lin = strip_linear(sk, base, outer)
            z, _ = second_stage(
                tile_of(sw, (side,), base), c, tile_of(sl, (side,), base), lin, get(sp, (side,), base), False
            )
            good = (ok & row_ok) if outer else ok
            put_field(sz, (side,), [jnp.where(good, s, 0.0) for s in z], base, outer)

        for step in (strip_load, strip_one, strip_two):
            step(0, 0, True)

            def body(j, carry):
                step(j, pl.multiple_of(j * ROWS, ROWS), False)
                return carry

            lax.fori_loop(1, tiles + 1, body, 0, unroll=2)

    def comb_body(j, carry):
        base = pl.multiple_of(j * ROWS, ROWS)
        for src, dst in ((sw, cw), (sk, ck), (sz, cz)):
            for i in range(2):
                if two:
                    at = jnp.where(py == npy - 1, 2, 3)
                    value = jnp.where(off == at, get(src, (i, 0), base), 0.0)
                else:
                    value = jnp.where(off == 2, get(src, (i, 0), base), get(src, (i, 1), base))
                put(dst, (i,), value, base)
        return carry

    lax.fori_loop(0, tiles + 1, comb_body, 0)

    first_lane = lane == 0
    last_lane = lane == cols - 1

    def field_linear(ref, comb, p, q, base, outer):
        c = tile_of(ref, (q,), base)
        xp, xm = x_pair(ref, (q,), base, outer)
        zp = tile_of(ref, (q + 1,), base)
        zm = tile_of(ref, (q - 1,), base)
        shift = cols - DEEP - 8 * p
        edge = [roll(get(comb, (i,), base), shift, 1) for i in range(2)]
        yp = [roll(jnp.where(first_lane, edge[i], c[i]), -1, 1) for i in range(2)]
        ym = [roll(jnp.where(last_lane, edge[i], c[i]), 1, 1) for i in range(2)]
        return c, linear(c, xp, xm, yp, ym, zp, zm, tile_of(coef, (), base), cy)

    def wait_plane(p):
        @pl.when(valid(p))
        def _():
            psi_copy(p).wait()

        if not isinstance(p, int):
            @pl.when(valid(p) & (p < slots - 1))
            def _():
                dis_copy(p).wait()

    wait_plane(0)
    wait_plane(jnp.int32(1))

    def one_body(p, carry):
        wait_plane(p + 1)
        zp = zcoord(z0 + p)
        level_at = table + STEP * (zp * zp)

        @pl.when(valid(p))
        def _():
            for j in range(tiles + 1):
                base, outer = j * ROWS, j == 0
                c, lin = field_linear(w, cw, p, p, base, outer)
                level = d[p - 1, pl.ds(base - ROWS if j else rows, ROWS), :]
                here = look_up(level_at, level) + get(dist, (), base)
                slope = first_slope(c, lin, here)
                if outer:
                    slope = [jnp.where(row_ok, s, 0.0) for s in slope]
                put_field(k, (p - 1,), slope, base, outer)
                put_field(lw, (p - 1,), lin, base, False)
                put(pot, (p - 1,), here, base)

        return carry

    lax.fori_loop(1, slots - 1, one_body, 0)

    def two_tile(p, j, full):
        base, outer = j * ROWS, j == 0
        c, lin = field_linear(k, ck, p, p - 1, base, outer)
        z, rest = second_stage(
            tile_of(w, (p,), base), c, tile_of(lw, (p - 1,), base), lin, get(pot, (p - 1,), base), full and not outer
        )
        if outer:
            z = [jnp.where(row_ok, s, 0.0) for s in z]
        put_field(zf, (p - 2,), z, base, outer)
        if rest is not None:
            for i in range(2):
                put(part, (i, p - DEEP), rest[i], base - ROWS)

    for p in (2, slots - 3):
        @pl.when(valid(p))
        def _():
            for j in range(tiles + 1):
                two_tile(p, j, False)

    def two_body(p, carry):
        for j in range(tiles + 1):
            two_tile(p, j, True)
        return carry

    lax.fori_loop(DEEP, DEEP + share, two_body, 0)

    def three_body(p, carry):
        for j in range(1, tiles + 1):
            base = j * ROWS
            _, lin = field_linear(zf, cz, p, p - 2, base, False)
            for i in range(2):
                at = (i, p - DEEP)
                put(part, at, get(part, at, base - ROWS) + lin[i], base - ROWS)
        out_copy(p).start()
        return carry

    lax.fori_loop(DEEP, DEEP + share, three_body, 0)
    for p in range(DEEP, DEEP + share):
        out_copy(p).wait()


def local(npx, npy, psi, disorder):
    planes, rows, cols = psi.shape[1:]
    share = planes // lax.axis_size("section")
    two = npy == 2
    n_sides = 1 if two else 2
    slots = share + 2 * DEEP
    any_space = pl.BlockSpec(memory_space=pl.ANY)
    vmem = pl.BlockSpec(memory_space=pltpu.VMEM)
    shape = jax.ShapeDtypeStruct
    x_tiles = slots - 2 + n_sides
    tile = shape((ROWS, LANES), F32)
    params = pltpu.CompilerParams(vmem_limit_bytes=40 * 1024 * 1024)

    packed = pl.pallas_call(
        functools.partial(pack_kernel, (planes, share, two, npy)),
        out_shape=[shape((x_tiles, ROWS, LANES), F32)] * 2 + [shape((rows, LANES), F32)] * n_sides + [tile] * (2 * n_sides),
        in_specs=[any_space] * 2,
        out_specs=[vmem] * (2 + 3 * n_sides),
        scratch_shapes=[
            pltpu.VMEM((2, slots - 2, rows, cols), F32),
            pltpu.VMEM((slots - 4, rows, cols), jnp.int32),
            pltpu.SemaphoreType.DMA((slots,)),
            pltpu.SemaphoreType.DMA((slots,)),
        ],
        compiler_params=params,
        name="pack",
    )(psi, disorder)
    xup, xdn = packed[:2]
    own_y = packed[2 : 2 + n_sides]
    corner = packed[2 + n_sides :]

    def send(value, dx, dy):
        pairs = []
        for i in range(npx):
            for j in range(npy):
                to_x, to_y = i + dx, (1 - j if two and dy else j + dy)
                if 0 <= to_x < npx and 0 <= to_y < npy:
                    pairs.append((i * npy + j, to_x * npy + to_y))
        return lax.ppermute(value, ("px", "py"), pairs)

    if two:
        got_y = [send(own_y[0], 0, 1)]
        got_up = [send(corner[0], 1, 1)]
        got_dn = [send(corner[1], -1, 1)]
    else:
        got_y = [send(own_y[1], 0, 1), send(own_y[0], 0, -1)]
        got_up = [send(corner[2], 1, 1), send(corner[0], 1, -1)]
        got_dn = [send(corner[3], -1, 1), send(corner[1], -1, -1)]
    got_xup = send(xup, 1, 0)
    got_xdn = send(xdn, -1, 0)

    field = lambda depth: pltpu.VMEM((2, depth, rows + 2 * ROWS, LANES), F32)
    scalar = lambda depth: pltpu.VMEM((depth, rows + ROWS, LANES), F32)
    comb = pltpu.VMEM((2, rows + ROWS, LANES), F32)
    flat = pltpu.VMEM((rows + ROWS, LANES), F32)
    return pl.pallas_call(
        functools.partial(main_kernel, (planes, share, two, npx, npy)),
        out_shape=shape((2, share, rows, cols), F32),
        in_specs=[any_space] * 2 + [vmem] * (2 + 4 * n_sides),
        out_specs=any_space,
        scratch_shapes=[
            field(slots),
            pltpu.VMEM((slots - 2, rows + ROWS, LANES), jnp.int32),
            field(slots - 2),
            field(slots - 2),
            scalar(slots - 2),
            field(slots - 4),
            pltpu.VMEM((2, share, rows, cols), F32),
            field(n_sides),
            field(n_sides),
            field(n_sides),
            scalar(n_sides),
            field(n_sides),
            comb,
            comb,
            comb,
            comb,
            flat,
            pltpu.SemaphoreType.DMA((slots,)),
            pltpu.SemaphoreType.DMA((slots,)),
            pltpu.SemaphoreType.DMA((share,)),
        ],
        compiler_params=params,
        name="step",
    )(psi, disorder, got_xup, got_xdn, *own_y, *got_y, *got_up, *got_dn)


def solution(mesh):
    in_specs = (P(None, None, "px", "py"), P(None, "px", "py"))
    out_specs = P(None, "section", "px", "py")
    run = functools.partial(local, mesh.shape["px"], mesh.shape["py"])
    return jax.shard_map(run, mesh=mesh, in_specs=in_specs, out_specs=out_specs, check_vma=False)
```

```python
import functools
import math

import jax
import jax.numpy as jnp
from jax import lax
from jax.experimental import pallas as pl
from jax.experimental.pallas import tpu as pltpu
from jax.sharding import PartitionSpec as P

LEVELS = 16
STEP = 0.05
ROTATION = 0.8
COUPLING = 0.25

ROOT_OUT = math.sqrt((3.0 + 2.0 * math.sqrt(1.2)) / 7.0)
ROOT_IN = math.sqrt((3.0 - 2.0 * math.sqrt(1.2)) / 7.0)
PAIRS = (
    (0.25 * ROOT_OUT * ROOT_OUT, (18.0 - math.sqrt(30.0)) / 36.0),
    (0.25 * ROOT_IN * ROOT_IN, (18.0 + math.sqrt(30.0)) / 36.0),
)
KAPPA = STEP * COUPLING
HALF = 0.5 * STEP
SPIN = 0.5 * STEP * ROTATION

DEEP = 3
WIDE = 3 * DEEP
LANES = 128
ROWS = 8
F32 = jnp.float32


def iota(dim):
    return lax.broadcasted_iota(jnp.int32, (ROWS, LANES), dim)


def roll(value, shift, axis):
    return pltpu.roll(value, shift % value.shape[axis] if isinstance(shift, int) else shift, axis)


def strip_lanes():
    lane = iota(1)
    slot = (lane * 57) >> 9
    return slot, lane - WIDE * slot


def level_table():
    lane = iota(1)
    table = jnp.zeros((ROWS, LANES), F32)
    for level in range(LEVELS):
        table = jnp.where(lane == level, F32(STEP * 1.5 * math.sin(2.3 * level + 0.4)), table)
    return table


def look_up(table, level):
    return jnp.take_along_axis(table, level, axis=1, mode="promise_in_bounds")


def to_level(value):
    return jnp.clip(value, 0.0, LEVELS - 1.0).astype(jnp.int32)


def linear(c, xp, xm, yp, ym, zp, zm, cyp, cym, cx):
    diag = [HALF * (zp[i] + zm[i]) - (6.0 * HALF) * c[i] for i in range(2)]
    real = cyp[1] * yp[0] - cym[0] * ym[0] - cx[0] * xp[0] + cx[1] * xm[0] - diag[0]
    imag = cyp[0] * yp[1] - cym[1] * ym[1] - cx[1] * xp[1] + cx[0] * xm[1] + diag[1]
    return real, imag


def first_slope(w, lin, pot):
    g = pot + KAPPA * (w[0] * w[0] + w[1] * w[1])
    return lin[0] + g * w[1], lin[1] - g * w[0]


def second_stage(w, k, lin_w, lin_k, pot, full):
    m = [w[i] + 0.5 * k[i] for i in range(2)]
    p0 = pot + KAPPA * (m[0] * m[0] + m[1] * m[1])
    p1 = (2.0 * KAPPA) * (m[0] * k[0] + m[1] * k[1])
    p2 = KAPPA * (k[0] * k[0] + k[1] * k[1])
    n0 = [p0 * m[i] for i in range(2)]
    n1 = [p0 * k[i] + p1 * m[i] for i in range(2)]
    n2 = [p1 * k[i] + p2 * m[i] for i in range(2)]
    n3 = [p2 * k[i] for i in range(2)]
    turn = lambda n: (n[1], -n[0])
    f0 = [lin_w[i] + 0.5 * lin_k[i] + turn(n0)[i] for i in range(2)]
    f1 = [lin_k[i] + turn(n1)[i] for i in range(2)]
    f2 = turn(n2)
    f3 = turn(n3)
    base = [w[i] + 0.5 * f0[i] + (1.0 / 24.0) * f2[i] for i in range(2)]
    z = [base[i] - (1.0 / 12.0) * f1[i] - (1.0 / 80.0) * f3[i] for i in range(2)]
    if not full:
        return z, None
    total = [pot * z[i] for i in range(2)]
    for sq, weight in PAIRS:
        even = [base[i] + (0.5 * sq - 0.125) * f1[i] + (0.25 * sq * sq - 1.0 / 64.0) * f3[i] for i in range(2)]
        odd = [f0[i] + (sq / 3.0) * f2[i] for i in range(2)]
        scale = weight * KAPPA
        p = scale * (even[0] * even[0] + even[1] * even[1]) + (scale * sq) * (odd[0] * odd[0] + odd[1] * odd[1])
        q = (2.0 * scale * sq) * (even[0] * odd[0] + even[1] * odd[1])
        total = [total[i] + p * even[i] + q * odd[i] for i in range(2)]
    return z, (w[0] + total[1], w[1] - total[0])


class Place:
    def __init__(self, dims):
        self.planes, self.share, self.rows, self.cols, self.npx, self.npy = dims
        self.slots = self.share + 2 * DEEP
        self.tiles = self.rows // ROWS
        self.two = self.npy == 2
        self.sides = 1 if self.two else 2
        self.z0 = lax.axis_index("section") * self.share - DEEP
        self.px = lax.axis_index("px")
        self.py = lax.axis_index("py")

    def valid(self, p):
        return (self.z0 + p >= 0) & (self.z0 + p < self.planes)

    def is_left(self, side):
        return self.py == 1 if self.two else side == 0

    def pick(self, side, left, right):
        if self.two:
            return jnp.where(self.py == 1, left, right)
        return left if side == 0 else right

    def coordinate(self, index, count):
        return (index.astype(F32) - (count - 1) / 2.0) / (count / 2.0)

    def xcoord(self, row):
        return self.coordinate(self.px * self.rows + row, self.rows * self.npx)

    def ycoord(self, col):
        return self.coordinate(self.py * self.cols + col, self.cols * self.npy)

    def zcoord(self, slot):
        return self.coordinate(self.z0 + slot, self.planes)


def unpack_rows(sub, even, first, second):
    up = jnp.where(even, second, first)
    dn = jnp.where(even, first, second)
    upper = sub >= 4
    a = jnp.where(upper, up, dn)
    b = jnp.where(upper, roll(up, 3, 0), roll(dn, -3, 0))
    level = jnp.where(upper, roll(up, -2, 0), roll(dn, 2, 0))
    return a, b, level


def rows_kernel(dims, psi, dis, first, second, vpsi, vdis, psem, dsem):
    at = Place(dims)
    ends = (pl.ds(0, ROWS), pl.ds(at.rows - ROWS, ROWS))

    def psi_copy(p, e):
        return pltpu.make_async_copy(psi.at[:, at.z0 + p, ends[e]], vpsi.at[:, p, e], psem.at[p, e])

    def dis_copy(p, e):
        return pltpu.make_async_copy(dis.at[at.z0 + p, ends[e]], vdis.at[p, e], dsem.at[p, e])

    for p in range(1, at.slots - 1):
        deep = 2 <= p < at.slots - 2

        @pl.when(at.valid(p))
        def _():
            for e in range(2):
                psi_copy(p, e).start()
                if deep:
                    dis_copy(p, e).start()

        @pl.when(jnp.logical_not(at.valid(p)))
        def _():
            vpsi[:, p] = jnp.zeros((2, 2, ROWS, LANES), F32)
            vdis[p] = jnp.zeros((2, ROWS, LANES), jnp.int32)

    sub = iota(0)
    even = at.px % 2 == 0
    for p in range(1, at.slots - 1):
        deep = 2 <= p < at.slots - 2

        @pl.when(at.valid(p))
        def _():
            for e in range(2):
                psi_copy(p, e).wait()
                if deep:
                    dis_copy(p, e).wait()

        level = [vdis[p, e].astype(F32) if deep else jnp.zeros((ROWS, LANES), F32) for e in range(2)]
        up = jnp.where(sub >= 5, vpsi[0, p, 1], jnp.where(sub >= 2, roll(vpsi[1, p, 1], -3, 0), roll(level[1], 2, 0)))
        dn = jnp.where(sub < 3, vpsi[0, p, 0], jnp.where(sub < 6, roll(vpsi[1, p, 0], 3, 0), roll(level[0], -2, 0)))
        first[p - 1] = jnp.where(even, up, dn)
        second[p - 1] = jnp.where(even, dn, up)


def columns_kernel(dims, psi, dis, *refs):
    at = Place(dims)
    own, message = refs[: at.sides], refs[at.sides : 2 * at.sides]
    vpsi, vdis, psem, dsem = refs[2 * at.sides :]

    def psi_copy(p):
        return pltpu.make_async_copy(psi.at[:, at.z0 + p], vpsi.at[:, p], psem.at[p])

    def dis_copy(p):
        return pltpu.make_async_copy(dis.at[at.z0 + p], vdis.at[p], dsem.at[p])

    for p in range(at.slots):
        @pl.when(at.valid(p))
        def _():
            psi_copy(p).start()
            dis_copy(p).start()

        @pl.when(jnp.logical_not(at.valid(p)))
        def _():
            vpsi[:, p] = jnp.zeros((2, at.rows, LANES), F32)
            vdis[p] = jnp.zeros((at.rows, LANES), jnp.int32)

    for p in range(at.slots):
        @pl.when(at.valid(p))
        def _():
            psi_copy(p).wait()
            dis_copy(p).wait()

    slot, off = strip_lanes()
    here = [slot == p for p in range(at.slots)]
    for side in range(at.sides):
        shift = at.pick(side, DEEP, LANES - at.cols + 2 * DEEP)
        back = at.pick(side, DEEP, LANES - DEEP)

        def body(j, carry):
            rows = pl.ds(pl.multiple_of(j * ROWS, ROWS), ROWS)
            strips = []
            for load in (
                lambda p: vpsi[0, p, rows, :],
                lambda p: vpsi[1, p, rows, :],
                lambda p: vdis[p, rows, :].astype(F32),
            ):
                acc = jnp.zeros((ROWS, LANES), F32)
                for p in range(at.slots):
                    acc = jnp.where(here[p], roll(load(p), shift + WIDE * p, 1), acc)
                strips.append(acc)
            for i in range(3):
                own[side][i, rows, :] = strips[i]
            message[side][rows, :] = strip_message(at, side, off, back, *strips)
            return carry

        lax.fori_loop(0, at.tiles, body, 0, unroll=2)


def strip_message(at, side, off, back, a, b, level):
    a, level = roll(a, back, 1), roll(level, LANES - back, 1)
    place = at.pick(side, 8 - off, off)
    return jnp.where(place < DEEP, a, jnp.where(place < 2 * DEEP, b, level))


def corner_kernel(dims, first, second, *refs):
    at = Place(dims)
    message = refs[: at.sides]
    outer, whole = refs[at.sides : 2 * at.sides], refs[2 * at.sides :]
    sub = iota(0)
    even = at.px % 2 == 0
    slot, off = strip_lanes()
    tiles = [unpack_rows(sub, even, first[p - 1], second[p - 1]) for p in range(1, at.slots - 1)]
    for side in range(at.sides):
        shift = at.pick(side, DEEP, LANES - at.cols + 2 * DEEP)
        back = at.pick(side, DEEP, LANES - DEEP)
        strips = []
        for i in range(3):
            acc = jnp.zeros((ROWS, LANES), F32)
            for p in range(1, at.slots - 1):
                acc = jnp.where(slot == p, roll(tiles[p - 1][i], shift + WIDE * p, 1), acc)
            strips.append(acc)
            outer[side][i] = acc
        whole[side][: at.rows] = message[side][...]
        whole[side][at.rows :] = strip_message(at, side, off, back, *strips)


def put(ref, lead, value, base):
    ref[lead + (pl.ds(base, ROWS), slice(None))] = value


def get(ref, lead, base):
    return ref[lead + (pl.ds(base, ROWS), slice(None))]


def tile_of(ref, lead, base):
    return [get(ref, (i,) + lead, base) for i in range(2)]


def x_pair(ref, lead, base, outer, end):
    if outer:
        return tile_of(ref, lead, 1), tile_of(ref, lead, end - 1)
    return tile_of(ref, lead, base + 1), tile_of(ref, lead, base - 1)


def put_field(ref, lead, values, base, outer, end):
    for i in range(2):
        put(ref, (i,) + lead, values[i], base)
        if outer:
            put(ref, (i,) + lead, values[i], end)


def step_kernel(dims, psi, dis, first, second, part, w, d, k, lw, pot, zf, coef, dist, psem, dsem):
    at = Place(dims)
    slots, tiles, rows, cols = at.slots, at.tiles, at.rows, at.cols
    end = ROWS + rows

    def psi_copy(p):
        return pltpu.make_async_copy(psi.at[:, at.z0 + p], w.at[:, p, pl.ds(ROWS, rows)], psem.at[p])

    def dis_copy(p):
        return pltpu.make_async_copy(dis.at[at.z0 + p], d.at[p - 1, pl.ds(0, rows)], dsem.at[p])

    zero_plane = jnp.zeros((2, rows + 2 * ROWS, LANES), F32)
    for p in range(slots):
        @pl.when(at.valid(p))
        def _():
            psi_copy(p).start()
            if 1 <= p < slots - 1:
                dis_copy(p).start()

        @pl.when(jnp.logical_not(at.valid(p)))
        def _():
            w[:, p] = zero_plane
            if 1 <= p < slots - 1:
                k[:, p - 1] = zero_plane
            if 2 <= p < slots - 2:
                zf[:, p - 2] = zero_plane

    sub = iota(0)
    lane = iota(1)
    table = level_table()
    even = at.px % 2 == 0
    outer_row = jnp.where(sub >= 4, sub - ROWS, rows + sub)
    global_row = at.px * rows + outer_row
    row_ok = (global_row >= 0) & (global_row < rows * at.npx)

    ys = at.ycoord(lane)
    cx = (SPIN * ys + HALF, SPIN * ys - HALF)
    has_next = jnp.where(lane < cols - 1, 1.0, 0.0)
    has_prev = jnp.where(lane > 0, 1.0, 0.0)
    for j in range(tiles + 1):
        xs = at.xcoord(outer_row if j == 0 else sub + (j - 1) * ROWS)
        here = slice(j * ROWS, (j + 1) * ROWS)
        coef[0, here] = (SPIN * xs + HALF) * has_next
        coef[1, here] = (SPIN * xs - HALF) * has_next
        coef[2, here] = (SPIN * xs + HALF) * has_prev
        coef[3, here] = (SPIN * xs - HALF) * has_prev
        dist[here] = STEP * (xs * xs + ys * ys)

    zero = jnp.zeros((ROWS, LANES), F32)
    for p in range(1, slots - 1):
        a, b, level = unpack_rows(sub, even, first[p - 1], second[p - 1])
        put_field(w, (p,), (a, b), 0, True, end)
        d[p - 1, rows : rows + ROWS, :] = to_level(level)
    for p in (0, slots - 1):
        put_field(w, (p,), (zero, zero), 0, True, end)

    def field_linear(ref, q, base, outer):
        c = tile_of(ref, (q,), base)
        xp, xm = x_pair(ref, (q,), base, outer, end)
        zp = tile_of(ref, (q + 1,), base)
        zm = tile_of(ref, (q - 1,), base)
        yp = [roll(c[i], -1, 1) for i in range(2)]
        ym = [roll(c[i], 1, 1) for i in range(2)]
        cyp = [get(coef, (i,), base) for i in (0, 1)]
        cym = [get(coef, (i,), base) for i in (2, 3)]
        return c, linear(c, xp, xm, yp, ym, zp, zm, cyp, cym, cx)

    def wait_plane(p, with_level):
        @pl.when(at.valid(p))
        def _():
            psi_copy(p).wait()

        if with_level:
            @pl.when(at.valid(p) & (p < slots - 1))
            def _():
                dis_copy(p).wait()

    wait_plane(0, False)
    wait_plane(1, True)

    def one_body(p, carry):
        wait_plane(p + 1, True)
        zp = at.zcoord(p)
        level_at = table + STEP * (zp * zp)

        @pl.when(at.valid(p))
        def _():
            for j in range(tiles + 1):
                base, outer = j * ROWS, j == 0
                c, lin = field_linear(w, p, base, outer)
                level = d[p - 1, pl.ds(base - ROWS if j else rows, ROWS), :]
                here = look_up(level_at, level) + get(dist, (), base)
                slope = first_slope(c, lin, here)
                if outer:
                    slope = [jnp.where(row_ok, s, 0.0) for s in slope]
                put_field(k, (p - 1,), slope, base, outer, end)
                put_field(lw, (p - 1,), lin, base, False, end)
                put(pot, (p - 1,), here, base)

        return carry

    lax.fori_loop(1, slots - 1, one_body, 0)

    def two_tile(p, j, full):
        base, outer = j * ROWS, j == 0
        c, lin = field_linear(k, p - 1, base, outer)
        z, rest = second_stage(
            tile_of(w, (p,), base), c, tile_of(lw, (p - 1,), base), lin, get(pot, (p - 1,), base), full and not outer
        )
        if outer:
            z = [jnp.where(row_ok, s, 0.0) for s in z]
        put_field(zf, (p - 2,), z, base, outer, end)
        if rest is not None:
            for i in range(2):
                put(part, (i, p - DEEP), rest[i], base - ROWS)

    for p in (2, slots - 3):
        @pl.when(at.valid(p))
        def _():
            for j in range(tiles + 1):
                two_tile(p, j, False)

    def two_body(p, carry):
        for j in range(tiles + 1):
            two_tile(p, j, True)
        return carry

    lax.fori_loop(DEEP, DEEP + at.share, two_body, 0)

    def three_body(p, carry):
        for j in range(1, tiles + 1):
            base = j * ROWS
            _, lin = field_linear(zf, p - 2, base, False)
            for i in range(2):
                lead = (i, p - DEEP)
                put(part, lead, get(part, lead, base - ROWS) + lin[i], base - ROWS)
        return carry

    lax.fori_loop(DEEP, DEEP + at.share, three_body, 0)


def strip_kernel(dims, part, *refs):
    at = Place(dims)
    own, outer_own, got = (refs[i * at.sides : (i + 1) * at.sides] for i in range(3))
    out, result, sw, sk, sl, sp, sz, coef, osem = refs[3 * at.sides :]
    tiles, rows, cols = at.tiles, at.rows, at.cols
    end = ROWS + rows
    sub = iota(0)
    lane = iota(1)
    slot, off = strip_lanes()
    table = level_table()
    outer_row = jnp.where(sub >= 4, sub - ROWS, rows + sub)
    inside = lambda index, count: (index >= 0) & (index < count)
    row_ok = inside(at.px * rows + outer_row, rows * at.npx)
    zs = at.zcoord(slot)

    for j in range(tiles + 1):
        xs = at.xcoord(outer_row if j == 0 else sub + (j - 1) * ROWS)
        here = slice(j * ROWS, (j + 1) * ROWS)
        coef[0, here] = SPIN * xs + HALF
        coef[1, here] = SPIN * xs - HALF
        coef[2, here] = STEP * (xs * xs)

    for side in range(at.sides):
        col = off + at.pick(side, -DEEP, cols - 2 * DEEP)
        ok = inside(at.z0 + slot, at.planes) & inside(at.py * cols + col, cols * at.npy)
        ys = at.ycoord(col)
        cx = (SPIN * ys + HALF, SPIN * ys - HALF)
        far = STEP * (zs * zs + ys * ys)
        halo = at.pick(side, off, 8 - off) < DEEP
        back_b = at.pick(side, LANES - DEEP, DEEP)
        back_d = at.pick(side, LANES - 2 * DEEP, 2 * DEEP)

        def strip_load(base, outer):
            if outer:
                new = got[side][rows:, :]
                mine = [outer_own[side][i] for i in range(3)]
            else:
                here = pl.ds(base - ROWS, ROWS)
                new = got[side][here, :]
                mine = [own[side][i, here, :] for i in range(3)]
            a = jnp.where(halo, new, mine[0])
            b = jnp.where(halo, roll(new, back_b, 1), mine[1])
            level = to_level(jnp.where(halo, roll(new, back_d, 1), mine[2]))
            put_field(sw, (side,), (a, b), base, outer, end)
            put(sp, (side,), look_up(table, level) + (far + get(coef, (2,), base)), base)

        def strip_linear(ref, base, outer):
            c = tile_of(ref, (side,), base)
            xp, xm = x_pair(ref, (side,), base, outer, end)
            yp, ym, zp, zm = [[roll(c[i], s, 1) for i in range(2)] for s in (-1, 1, -WIDE, WIDE)]
            cy = [get(coef, (i,), base) for i in (0, 1)]
            return c, linear(c, xp, xm, yp, ym, zp, zm, cy, cy, cx)

        def keep(values, outer):
            good = (ok & row_ok) if outer else ok
            return [jnp.where(good, s, 0.0) for s in values]

        def strip_one(base, outer):
            c, lin = strip_linear(sw, base, outer)
            slope = first_slope(c, lin, get(sp, (side,), base))
            put_field(sk, (side,), keep(slope, outer), base, outer, end)
            put_field(sl, (side,), lin, base, False, end)

        def strip_two(base, outer):
            c, lin = strip_linear(sk, base, outer)
            z, rest = second_stage(
                tile_of(sw, (side,), base), c, tile_of(sl, (side,), base), lin, get(sp, (side,), base), not outer
            )
            put_field(sz, (side,), keep(z, outer), base, outer, end)
            if rest is not None:
                put_field(sl, (side,), rest, base, False, end)

        for stage in (strip_load, strip_one, strip_two):
            for j in range(tiles + 1):
                stage(j * ROWS, j == 0)

    def out_copy(p):
        return pltpu.make_async_copy(result.at[:, p], out.at[:, p], osem.at[p])

    def finish(j, carry):
        base = pl.multiple_of(j * ROWS, ROWS)
        faces = []
        for side in range(at.sides):
            c = tile_of(sz, (side,), base + ROWS)
            xp, xm = x_pair(sz, (side,), base + ROWS, False, end)
            yp, ym, zp, zm = [[roll(c[i], s, 1) for i in range(2)] for s in (-1, 1, -WIDE, WIDE)]
            cy = [get(coef, (i,), base + ROWS) for i in (0, 1)]
            col = off + at.pick(side, -DEEP, cols - 2 * DEEP)
            ys = at.ycoord(col)
            lin = linear(c, xp, xm, yp, ym, zp, zm, cy, cy, (SPIN * ys + HALF, SPIN * ys - HALF))
            faces.append([get(sl, (i, side), base + ROWS) + lin[i] for i in range(2)])
        for p in range(at.share):
            for i in range(2):
                value = get(part, (i, p), base)
                for side in range(at.sides):
                    from_lane = DEEP + WIDE * (p + DEEP)
                    shift = at.pick(side, LANES - from_lane, cols - DEEP - from_lane)
                    if not at.two and side == 1:
                        shift = shift % LANES
                    elif at.two:
                        shift = jnp.where(shift < 0, shift + LANES, shift)
                    face = at.pick(side, lane, cols - 1 - lane) < DEEP
                    value = jnp.where(face, roll(faces[side][i], shift, 1), value)
                put(result, (i, p), value, base)
        return carry

    lax.fori_loop(0, tiles, finish, 0, unroll=2)
    for p in range(at.share):
        out_copy(p).start()
    for p in range(at.share):
        out_copy(p).wait()


def local(npx, npy, psi, disorder):
    planes, rows, cols = psi.shape[1:]
    share = planes // lax.axis_size("section")
    two = npy == 2
    sides = 1 if two else 2
    slots = share + 2 * DEEP
    tall = rows + ROWS
    dims = (planes, share, rows, cols, npx, npy)
    hbm = pl.BlockSpec(memory_space=pltpu.HBM)
    vmem = pl.BlockSpec(memory_space=pltpu.VMEM)
    f32 = lambda *shape: jax.ShapeDtypeStruct(shape, F32)
    scratch = lambda *shape: pltpu.VMEM(shape, F32)
    levels = lambda *shape: pltpu.VMEM(shape, jnp.int32)
    dma = lambda *shape: pltpu.SemaphoreType.DMA(shape)

    def call(kernel, name, ins, outs, out_specs, scratches, flops, moved, *args):
        return pl.pallas_call(
            functools.partial(kernel, dims),
            out_shape=outs,
            in_specs=ins,
            out_specs=out_specs,
            scratch_shapes=scratches,
            compiler_params=pltpu.CompilerParams(vmem_limit_bytes=52 * 1024 * 1024),
            cost_estimate=pl.CostEstimate(flops=flops, bytes_accessed=moved, transcendentals=0),
            name=name,
        )(*args)

    def send(value, pairs):
        return lax.ppermute(value, ("px", "py"), pairs)

    def row_pairs(start):
        found = []
        for i in range(start, npx - 1, 2):
            for j in range(npy):
                found += [(i * npy + j, (i + 1) * npy + j), ((i + 1) * npy + j, i * npy + j)]
        return found

    cells = share * rows * cols
    block = 4 * slots * rows * cols
    first, second = call(
        rows_kernel, "pack_rows", [hbm] * 2, [f32(slots - 2, ROWS, LANES)] * 2, [vmem] * 2,
        [scratch(2, slots, 2, ROWS, LANES), levels(slots, 2, ROWS, LANES), dma(slots, 2), dma(slots, 2)],
        cells // 16, block // 8, psi, disorder,
    )
    first = send(first, row_pairs(0))
    second = send(second, row_pairs(1))

    packed = call(
        columns_kernel, "pack_columns", [hbm] * 2, [f32(3, rows, LANES)] * sides + [f32(rows, LANES)] * sides,
        [vmem] * (2 * sides),
        [scratch(2, slots, rows, cols), levels(slots, rows, cols), dma(slots), dma(slots)],
        9 * cells, 3 * block, psi, disorder,
    )
    own, message = packed[:sides], packed[sides:]

    made = call(
        corner_kernel, "pack_corners", [vmem] * (2 + sides), [f32(3, ROWS, LANES)] * sides + [f32(tall, LANES)] * sides,
        [vmem] * (2 * sides), [], cells // 8, block // 16, first, second, *message,
    )
    outer, message = made[:sides], made[sides:]
    right = [(i * npy + j, i * npy + j + 1) for i in range(npx) for j in range(npy - 1)]
    left = [(b, a) for a, b in right]
    if two:
        got = [send(message[0], right + left)]
    else:
        got = [send(message[1], right), send(message[0], left)]

    field = lambda depth: scratch(2, depth, tall + ROWS, LANES)
    part = call(
        step_kernel, "step", [hbm] * 2 + [vmem] * 2, f32(2, share, rows, cols), vmem,
        [
            field(slots),
            levels(slots - 2, tall, LANES),
            field(slots - 2),
            field(slots - 2),
            scratch(slots - 2, tall, LANES),
            field(slots - 4),
            scratch(4, tall, LANES),
            scratch(tall, LANES),
            dma(slots),
            dma(slots),
        ],
        300 * cells, 4 * block, psi, disorder, first, second,
    )
    return call(
        strip_kernel, "strips", [vmem] * (1 + 3 * sides), f32(2, share, rows, cols), hbm,
        [
            scratch(2, share, rows, cols),
            field(sides),
            field(sides),
            field(sides),
            scratch(sides, tall, LANES),
            field(sides),
            scratch(3, tall, LANES),
            dma(share),
        ],
        30 * cells, 2 * block, part, *own, *outer, *got,
    )


def solution(mesh):
    in_specs = (P(None, None, "px", "py"), P(None, "px", "py"))
    out_specs = P(None, "section", "px", "py")
    run = functools.partial(local, mesh.shape["px"], mesh.shape["py"])
    return jax.shard_map(run, mesh=mesh, in_specs=in_specs, out_specs=out_specs, check_vma=False)
```

```python
import functools
import math

import jax
import jax.numpy as jnp
from jax import lax
from jax.experimental import pallas as pl
from jax.experimental.pallas import tpu as pltpu
from jax.sharding import PartitionSpec as P

LEVELS = 16
STEP = 0.05
ROTATION = 0.8
COUPLING = 0.25

ROOT_OUT = math.sqrt((3.0 + 2.0 * math.sqrt(1.2)) / 7.0)
ROOT_IN = math.sqrt((3.0 - 2.0 * math.sqrt(1.2)) / 7.0)
PAIRS = (
    (0.25 * ROOT_OUT * ROOT_OUT, (18.0 - math.sqrt(30.0)) / 36.0),
    (0.25 * ROOT_IN * ROOT_IN, (18.0 + math.sqrt(30.0)) / 36.0),
)
KAPPA = STEP * COUPLING
HALF = 0.5 * STEP
SPIN = 0.5 * STEP * ROTATION

DEEP = 3
WIDE = 3 * DEEP
LANES = 128
ROWS = 8
F32 = jnp.float32


def iota(dim):
    return lax.broadcasted_iota(jnp.int32, (ROWS, LANES), dim)


def roll(value, shift, axis):
    return pltpu.roll(value, shift % value.shape[axis] if isinstance(shift, int) else shift, axis)


def strip_lanes():
    lane = iota(1)
    slot = (lane * 57) >> 9
    return slot, lane - WIDE * slot


def level_table():
    lane = iota(1)
    table = jnp.zeros((ROWS, LANES), F32)
    for level in range(LEVELS):
        table = jnp.where(lane == level, F32(STEP * 1.5 * math.sin(2.3 * level + 0.4)), table)
    return table


def look_up(table, level):
    return jnp.take_along_axis(table, level, axis=1, mode="promise_in_bounds")


def to_level(value):
    return jnp.clip(value, 0.0, LEVELS - 1.0).astype(jnp.int32)


def linear(c, xp, xm, yp, ym, zp, zm, cyp, cym, cx):
    diag = [HALF * (zp[i] + zm[i]) - (6.0 * HALF) * c[i] for i in range(2)]
    real = cyp[1] * yp[0] - cym[0] * ym[0] - cx[0] * xp[0] + cx[1] * xm[0] - diag[0]
    imag = cyp[0] * yp[1] - cym[1] * ym[1] - cx[1] * xp[1] + cx[0] * xm[1] + diag[1]
    return real, imag


def first_slope(w, lin, pot):
    g = pot + KAPPA * (w[0] * w[0] + w[1] * w[1])
    return lin[0] + g * w[1], lin[1] - g * w[0]


def second_stage(w, k, lin_w, lin_k, pot, full):
    m = [w[i] + 0.5 * k[i] for i in range(2)]
    p0 = pot + KAPPA * (m[0] * m[0] + m[1] * m[1])
    p1 = (2.0 * KAPPA) * (m[0] * k[0] + m[1] * k[1])
    p2 = KAPPA * (k[0] * k[0] + k[1] * k[1])
    n0 = [p0 * m[i] for i in range(2)]
    n1 = [p0 * k[i] + p1 * m[i] for i in range(2)]
    n2 = [p1 * k[i] + p2 * m[i] for i in range(2)]
    n3 = [p2 * k[i] for i in range(2)]
    turn = lambda n: (n[1], -n[0])
    f0 = [lin_w[i] + 0.5 * lin_k[i] + turn(n0)[i] for i in range(2)]
    f1 = [lin_k[i] + turn(n1)[i] for i in range(2)]
    f2 = turn(n2)
    f3 = turn(n3)
    base = [w[i] + 0.5 * f0[i] + (1.0 / 24.0) * f2[i] for i in range(2)]
    z = [base[i] - (1.0 / 12.0) * f1[i] - (1.0 / 80.0) * f3[i] for i in range(2)]
    if not full:
        return z, None
    total = [pot * z[i] for i in range(2)]
    for sq, weight in PAIRS:
        even = [base[i] + (0.5 * sq - 0.125) * f1[i] + (0.25 * sq * sq - 1.0 / 64.0) * f3[i] for i in range(2)]
        odd = [f0[i] + (sq / 3.0) * f2[i] for i in range(2)]
        scale = weight * KAPPA
        p = scale * (even[0] * even[0] + even[1] * even[1]) + (scale * sq) * (odd[0] * odd[0] + odd[1] * odd[1])
        q = (2.0 * scale * sq) * (even[0] * odd[0] + even[1] * odd[1])
        total = [total[i] + p * even[i] + q * odd[i] for i in range(2)]
    return z, (w[0] + total[1], w[1] - total[0])


class Place:
    def __init__(self, dims):
        self.planes, self.share, self.rows, self.cols, self.npx, self.npy = dims
        self.slots = self.share + 2 * DEEP
        self.tiles = self.rows // ROWS
        self.two = self.npy == 2
        self.sides = 1 if self.two else 2
        self.z0 = lax.axis_index("section") * self.share - DEEP
        self.px = lax.axis_index("px")
        self.py = lax.axis_index("py")

    def valid(self, p):
        return (self.z0 + p >= 0) & (self.z0 + p < self.planes)

    def is_left(self, side):
        return self.py == 1 if self.two else side == 0

    def pick(self, side, left, right):
        if self.two:
            return jnp.where(self.py == 1, left, right)
        return left if side == 0 else right

    def coordinate(self, index, count):
        return (index.astype(F32) - (count - 1) / 2.0) / (count / 2.0)

    def xcoord(self, row):
        return self.coordinate(self.px * self.rows + row, self.rows * self.npx)

    def ycoord(self, col):
        return self.coordinate(self.py * self.cols + col, self.cols * self.npy)

    def zcoord(self, slot):
        return self.coordinate(self.z0 + slot, self.planes)


def unpack_rows(sub, even, first, second):
    up = jnp.where(even, second, first)
    dn = jnp.where(even, first, second)
    upper = sub >= 4
    a = jnp.where(upper, up, dn)
    b = jnp.where(upper, roll(up, 3, 0), roll(dn, -3, 0))
    level = jnp.where(upper, roll(up, -2, 0), roll(dn, 2, 0))
    return a, b, level


def rows_kernel(dims, psi, dis, first, second, vpsi, vdis, psem, dsem):
    at = Place(dims)
    ends = (pl.ds(0, ROWS), pl.ds(at.rows - ROWS, ROWS))

    def psi_copy(p, e):
        return pltpu.make_async_copy(psi.at[:, at.z0 + p, ends[e]], vpsi.at[:, p, e], psem.at[p, e])

    def dis_copy(p, e):
        return pltpu.make_async_copy(dis.at[at.z0 + p, ends[e]], vdis.at[p, e], dsem.at[p, e])

    for p in range(1, at.slots - 1):
        deep = 2 <= p < at.slots - 2

        @pl.when(at.valid(p))
        def _():
            for e in range(2):
                psi_copy(p, e).start()
                if deep:
                    dis_copy(p, e).start()

        @pl.when(jnp.logical_not(at.valid(p)))
        def _():
            vpsi[:, p] = jnp.zeros((2, 2, ROWS, LANES), F32)
            vdis[p] = jnp.zeros((2, ROWS, LANES), jnp.int32)

    sub = iota(0)
    even = at.px % 2 == 0
    for p in range(1, at.slots - 1):
        deep = 2 <= p < at.slots - 2

        @pl.when(at.valid(p))
        def _():
            for e in range(2):
                psi_copy(p, e).wait()
                if deep:
                    dis_copy(p, e).wait()

        level = [vdis[p, e].astype(F32) if deep else jnp.zeros((ROWS, LANES), F32) for e in range(2)]
        up = jnp.where(sub >= 5, vpsi[0, p, 1], jnp.where(sub >= 2, roll(vpsi[1, p, 1], -3, 0), roll(level[1], 2, 0)))
        dn = jnp.where(sub < 3, vpsi[0, p, 0], jnp.where(sub < 6, roll(vpsi[1, p, 0], 3, 0), roll(level[0], -2, 0)))
        first[p - 1] = jnp.where(even, up, dn)
        second[p - 1] = jnp.where(even, dn, up)


def columns_kernel(dims, psi, dis, *refs):
    at = Place(dims)
    own, message = refs[: at.sides], refs[at.sides : 2 * at.sides]
    vpsi, vdis, psem, dsem = refs[2 * at.sides :]

    def psi_copy(p):
        return pltpu.make_async_copy(psi.at[:, at.z0 + p], vpsi.at[:, p], psem.at[p])

    def dis_copy(p):
        return pltpu.make_async_copy(dis.at[at.z0 + p], vdis.at[p], dsem.at[p])

    for p in range(at.slots):
        @pl.when(at.valid(p))
        def _():
            psi_copy(p).start()
            dis_copy(p).start()

        @pl.when(jnp.logical_not(at.valid(p)))
        def _():
            vpsi[:, p] = jnp.zeros((2, at.rows, LANES), F32)
            vdis[p] = jnp.zeros((at.rows, LANES), jnp.int32)

    slot, off = strip_lanes()
    here = [slot == p for p in range(at.slots)]
    third = -(-at.slots // 3)
    for start in range(0, at.slots, third):
        group = range(start, min(start + third, at.slots))
        for p in group:
            @pl.when(at.valid(p))
            def _():
                psi_copy(p).wait()
                dis_copy(p).wait()

        for side in range(at.sides):
            shift = at.pick(side, DEEP, LANES - at.cols + 2 * DEEP)
            back = at.pick(side, DEEP, LANES - DEEP)
            for j in range(at.tiles):
                rows = slice(j * ROWS, (j + 1) * ROWS)
                strips = []
                for i in range(3):
                    acc = own[side][i, rows, :] if start else jnp.zeros((ROWS, LANES), F32)
                    for p in group:
                        if i == 2 and p in (0, at.slots - 1):
                            continue
                        value = vpsi[i, p, rows, :] if i < 2 else vdis[p, rows, :].astype(F32)
                        acc = jnp.where(here[p], roll(value, shift + WIDE * p, 1), acc)
                    own[side][i, rows, :] = acc
                    strips.append(acc)
                if group[-1] == at.slots - 1:
                    message[side][rows, :] = strip_message(at, side, off, back, *strips)


def strip_message(at, side, off, back, a, b, level):
    a, level = roll(a, back, 1), roll(level, LANES - back, 1)
    place = at.pick(side, 8 - off, off)
    return jnp.where(place < DEEP, a, jnp.where(place < 2 * DEEP, b, level))


def corner_kernel(dims, first, second, *refs):
    at = Place(dims)
    message = refs[: at.sides]
    outer, whole = refs[at.sides : 2 * at.sides], refs[2 * at.sides :]
    sub = iota(0)
    even = at.px % 2 == 0
    slot, off = strip_lanes()
    tiles = [unpack_rows(sub, even, first[p - 1], second[p - 1]) for p in range(1, at.slots - 1)]
    for side in range(at.sides):
        shift = at.pick(side, DEEP, LANES - at.cols + 2 * DEEP)
        back = at.pick(side, DEEP, LANES - DEEP)
        strips = []
        for i in range(3):
            acc = jnp.zeros((ROWS, LANES), F32)
            for p in range(1, at.slots - 1):
                acc = jnp.where(slot == p, roll(tiles[p - 1][i], shift + WIDE * p, 1), acc)
            strips.append(acc)
            outer[side][i] = acc
        whole[side][: at.rows] = message[side][...]
        whole[side][at.rows :] = strip_message(at, side, off, back, *strips)


def put(ref, lead, value, base):
    ref[lead + (pl.ds(base, ROWS), slice(None))] = value


def get(ref, lead, base):
    return ref[lead + (pl.ds(base, ROWS), slice(None))]


def tile_of(ref, lead, base):
    return [get(ref, (i,) + lead, base) for i in range(2)]


def x_pair(ref, lead, base, outer, end):
    if outer:
        return tile_of(ref, lead, 1), tile_of(ref, lead, end - 1)
    return tile_of(ref, lead, base + 1), tile_of(ref, lead, base - 1)


def put_field(ref, lead, values, base, outer, end):
    for i in range(2):
        put(ref, (i,) + lead, values[i], base)
        if outer:
            put(ref, (i,) + lead, values[i], end)


def step_kernel(dims, psi, dis, first, second, part, w, d, k, lw, pot, zf, coef, dist, psem, dsem):
    at = Place(dims)
    slots, tiles, rows, cols = at.slots, at.tiles, at.rows, at.cols
    end = ROWS + rows

    def psi_copy(p):
        return pltpu.make_async_copy(psi.at[:, at.z0 + p], w.at[:, p, pl.ds(ROWS, rows)], psem.at[p])

    def dis_copy(p):
        return pltpu.make_async_copy(dis.at[at.z0 + p], d.at[p - 1, pl.ds(0, rows)], dsem.at[p])

    zero_plane = jnp.zeros((2, rows + 2 * ROWS, LANES), F32)
    for p in range(slots):
        @pl.when(at.valid(p))
        def _():
            psi_copy(p).start()
            if 1 <= p < slots - 1:
                dis_copy(p).start()

        @pl.when(jnp.logical_not(at.valid(p)))
        def _():
            w[:, p] = zero_plane
            if 1 <= p < slots - 1:
                d[p - 1] = jnp.zeros((rows + ROWS, LANES), jnp.int32)

    sub = iota(0)
    lane = iota(1)
    table = level_table()
    even = at.px % 2 == 0
    outer_row = jnp.where(sub >= 4, sub - ROWS, rows + sub)
    global_row = at.px * rows + outer_row
    row_ok = (global_row >= 0) & (global_row < rows * at.npx)

    ys = at.ycoord(lane)
    cx = (SPIN * ys + HALF, SPIN * ys - HALF)
    has_next = jnp.where(lane < cols - 1, 1.0, 0.0)
    has_prev = jnp.where(lane > 0, 1.0, 0.0)
    for j in range(tiles + 1):
        xs = at.xcoord(outer_row if j == 0 else sub + (j - 1) * ROWS)
        here = slice(j * ROWS, (j + 1) * ROWS)
        coef[0, here] = (SPIN * xs + HALF) * has_next
        coef[1, here] = (SPIN * xs - HALF) * has_next
        coef[2, here] = (SPIN * xs + HALF) * has_prev
        coef[3, here] = (SPIN * xs - HALF) * has_prev
        dist[here] = STEP * (xs * xs + ys * ys)

    zero = jnp.zeros((ROWS, LANES), F32)
    for p in range(1, slots - 1):
        a, b, level = unpack_rows(sub, even, first[p - 1], second[p - 1])
        put_field(w, (p,), (a, b), 0, True, end)
        d[p - 1, rows : rows + ROWS, :] = to_level(level)
    for p in (0, slots - 1):
        put_field(w, (p,), (zero, zero), 0, True, end)

    def field_linear(ref, q, base, outer):
        c = tile_of(ref, (q,), base)
        xp, xm = x_pair(ref, (q,), base, outer, end)
        zp = tile_of(ref, (q + 1,), base)
        zm = tile_of(ref, (q - 1,), base)
        yp = [roll(c[i], -1, 1) for i in range(2)]
        ym = [roll(c[i], 1, 1) for i in range(2)]
        cyp = [get(coef, (i,), base) for i in (0, 1)]
        cym = [get(coef, (i,), base) for i in (2, 3)]
        return c, linear(c, xp, xm, yp, ym, zp, zm, cyp, cym, cx)

    def wait_plane(p, with_level):
        @pl.when(at.valid(p))
        def _():
            psi_copy(p).wait()

        if with_level:
            @pl.when(at.valid(p) & (p < slots - 1))
            def _():
                dis_copy(p).wait()

    wait_plane(0, False)
    wait_plane(1, True)

    def one_tile(p, j, level_at, masked):
        base, outer = j * ROWS, j == 0
        c, lin = field_linear(w, p, base, outer)
        level = d[p - 1, pl.ds(base - ROWS if j else rows, ROWS), :]
        here = look_up(level_at, level) + get(dist, (), base)
        slope = first_slope(c, lin, here)
        if outer:
            slope = [jnp.where(row_ok, s, 0.0) for s in slope]
        if masked:
            slope = [jnp.where(at.valid(p), s, 0.0) for s in slope]
        put_field(k, (p - 1,), slope, base, outer, end)
        put_field(lw, (p - 1,), lin, base, False, end)
        put(pot, (p - 1,), here, base)

    def two_tile(p, j, full):
        base, outer = j * ROWS, j == 0
        c, lin = field_linear(k, p - 1, base, outer)
        z, rest = second_stage(
            tile_of(w, (p,), base), c, tile_of(lw, (p - 1,), base), lin, get(pot, (p - 1,), base), full and not outer
        )
        if outer:
            z = [jnp.where(row_ok, s, 0.0) for s in z]
        if not full:
            z = [jnp.where(at.valid(p), s, 0.0) for s in z]
        put_field(zf, (p - 2,), z, base, outer, end)
        if rest is not None:
            for i in range(2):
                put(part, (i, p - DEEP), rest[i], base - ROWS)

    def three_tile(p, j):
        base = j * ROWS
        _, lin = field_linear(zf, p - 2, base, False)
        for i in range(2):
            lead = (i, p - DEEP)
            put(part, lead, get(part, lead, base - ROWS) + lin[i], base - ROWS)

    def planes(p, masked, two, three):
        wait_plane(p + 1, True)
        zp = at.zcoord(p)
        level_at = table + STEP * (zp * zp)
        for j in range(tiles + 1):
            one_tile(p, j, level_at, masked)
            if two is not None:
                two_tile(p - 1, j, two)
            if three and j:
                three_tile(p - 2, j)

    def loop(start, stop, *what):
        def body(p, carry):
            planes(p, *what)
            return carry

        lax.fori_loop(start, stop, body, 0)

    last = slots - 2
    loop(1, DEEP, True, None, False)
    planes(jnp.int32(DEEP), False, False, False)
    planes(jnp.int32(DEEP + 1), False, True, False)
    loop(DEEP + 2, last, True, True, True)
    planes(jnp.int32(last), True, False, True)


def strip_kernel(dims, part, *refs):
    at = Place(dims)
    own, outer_own, got = (refs[i * at.sides : (i + 1) * at.sides] for i in range(3))
    out, result, sw, sk, sl, sp, sz, coef, osem = refs[3 * at.sides :]
    tiles, rows, cols = at.tiles, at.rows, at.cols
    end = ROWS + rows
    sub = iota(0)
    lane = iota(1)
    slot, off = strip_lanes()
    table = level_table()
    outer_row = jnp.where(sub >= 4, sub - ROWS, rows + sub)
    inside = lambda index, count: (index >= 0) & (index < count)
    row_ok = inside(at.px * rows + outer_row, rows * at.npx)
    zs = at.zcoord(slot)

    for j in range(tiles + 1):
        xs = at.xcoord(outer_row if j == 0 else sub + (j - 1) * ROWS)
        here = slice(j * ROWS, (j + 1) * ROWS)
        coef[0, here] = SPIN * xs + HALF
        coef[1, here] = SPIN * xs - HALF
        coef[2, here] = STEP * (xs * xs)

    for side in range(at.sides):
        col = off + at.pick(side, -DEEP, cols - 2 * DEEP)
        ok = inside(at.z0 + slot, at.planes) & inside(at.py * cols + col, cols * at.npy)
        ys = at.ycoord(col)
        cx = (SPIN * ys + HALF, SPIN * ys - HALF)
        far = STEP * (zs * zs + ys * ys)
        halo = at.pick(side, off, 8 - off) < DEEP
        back_b = at.pick(side, LANES - DEEP, DEEP)
        back_d = at.pick(side, LANES - 2 * DEEP, 2 * DEEP)

        def strip_load(base, outer):
            if outer:
                new = got[side][rows:, :]
                mine = [outer_own[side][i] for i in range(3)]
            else:
                here = pl.ds(base - ROWS, ROWS)
                new = got[side][here, :]
                mine = [own[side][i, here, :] for i in range(3)]
            a = jnp.where(halo, new, mine[0])
            b = jnp.where(halo, roll(new, back_b, 1), mine[1])
            level = to_level(jnp.where(halo, roll(new, back_d, 1), mine[2]))
            put_field(sw, (side,), (a, b), base, outer, end)
            put(sp, (side,), look_up(table, level) + (far + get(coef, (2,), base)), base)

        def strip_linear(ref, base, outer):
            c = tile_of(ref, (side,), base)
            xp, xm = x_pair(ref, (side,), base, outer, end)
            yp, ym, zp, zm = [[roll(c[i], s, 1) for i in range(2)] for s in (-1, 1, -WIDE, WIDE)]
            cy = [get(coef, (i,), base) for i in (0, 1)]
            return c, linear(c, xp, xm, yp, ym, zp, zm, cy, cy, cx)

        def keep(values, outer):
            good = (ok & row_ok) if outer else ok
            return [jnp.where(good, s, 0.0) for s in values]

        def strip_one(base, outer):
            c, lin = strip_linear(sw, base, outer)
            slope = first_slope(c, lin, get(sp, (side,), base))
            put_field(sk, (side,), keep(slope, outer), base, outer, end)
            put_field(sl, (side,), lin, base, False, end)

        def strip_two(base, outer):
            c, lin = strip_linear(sk, base, outer)
            z, rest = second_stage(
                tile_of(sw, (side,), base), c, tile_of(sl, (side,), base), lin, get(sp, (side,), base), not outer
            )
            put_field(sz, (side,), keep(z, outer), base, outer, end)
            if rest is not None:
                put_field(sl, (side,), rest, base, False, end)

        for stage in (strip_load, strip_one, strip_two):
            for j in range(tiles + 1):
                stage(j * ROWS, j == 0)

    def out_copy(p):
        return pltpu.make_async_copy(result.at[:, p], out.at[:, p], osem.at[p])

    for side in range(at.sides):
        ys = at.ycoord(off + at.pick(side, -DEEP, cols - 2 * DEEP))
        cx = (SPIN * ys + HALF, SPIN * ys - HALF)
        for j in range(1, tiles + 1):
            base = j * ROWS
            c = tile_of(sz, (side,), base)
            xp, xm = x_pair(sz, (side,), base, False, end)
            yp, ym, zp, zm = [[roll(c[i], s, 1) for i in range(2)] for s in (-1, 1, -WIDE, WIDE)]
            cy = [get(coef, (i,), base) for i in (0, 1)]
            lin = linear(c, xp, xm, yp, ym, zp, zm, cy, cy, cx)
            put_field(sk, (side,), [get(sl, (i, side), base) + lin[i] for i in range(2)], base, False, end)

    def finish(p, carry):
        from_lane = DEEP + WIDE * (p + DEEP)
        for j in range(tiles):
            for i in range(2):
                value = get(part, (i, p), j * ROWS)
                for side in range(at.sides):
                    shift = (at.pick(side, 0, cols - DEEP) + 2 * LANES - from_lane) % LANES
                    face = at.pick(side, lane, cols - 1 - lane) < DEEP
                    value = jnp.where(face, roll(get(sk, (i, side), (j + 1) * ROWS), shift, 1), value)
                put(result, (i, p), value, j * ROWS)
        out_copy(p).start()
        return carry

    lax.fori_loop(0, at.share, finish, 0)
    for p in range(at.share):
        out_copy(p).wait()


def local(npx, npy, psi, disorder):
    planes, rows, cols = psi.shape[1:]
    share = planes // lax.axis_size("section")
    two = npy == 2
    sides = 1 if two else 2
    slots = share + 2 * DEEP
    tall = rows + ROWS
    dims = (planes, share, rows, cols, npx, npy)
    hbm = pl.BlockSpec(memory_space=pltpu.HBM)
    vmem = pl.BlockSpec(memory_space=pltpu.VMEM)
    f32 = lambda *shape: jax.ShapeDtypeStruct(shape, F32)
    scratch = lambda *shape: pltpu.VMEM(shape, F32)
    levels = lambda *shape: pltpu.VMEM(shape, jnp.int32)
    dma = lambda *shape: pltpu.SemaphoreType.DMA(shape)

    def call(kernel, name, ins, outs, out_specs, scratches, flops, moved, *args):
        return pl.pallas_call(
            functools.partial(kernel, dims),
            out_shape=outs,
            in_specs=ins,
            out_specs=out_specs,
            scratch_shapes=scratches,
            compiler_params=pltpu.CompilerParams(vmem_limit_bytes=52 * 1024 * 1024),
            cost_estimate=pl.CostEstimate(flops=flops, bytes_accessed=moved, transcendentals=0),
            name=name,
        )(*args)

    def send(value, pairs):
        return lax.ppermute(value, ("px", "py"), pairs)

    def row_pairs(start):
        found = []
        for i in range(start, npx - 1, 2):
            for j in range(npy):
                found += [(i * npy + j, (i + 1) * npy + j), ((i + 1) * npy + j, i * npy + j)]
        return found

    cells = share * rows * cols
    block = 4 * slots * rows * cols
    first, second = call(
        rows_kernel, "pack_rows", [hbm] * 2, [f32(slots - 2, ROWS, LANES)] * 2, [vmem] * 2,
        [scratch(2, slots, 2, ROWS, LANES), levels(slots, 2, ROWS, LANES), dma(slots, 2), dma(slots, 2)],
        cells // 16, block // 8, psi, disorder,
    )
    first = send(first, row_pairs(0))
    second = send(second, row_pairs(1))

    packed = call(
        columns_kernel, "pack_columns", [hbm] * 2, [f32(3, rows, LANES)] * sides + [f32(rows, LANES)] * sides,
        [vmem] * (2 * sides),
        [scratch(2, slots, rows, cols), levels(slots, rows, cols), dma(slots), dma(slots)],
        9 * cells, 3 * block, psi, disorder,
    )
    own, message = packed[:sides], packed[sides:]

    made = call(
        corner_kernel, "pack_corners", [vmem] * (2 + sides), [f32(3, ROWS, LANES)] * sides + [f32(tall, LANES)] * sides,
        [vmem] * (2 * sides), [], cells // 8, block // 16, first, second, *message,
    )
    outer, message = made[:sides], made[sides:]
    right = [(i * npy + j, i * npy + j + 1) for i in range(npx) for j in range(npy - 1)]
    left = [(b, a) for a, b in right]
    if two:
        got = [send(message[0], right + left)]
    else:
        got = [send(message[1], right), send(message[0], left)]

    field = lambda depth: scratch(2, depth, tall + ROWS, LANES)
    part = call(
        step_kernel, "step", [hbm] * 2 + [vmem] * 2, f32(2, share, rows, cols), vmem,
        [
            field(slots),
            levels(slots - 2, tall, LANES),
            field(slots - 2),
            field(slots - 2),
            scratch(slots - 2, tall, LANES),
            field(slots - 4),
            scratch(4, tall, LANES),
            scratch(tall, LANES),
            dma(slots),
            dma(slots),
        ],
        300 * cells, 4 * block, psi, disorder, first, second,
    )
    return call(
        strip_kernel, "strips", [vmem] * (1 + 3 * sides), f32(2, share, rows, cols), hbm,
        [
            scratch(2, share, rows, cols),
            field(sides),
            field(sides),
            field(sides),
            scratch(sides, tall, LANES),
            field(sides),
            scratch(3, tall, LANES),
            dma(share),
        ],
        30 * cells, 2 * block, part, *own, *outer, *got,
    )


def solution(mesh):
    in_specs = (P(None, None, "px", "py"), P(None, "px", "py"))
    out_specs = P(None, "section", "px", "py")
    run = functools.partial(local, mesh.shape["px"], mesh.shape["py"])
    return jax.shard_map(run, mesh=mesh, in_specs=in_specs, out_specs=out_specs, check_vma=False)
```

```python
import functools
import math

import jax
import jax.numpy as jnp
from jax import lax
from jax.experimental import pallas as pl
from jax.experimental.pallas import tpu as pltpu
from jax.sharding import PartitionSpec as P

LEVELS = 16
STEP = 0.05
ROTATION = 0.8
COUPLING = 0.25

ROOT_OUT = math.sqrt((3.0 + 2.0 * math.sqrt(1.2)) / 7.0)
ROOT_IN = math.sqrt((3.0 - 2.0 * math.sqrt(1.2)) / 7.0)
PAIRS = (
    (0.25 * ROOT_OUT * ROOT_OUT, (18.0 - math.sqrt(30.0)) / 36.0),
    (0.25 * ROOT_IN * ROOT_IN, (18.0 + math.sqrt(30.0)) / 36.0),
)
KAPPA = STEP * COUPLING
HALF = 0.5 * STEP
SPIN = 0.5 * STEP * ROTATION

DEEP = 3
WIDE = 3 * DEEP
LANES = 128
ROWS = 8
F32 = jnp.float32


def iota(dim):
    return lax.broadcasted_iota(jnp.int32, (ROWS, LANES), dim)


def roll(value, shift, axis):
    return pltpu.roll(value, shift % value.shape[axis] if isinstance(shift, int) else shift, axis)


def strip_lanes():
    lane = iota(1)
    slot = (lane * 57) >> 9
    return slot, lane - WIDE * slot


def level_table():
    lane = iota(1)
    table = jnp.zeros((ROWS, LANES), F32)
    for level in range(LEVELS):
        table = jnp.where(lane == level, F32(STEP * 1.5 * math.sin(2.3 * level + 0.4)), table)
    return table


def look_up(table, level):
    return jnp.take_along_axis(table, level, axis=1, mode="promise_in_bounds")


def to_level(value):
    return jnp.clip(value, 0.0, LEVELS - 1.0).astype(jnp.int32)


def linear(c, xp, xm, yp, ym, zp, zm, cyp, cym, cx):
    diag = [HALF * (zp[i] + zm[i]) - (6.0 * HALF) * c[i] for i in range(2)]
    real = cyp[1] * yp[0] - cym[0] * ym[0] - cx[0] * xp[0] + cx[1] * xm[0] - diag[0]
    imag = cyp[0] * yp[1] - cym[1] * ym[1] - cx[1] * xp[1] + cx[0] * xm[1] + diag[1]
    return real, imag


def first_slope(w, lin, pot):
    g = pot + KAPPA * (w[0] * w[0] + w[1] * w[1])
    return lin[0] + g * w[1], lin[1] - g * w[0]


def second_stage(w, k, lin_w, lin_k, pot, full):
    m = [w[i] + 0.5 * k[i] for i in range(2)]
    p0 = pot + KAPPA * (m[0] * m[0] + m[1] * m[1])
    p1 = (2.0 * KAPPA) * (m[0] * k[0] + m[1] * k[1])
    p2 = KAPPA * (k[0] * k[0] + k[1] * k[1])
    n0 = [p0 * m[i] for i in range(2)]
    n1 = [p0 * k[i] + p1 * m[i] for i in range(2)]
    n2 = [p1 * k[i] + p2 * m[i] for i in range(2)]
    n3 = [p2 * k[i] for i in range(2)]
    turn = lambda n: (n[1], -n[0])
    f0 = [lin_w[i] + 0.5 * lin_k[i] + turn(n0)[i] for i in range(2)]
    f1 = [lin_k[i] + turn(n1)[i] for i in range(2)]
    f2 = turn(n2)
    f3 = turn(n3)
    base = [w[i] + 0.5 * f0[i] + (1.0 / 24.0) * f2[i] for i in range(2)]
    z = [base[i] - (1.0 / 12.0) * f1[i] - (1.0 / 80.0) * f3[i] for i in range(2)]
    if not full:
        return z, None
    total = [pot * z[i] for i in range(2)]
    for sq, weight in PAIRS:
        even = [base[i] + (0.5 * sq - 0.125) * f1[i] + (0.25 * sq * sq - 1.0 / 64.0) * f3[i] for i in range(2)]
        odd = [f0[i] + (sq / 3.0) * f2[i] for i in range(2)]
        scale = weight * KAPPA
        p = scale * (even[0] * even[0] + even[1] * even[1]) + (scale * sq) * (odd[0] * odd[0] + odd[1] * odd[1])
        q = (2.0 * scale * sq) * (even[0] * odd[0] + even[1] * odd[1])
        total = [total[i] + p * even[i] + q * odd[i] for i in range(2)]
    return z, (w[0] + total[1], w[1] - total[0])


class Place:
    def __init__(self, dims):
        self.planes, self.share, self.rows, self.cols, self.npx, self.npy = dims
        self.slots = self.share + 2 * DEEP
        self.tiles = self.rows // ROWS
        self.two = self.npy == 2
        self.sides = 1 if self.two else 2
        self.z0 = lax.axis_index("section") * self.share - DEEP
        self.px = lax.axis_index("px")
        self.py = lax.axis_index("py")

    def valid(self, p):
        return (self.z0 + p >= 0) & (self.z0 + p < self.planes)

    def plane(self, p):
        return jnp.clip(self.z0 + p, 0, self.planes - 1)

    def is_left(self, side):
        return self.py == 1 if self.two else side == 0

    def pick(self, side, left, right):
        if self.two:
            return jnp.where(self.py == 1, left, right)
        return left if side == 0 else right

    def coordinate(self, index, count):
        return (index.astype(F32) - (count - 1) / 2.0) / (count / 2.0)

    def xcoord(self, row):
        return self.coordinate(self.px * self.rows + row, self.rows * self.npx)

    def ycoord(self, col):
        return self.coordinate(self.py * self.cols + col, self.cols * self.npy)

    def zcoord(self, slot):
        return self.coordinate(self.z0 + slot, self.planes)


def unpack_rows(sub, even, first, second):
    up = jnp.where(even, second, first)
    dn = jnp.where(even, first, second)
    upper = sub >= 4
    a = jnp.where(upper, up, dn)
    b = jnp.where(upper, roll(up, 3, 0), roll(dn, -3, 0))
    level = jnp.where(upper, roll(up, -2, 0), roll(dn, 2, 0))
    return a, b, level


def rows_kernel(dims, psi, dis, first, second, vpsi, vdis, psem, dsem):
    at = Place(dims)
    count = at.slots - 2
    start = at.z0 + 1
    window = jnp.clip(start, 0, at.planes - count)
    span = pl.ds(window, count)
    copies = []
    for e, edge in enumerate((pl.ds(0, ROWS), pl.ds(at.rows - ROWS, ROWS))):
        copies.append(pltpu.make_async_copy(psi.at[:, span, edge], vpsi.at[e], psem.at[e]))
        copies.append(pltpu.make_async_copy(dis.at[span, edge], vdis.at[e], dsem.at[e]))
    for copy in copies:
        copy.start()
    sub = iota(0)
    even = at.px % 2 == 0
    for copy in copies:
        copy.wait()
    for t in range(count):
        z = start + t
        index = jnp.clip(z - window, 0, count - 1)
        inside = (z >= 0) & (z < at.planes)
        a, b = [[vpsi[e, i, index] for e in range(2)] for i in range(2)]
        level = [vdis[e, index].astype(F32) for e in range(2)]
        up = jnp.where(sub >= 5, a[1], jnp.where(sub >= 2, roll(b[1], -3, 0), roll(level[1], 2, 0)))
        dn = jnp.where(sub < 3, a[0], jnp.where(sub < 6, roll(b[0], 3, 0), roll(level[0], -2, 0)))
        first[t] = jnp.where(inside, jnp.where(even, up, dn), 0.0)
        second[t] = jnp.where(inside, jnp.where(even, dn, up), 0.0)


def columns_kernel(dims, psi, dis, pot, *refs):
    at = Place(dims)
    own, message = refs[: at.sides], refs[at.sides :]
    slot, off = strip_lanes()
    sub = iota(0)
    table = level_table()
    ys = at.ycoord(iota(1))
    here = [slot == jnp.where(at.valid(p), p, -1) for p in range(at.slots)]
    level_at = [table + STEP * (at.zcoord(p) * at.zcoord(p)) for p in range(at.slots)]
    for j in range(at.tiles):
        rows = slice(j * ROWS, (j + 1) * ROWS)
        xs = at.xcoord(sub + j * ROWS)
        dist = STEP * (xs * xs + ys * ys)
        for p in range(1, at.slots - 1):
            pot[p - 1, rows, :] = look_up(level_at[p], dis[at.plane(p), rows, :]) + dist
        for side in range(at.sides):
            shift = at.pick(side, DEEP, LANES - at.cols + 2 * DEEP)
            back = at.pick(side, DEEP, LANES - DEEP)
            strips = []
            for i in range(3):
                acc = jnp.zeros((ROWS, LANES), F32)
                for p in range(at.slots):
                    if i == 2 and p in (0, at.slots - 1):
                        continue
                    z = at.plane(p)
                    value = psi[i, z, rows, :] if i < 2 else dis[z, rows, :].astype(F32)
                    acc = jnp.where(here[p], roll(value, shift + WIDE * p, 1), acc)
                own[side][i, rows, :] = acc
                strips.append(acc)
            message[side][rows, :] = strip_message(at, side, off, back, *strips)


def strip_message(at, side, off, back, a, b, level):
    a, level = roll(a, back, 1), roll(level, LANES - back, 1)
    place = at.pick(side, 8 - off, off)
    return jnp.where(place < DEEP, a, jnp.where(place < 2 * DEEP, b, level))


def corner_kernel(dims, first, second, *refs):
    at = Place(dims)
    message = refs[: at.sides]
    outer, whole = refs[at.sides : 2 * at.sides], refs[2 * at.sides :]
    sub = iota(0)
    even = at.px % 2 == 0
    slot, off = strip_lanes()
    tiles = [unpack_rows(sub, even, first[p - 1], second[p - 1]) for p in range(1, at.slots - 1)]
    for side in range(at.sides):
        shift = at.pick(side, DEEP, LANES - at.cols + 2 * DEEP)
        back = at.pick(side, DEEP, LANES - DEEP)
        strips = []
        for i in range(3):
            acc = jnp.zeros((ROWS, LANES), F32)
            for p in range(1, at.slots - 1):
                acc = jnp.where(slot == p, roll(tiles[p - 1][i], shift + WIDE * p, 1), acc)
            strips.append(acc)
            outer[side][i] = acc
        whole[side][: at.rows] = message[side][...]
        whole[side][at.rows :] = strip_message(at, side, off, back, *strips)


def put(ref, lead, value, base):
    ref[lead + (pl.ds(base, ROWS), slice(None))] = value


def get(ref, lead, base):
    return ref[lead + (pl.ds(base, ROWS), slice(None))]


def tile_of(ref, lead, base):
    return [get(ref, (i,) + lead, base) for i in range(2)]


def x_pair(ref, lead, base, outer, end):
    if outer:
        return tile_of(ref, lead, 1), tile_of(ref, lead, end - 1)
    return tile_of(ref, lead, base + 1), tile_of(ref, lead, base - 1)


def put_field(ref, lead, values, base, outer, end):
    for i in range(2):
        put(ref, (i,) + lead, values[i], base)
        if outer:
            put(ref, (i,) + lead, values[i], end)


def step_kernel(dims, psi, pot, first, second, part, w, k, lw, outer_pot, zf, coef):
    at = Place(dims)
    slots, tiles, rows, cols = at.slots, at.tiles, at.rows, at.cols
    end = ROWS + rows
    sub = iota(0)
    lane = iota(1)
    table = level_table()
    even = at.px % 2 == 0
    outer_row = jnp.where(sub >= 4, sub - ROWS, rows + sub)
    global_row = at.px * rows + outer_row
    row_ok = (global_row >= 0) & (global_row < rows * at.npx)

    ys = at.ycoord(lane)
    cx = (SPIN * ys + HALF, SPIN * ys - HALF)
    has_next = jnp.where(lane < cols - 1, 1.0, 0.0)
    has_prev = jnp.where(lane > 0, 1.0, 0.0)
    for j in range(tiles + 1):
        xs = at.xcoord(outer_row if j == 0 else sub + (j - 1) * ROWS)
        here = slice(j * ROWS, (j + 1) * ROWS)
        coef[0, here] = (SPIN * xs + HALF) * has_next
        coef[1, here] = (SPIN * xs - HALF) * has_next
        coef[2, here] = (SPIN * xs + HALF) * has_prev
        coef[3, here] = (SPIN * xs - HALF) * has_prev

    zero = jnp.zeros((ROWS, LANES), F32)
    xs = at.xcoord(outer_row)
    dist = STEP * (xs * xs + ys * ys)
    for p in range(1, slots - 1):
        a, b, level = unpack_rows(sub, even, first[p - 1], second[p - 1])
        put_field(w, (p,), (a, b), 0, True, end)
        zs = at.zcoord(p)
        outer_pot[p - 1] = look_up(table + STEP * (zs * zs), to_level(level)) + dist
    for p in (0, slots - 1):
        put_field(w, (p,), (zero, zero), 0, True, end)

    def field_linear(ref, q, base, outer):
        c = tile_of(ref, (q,), base)
        xp, xm = x_pair(ref, (q,), base, outer, end)
        zp = tile_of(ref, (q + 1,), base)
        zm = tile_of(ref, (q - 1,), base)
        yp = [roll(c[i], -1, 1) for i in range(2)]
        ym = [roll(c[i], 1, 1) for i in range(2)]
        cyp = [get(coef, (i,), base) for i in (0, 1)]
        cym = [get(coef, (i,), base) for i in (2, 3)]
        return c, linear(c, xp, xm, yp, ym, zp, zm, cyp, cym, cx)

    def fill(p, j):
        for i in range(2):
            value = psi[i, at.plane(p), (j - 1) * ROWS : j * ROWS, :]
            put(w, (i, p), jnp.where(at.valid(p), value, 0.0), j * ROWS)

    for p in range(2):
        for j in range(1, tiles + 1):
            fill(p, j)

    def potential(p, j):
        return get(pot, (p - 1,), (j - 1) * ROWS) if j else outer_pot[p - 1]

    def one_tile(p, j, masked):
        base, outer = j * ROWS, j == 0
        c, lin = field_linear(w, p, base, outer)
        slope = first_slope(c, lin, potential(p, j))
        if outer:
            slope = [jnp.where(row_ok, s, 0.0) for s in slope]
        if masked:
            slope = [jnp.where(at.valid(p), s, 0.0) for s in slope]
        put_field(k, (p - 1,), slope, base, outer, end)
        put_field(lw, (p - 1,), lin, base, False, end)

    def two_tile(p, j, full):
        base, outer = j * ROWS, j == 0
        c, lin = field_linear(k, p - 1, base, outer)
        z, rest = second_stage(
            tile_of(w, (p,), base), c, tile_of(lw, (p - 1,), base), lin, potential(p, j), full and not outer
        )
        if outer:
            z = [jnp.where(row_ok, s, 0.0) for s in z]
        if not full:
            z = [jnp.where(at.valid(p), s, 0.0) for s in z]
        put_field(zf, (p - 2,), z, base, outer, end)
        if rest is not None:
            for i in range(2):
                put(part, (i, p - DEEP), rest[i], base - ROWS)

    def three_tile(p, j):
        base = j * ROWS
        _, lin = field_linear(zf, p - 2, base, False)
        for i in range(2):
            lead = (i, p - DEEP)
            put(part, lead, get(part, lead, base - ROWS) + lin[i], base - ROWS)

    def planes(p, masked, two, three):
        for j in range(1, tiles + 1):
            fill(p + 1, j)
        for j in range(tiles + 1):
            one_tile(p, j, masked)
            if two is not None:
                two_tile(p - 1, j, two)
            if three and j:
                three_tile(p - 2, j)

    def loop(start, stop, *what):
        def body(p, carry):
            planes(p, *what)
            return carry

        lax.fori_loop(start, stop, body, 0)

    last = slots - 2
    loop(1, DEEP, True, None, False)
    planes(jnp.int32(DEEP), False, False, False)
    planes(jnp.int32(DEEP + 1), False, True, False)
    loop(DEEP + 2, last, True, True, True)
    planes(jnp.int32(last), True, False, True)


def strip_kernel(dims, part, *refs):
    at = Place(dims)
    own, outer_own, got = (refs[i * at.sides : (i + 1) * at.sides] for i in range(3))
    out, result, sw, sk, sl, sp, sz, coef, osem = refs[3 * at.sides :]
    tiles, rows, cols = at.tiles, at.rows, at.cols
    end = ROWS + rows
    sub = iota(0)
    lane = iota(1)
    slot, off = strip_lanes()
    table = level_table()
    outer_row = jnp.where(sub >= 4, sub - ROWS, rows + sub)
    inside = lambda index, count: (index >= 0) & (index < count)
    row_ok = inside(at.px * rows + outer_row, rows * at.npx)
    zs = at.zcoord(slot)

    for j in range(tiles + 1):
        xs = at.xcoord(outer_row if j == 0 else sub + (j - 1) * ROWS)
        here = slice(j * ROWS, (j + 1) * ROWS)
        coef[0, here] = SPIN * xs + HALF
        coef[1, here] = SPIN * xs - HALF
        coef[2, here] = STEP * (xs * xs)

    for side in range(at.sides):
        col = off + at.pick(side, -DEEP, cols - 2 * DEEP)
        ok = inside(at.z0 + slot, at.planes) & inside(at.py * cols + col, cols * at.npy)
        ys = at.ycoord(col)
        cx = (SPIN * ys + HALF, SPIN * ys - HALF)
        far = STEP * (zs * zs + ys * ys)
        halo = at.pick(side, off, 8 - off) < DEEP
        back_b = at.pick(side, LANES - DEEP, DEEP)
        back_d = at.pick(side, LANES - 2 * DEEP, 2 * DEEP)

        def strip_load(base, outer):
            if outer:
                new = got[side][rows:, :]
                mine = [outer_own[side][i] for i in range(3)]
            else:
                here = pl.ds(base - ROWS, ROWS)
                new = got[side][here, :]
                mine = [own[side][i, here, :] for i in range(3)]
            a = jnp.where(halo, new, mine[0])
            b = jnp.where(halo, roll(new, back_b, 1), mine[1])
            level = to_level(jnp.where(halo, roll(new, back_d, 1), mine[2]))
            put_field(sw, (side,), (a, b), base, outer, end)
            put(sp, (side,), look_up(table, level) + (far + get(coef, (2,), base)), base)

        def strip_linear(ref, base, outer):
            c = tile_of(ref, (side,), base)
            xp, xm = x_pair(ref, (side,), base, outer, end)
            yp, ym, zp, zm = [[roll(c[i], s, 1) for i in range(2)] for s in (-1, 1, -WIDE, WIDE)]
            cy = [get(coef, (i,), base) for i in (0, 1)]
            return c, linear(c, xp, xm, yp, ym, zp, zm, cy, cy, cx)

        def keep(values, outer):
            good = (ok & row_ok) if outer else ok
            return [jnp.where(good, s, 0.0) for s in values]

        def strip_one(base, outer):
            c, lin = strip_linear(sw, base, outer)
            slope = first_slope(c, lin, get(sp, (side,), base))
            put_field(sk, (side,), keep(slope, outer), base, outer, end)
            put_field(sl, (side,), lin, base, False, end)

        def strip_two(base, outer):
            c, lin = strip_linear(sk, base, outer)
            z, rest = second_stage(
                tile_of(sw, (side,), base), c, tile_of(sl, (side,), base), lin, get(sp, (side,), base), not outer
            )
            put_field(sz, (side,), keep(z, outer), base, outer, end)
            if rest is not None:
                put_field(sl, (side,), rest, base, False, end)

        for stage in (strip_load, strip_one, strip_two):
            for j in range(tiles + 1):
                stage(j * ROWS, j == 0)

    def out_copy(p):
        return pltpu.make_async_copy(result.at[:, p], out.at[:, p], osem.at[p])

    for side in range(at.sides):
        ys = at.ycoord(off + at.pick(side, -DEEP, cols - 2 * DEEP))
        cx = (SPIN * ys + HALF, SPIN * ys - HALF)
        for j in range(1, tiles + 1):
            base = j * ROWS
            c = tile_of(sz, (side,), base)
            xp, xm = x_pair(sz, (side,), base, False, end)
            yp, ym, zp, zm = [[roll(c[i], s, 1) for i in range(2)] for s in (-1, 1, -WIDE, WIDE)]
            cy = [get(coef, (i,), base) for i in (0, 1)]
            lin = linear(c, xp, xm, yp, ym, zp, zm, cy, cy, cx)
            put_field(sk, (side,), [get(sl, (i, side), base) + lin[i] for i in range(2)], base, False, end)

    def finish(p, carry):
        from_lane = DEEP + WIDE * (p + DEEP)
        for j in range(tiles):
            for i in range(2):
                value = get(part, (i, p), j * ROWS)
                for side in range(at.sides):
                    shift = (at.pick(side, 0, cols - DEEP) + 2 * LANES - from_lane) % LANES
                    face = at.pick(side, lane, cols - 1 - lane) < DEEP
                    value = jnp.where(face, roll(get(sk, (i, side), (j + 1) * ROWS), shift, 1), value)
                put(result, (i, p), value, j * ROWS)
        out_copy(p).start()
        return carry

    lax.fori_loop(0, at.share, finish, 0)
    for p in range(at.share):
        out_copy(p).wait()


def local(npx, npy, psi, disorder):
    planes, rows, cols = psi.shape[1:]
    share = planes // lax.axis_size("section")
    two = npy == 2
    sides = 1 if two else 2
    slots = share + 2 * DEEP
    tall = rows + ROWS
    dims = (planes, share, rows, cols, npx, npy)
    hbm = pl.BlockSpec(memory_space=pltpu.HBM)
    vmem = pl.BlockSpec(memory_space=pltpu.VMEM)
    f32 = lambda *shape: jax.ShapeDtypeStruct(shape, F32)
    scratch = lambda *shape: pltpu.VMEM(shape, F32)
    levels = lambda *shape: pltpu.VMEM(shape, jnp.int32)
    dma = lambda *shape: pltpu.SemaphoreType.DMA(shape)

    def call(kernel, name, room, ins, outs, out_specs, scratches, flops, moved, *args):
        return pl.pallas_call(
            functools.partial(kernel, dims),
            out_shape=outs,
            in_specs=ins,
            out_specs=out_specs,
            scratch_shapes=scratches,
            compiler_params=pltpu.CompilerParams(vmem_limit_bytes=room * 1024 * 1024),
            cost_estimate=pl.CostEstimate(flops=flops, bytes_accessed=moved, transcendentals=0),
            name=name,
        )(*args)

    def send(value, pairs):
        return lax.ppermute(value, ("px", "py"), pairs)

    def row_pairs(start):
        found = []
        for i in range(start, npx - 1, 2):
            for j in range(npy):
                found += [(i * npy + j, (i + 1) * npy + j), ((i + 1) * npy + j, i * npy + j)]
        return found

    cells = share * rows * cols
    block = 4 * slots * rows * cols
    first, second = call(
        rows_kernel, "pack_rows", 52, [hbm] * 2, [f32(slots - 2, ROWS, LANES)] * 2, [vmem] * 2,
        [scratch(2, 2, slots - 2, ROWS, LANES), levels(2, slots - 2, ROWS, LANES), dma(2), dma(2)],
        cells // 16, block // 8, psi, disorder,
    )
    first = send(first, row_pairs(0))
    second = send(second, row_pairs(1))

    packed = call(
        columns_kernel, "pack_columns", 24, [vmem] * 2,
        [f32(slots - 2, rows, cols)] + [f32(3, rows, LANES)] * sides + [f32(rows, LANES)] * sides,
        [vmem] * (1 + 2 * sides), [], 12 * cells, 3 * block, psi, disorder,
    )
    pot = packed[0]
    own, message = packed[1 : 1 + sides], packed[1 + sides :]

    made = call(
        corner_kernel, "pack_corners", 24, [vmem] * (2 + sides), [f32(3, ROWS, LANES)] * sides + [f32(tall, LANES)] * sides,
        [vmem] * (2 * sides), [], cells // 8, block // 16, first, second, *message,
    )
    outer, message = made[:sides], made[sides:]
    right = [(i * npy + j, i * npy + j + 1) for i in range(npx) for j in range(npy - 1)]
    left = [(b, a) for a, b in right]
    if two:
        got = [send(message[0], right + left)]
    else:
        got = [send(message[1], right), send(message[0], left)]

    field = lambda depth: scratch(2, depth, tall + ROWS, LANES)
    part = call(
        step_kernel, "step", 24, [vmem] * 4, f32(2, share, rows, cols), vmem,
        [
            field(slots),
            field(slots - 2),
            field(slots - 2),
            scratch(slots - 2, ROWS, LANES),
            field(slots - 4),
            scratch(4, tall, LANES),
        ],
        300 * cells, 4 * block, psi, pot, first, second,
    )
    return call(
        strip_kernel, "strips", 24, [vmem] * (1 + 3 * sides), f32(2, share, rows, cols), hbm,
        [
            scratch(2, share, rows, cols),
            field(sides),
            field(sides),
            field(sides),
            scratch(sides, tall, LANES),
            field(sides),
            scratch(3, tall, LANES),
            dma(share),
        ],
        30 * cells, 2 * block, part, *own, *outer, *got,
    )


def solution(mesh):
    in_specs = (P(None, None, "px", "py"), P(None, "px", "py"))
    out_specs = P(None, "section", "px", "py")
    run = functools.partial(local, mesh.shape["px"], mesh.shape["py"])
    return jax.shard_map(run, mesh=mesh, in_specs=in_specs, out_specs=out_specs, check_vma=False)
```

```python
import functools
import math

import jax
import jax.numpy as jnp
from jax import lax
from jax.experimental import pallas as pl
from jax.experimental.pallas import tpu as pltpu
from jax.sharding import PartitionSpec as P

LEVELS = 16
STEP = 0.05
ROTATION = 0.8
COUPLING = 0.25

ROOT_OUT = math.sqrt((3.0 + 2.0 * math.sqrt(1.2)) / 7.0)
ROOT_IN = math.sqrt((3.0 - 2.0 * math.sqrt(1.2)) / 7.0)
WEIGHT_OUT = (18.0 - math.sqrt(30.0)) / 36.0
WEIGHT_IN = 1.0 - WEIGHT_OUT

LAP = 0.5 * STEP
SPIN = 0.5 * STEP * ROTATION
KAPPA = 0.5 * STEP * COUPLING

DEEP = 3
WIDE = 3 * DEEP
LANES = 128
ROWS = 8
F32 = jnp.float32


def iota(dim):
    return lax.broadcasted_iota(jnp.int32, (ROWS, LANES), dim)


def roll(value, shift, axis):
    return pltpu.roll(value, shift % value.shape[axis] if isinstance(shift, int) else shift, axis)


def strip_lanes():
    lane = iota(1)
    slot = (lane * 57) >> 9
    return slot, lane - WIDE * slot


def level_table():
    lane = iota(1)
    table = jnp.zeros((ROWS, LANES), F32)
    for level in range(LEVELS):
        table = jnp.where(lane == level, F32(0.75 * STEP * math.sin(2.3 * level + 0.4)), table)
    return table


def look_up(table, level):
    return jnp.take_along_axis(table, level, axis=1, mode="promise_in_bounds")


def to_level(value):
    return jnp.clip(value, 0.0, LEVELS - 1.0).astype(jnp.int32)


def factors(spin, lap, scale):
    return scale * (spin + lap), scale * (spin - lap)


def linear(c, xp, xm, yp, ym, zp, zm, cyp, cym, cx, lap, lap_z):
    diag = [lap_z * (zp[i] + zm[i]) - (6.0 * lap) * c[i] for i in range(2)]
    real = cyp[1] * yp[0] - cym[0] * ym[0] - cx[0] * xp[0] + cx[1] * xm[0] - diag[0]
    imag = cyp[0] * yp[1] - cym[1] * ym[1] - cx[1] * xp[1] + cx[0] * xm[1] + diag[1]
    return real, imag


def first_slope(w, lin, pot):
    g = pot + KAPPA * (w[0] * w[0] + w[1] * w[1])
    return lin[0] + g * w[1], lin[1] - g * w[0]


def second_stage(w, k, lin_w, lin_k, pot, full):
    m = [w[i] + k[i] for i in range(2)]
    p0 = pot + KAPPA * (m[0] * m[0] + m[1] * m[1])
    p1 = (2.0 * KAPPA) * (m[0] * k[0] + m[1] * k[1])
    p2 = KAPPA * (k[0] * k[0] + k[1] * k[1])
    f0 = lin_w[0] + lin_k[0] + p0 * m[1], lin_w[1] + lin_k[1] - p0 * m[0]
    f1 = lin_k[0] + (p0 * k[1] + p1 * m[1]), lin_k[1] - (p0 * k[0] + p1 * m[0])
    f2 = p1 * k[1] + p2 * m[1], p1 * k[0] + p2 * m[0]
    f3 = p2 * k[1], p2 * k[0]
    sign = 1.0, -1.0
    base = [w[i] + f0[i] + (sign[i] / 3.0) * f2[i] for i in range(2)]
    z = [base[i] - (1.0 / 3.0) * f1[i] - (sign[i] / 5.0) * f3[i] for i in range(2)]
    if not full:
        return z, None
    square = ROOT_OUT * ROOT_OUT
    even_out = [
        base[i] + (0.5 * (square - 1.0)) * f1[i] + (sign[i] * 0.25 * (square * square - 1.0)) * f3[i] for i in range(2)
    ]
    even_in = [z[i] + (WEIGHT_OUT / WEIGHT_IN) * (z[i] - even_out[i]) for i in range(2)]
    total = [(pot + pot) * z[i] for i in range(2)]
    for even, square, weight in (
        (even_out, ROOT_OUT * ROOT_OUT, WEIGHT_OUT),
        (even_in, ROOT_IN * ROOT_IN, WEIGHT_IN),
    ):
        odd = [f0[i] + (sign[i] * square / 3.0) * f2[i] for i in range(2)]
        scale = 2.0 * KAPPA * weight
        p = scale * (even[0] * even[0] + even[1] * even[1]) + (scale * square) * (odd[0] * odd[0] + odd[1] * odd[1])
        q = (2.0 * scale * square) * (even[0] * odd[0] + even[1] * odd[1])
        total = [total[i] + p * even[i] + q * odd[i] for i in range(2)]
    return z, (w[0] + total[1], w[1] - total[0])


class Place:
    def __init__(self, dims):
        self.planes, self.share, self.rows, self.cols, self.npx, self.npy = dims
        self.slots = self.share + 2 * DEEP
        self.tiles = self.rows // ROWS
        self.two = self.npy == 2
        self.sides = 1 if self.two else 2
        self.z0 = lax.axis_index("section") * self.share - DEEP
        self.px = lax.axis_index("px")
        self.py = lax.axis_index("py")

    def valid(self, p):
        return (self.z0 + p >= 0) & (self.z0 + p < self.planes)

    def plane(self, p):
        return jnp.clip(self.z0 + p, 0, self.planes - 1)

    def is_left(self, side):
        return self.py == 1 if self.two else side == 0

    def pick(self, side, left, right):
        if self.two:
            return jnp.where(self.py == 1, left, right)
        return left if side == 0 else right

    def coordinate(self, index, count):
        return (index.astype(F32) - (count - 1) / 2.0) / (count / 2.0)

    def xcoord(self, row):
        return self.coordinate(self.px * self.rows + row, self.rows * self.npx)

    def ycoord(self, col):
        return self.coordinate(self.py * self.cols + col, self.cols * self.npy)

    def zcoord(self, slot):
        return self.coordinate(self.z0 + slot, self.planes)


def unpack_rows(sub, even, first, second):
    up = jnp.where(even, second, first)
    dn = jnp.where(even, first, second)
    upper = sub >= 4
    a = jnp.where(upper, up, dn)
    b = jnp.where(upper, roll(up, 3, 0), roll(dn, -3, 0))
    level = jnp.where(upper, roll(up, -2, 0), roll(dn, 2, 0))
    return a, b, level


def rows_kernel(dims, psi, dis, first, second, vpsi, vdis, psem, dsem):
    at = Place(dims)
    count = at.slots - 2
    start = at.z0 + 1
    window = jnp.clip(start, 0, at.planes - count)
    span = pl.ds(window, count)
    copies = []
    for e, edge in enumerate((pl.ds(0, ROWS), pl.ds(at.rows - ROWS, ROWS))):
        copies.append(pltpu.make_async_copy(psi.at[:, span, edge], vpsi.at[e], psem.at[e]))
        copies.append(pltpu.make_async_copy(dis.at[span, edge], vdis.at[e], dsem.at[e]))
    for copy in copies:
        copy.start()
    sub = iota(0)
    even = at.px % 2 == 0
    for copy in copies:
        copy.wait()
    for t in range(count):
        z = start + t
        index = jnp.clip(z - window, 0, count - 1)
        inside = (z >= 0) & (z < at.planes)
        a, b = [[vpsi[e, i, index] for e in range(2)] for i in range(2)]
        level = [vdis[e, index].astype(F32) for e in range(2)]
        up = jnp.where(sub >= 5, a[1], jnp.where(sub >= 2, roll(b[1], -3, 0), roll(level[1], 2, 0)))
        dn = jnp.where(sub < 3, a[0], jnp.where(sub < 6, roll(b[0], 3, 0), roll(level[0], -2, 0)))
        first[t] = jnp.where(inside, jnp.where(even, up, dn), 0.0)
        second[t] = jnp.where(inside, jnp.where(even, dn, up), 0.0)


def columns_kernel(dims, psi, dis, pot, *refs):
    at = Place(dims)
    own, message = refs[: at.sides], refs[at.sides :]
    slot, off = strip_lanes()
    sub = iota(0)
    table = level_table()
    ys = at.ycoord(iota(1))
    here = [slot == jnp.where(at.valid(p), p, -1) for p in range(at.slots)]
    level_at = [table + (0.5 * STEP) * (at.zcoord(p) * at.zcoord(p)) for p in range(at.slots)]
    for j in range(at.tiles):
        rows = slice(j * ROWS, (j + 1) * ROWS)
        xs = at.xcoord(sub + j * ROWS)
        dist = (0.5 * STEP) * (xs * xs + ys * ys)
        for p in range(1, at.slots - 1):
            pot[p - 1, rows, :] = look_up(level_at[p], dis[at.plane(p), rows, :]) + dist
        for side in range(at.sides):
            shift = at.pick(side, DEEP, LANES - at.cols + 2 * DEEP)
            back = at.pick(side, DEEP, LANES - DEEP)
            strips = []
            for i in range(3):
                acc = jnp.zeros((ROWS, LANES), F32)
                for p in range(at.slots):
                    if i == 2 and p in (0, at.slots - 1):
                        continue
                    z = at.plane(p)
                    value = psi[i, z, rows, :] if i < 2 else dis[z, rows, :].astype(F32)
                    acc = jnp.where(here[p], roll(value, shift + WIDE * p, 1), acc)
                own[side][i, rows, :] = acc
                strips.append(acc)
            message[side][rows, :] = strip_message(at, side, off, back, *strips)


def strip_message(at, side, off, back, a, b, level):
    a, level = roll(a, back, 1), roll(level, LANES - back, 1)
    place = at.pick(side, 8 - off, off)
    return jnp.where(place < DEEP, a, jnp.where(place < 2 * DEEP, b, level))


def corner_kernel(dims, first, second, *refs):
    at = Place(dims)
    message = refs[: at.sides]
    outer, whole = refs[at.sides : 2 * at.sides], refs[2 * at.sides :]
    sub = iota(0)
    even = at.px % 2 == 0
    slot, off = strip_lanes()
    tiles = [unpack_rows(sub, even, first[p - 1], second[p - 1]) for p in range(1, at.slots - 1)]
    for side in range(at.sides):
        shift = at.pick(side, DEEP, LANES - at.cols + 2 * DEEP)
        back = at.pick(side, DEEP, LANES - DEEP)
        strips = []
        for i in range(3):
            acc = jnp.zeros((ROWS, LANES), F32)
            for p in range(1, at.slots - 1):
                acc = jnp.where(slot == p, roll(tiles[p - 1][i], shift + WIDE * p, 1), acc)
            strips.append(acc)
            outer[side][i] = acc
        whole[side][: at.rows] = message[side][...]
        whole[side][at.rows :] = strip_message(at, side, off, back, *strips)


def put(ref, lead, value, base):
    ref[lead + (pl.ds(base, ROWS), slice(None))] = value


def get(ref, lead, base):
    return ref[lead + (pl.ds(base, ROWS), slice(None))]


def tile_of(ref, lead, base):
    return [get(ref, (i,) + lead, base) for i in range(2)]


def x_pair(ref, lead, base, outer, end):
    if outer:
        return tile_of(ref, lead, 1), tile_of(ref, lead, end - 1)
    return tile_of(ref, lead, base + 1), tile_of(ref, lead, base - 1)


def put_field(ref, lead, values, base, outer, end):
    for i in range(2):
        put(ref, (i,) + lead, values[i], base)
        if outer:
            put(ref, (i,) + lead, values[i], end)


def step_kernel(dims, psi, pot, first, second, part, w, k, lw, outer_pot, zf, coef):
    at = Place(dims)
    slots, tiles, rows, cols = at.slots, at.tiles, at.rows, at.cols
    end = ROWS + rows
    sub = iota(0)
    lane = iota(1)
    table = level_table()
    even = at.px % 2 == 0
    outer_row = jnp.where(sub >= 4, sub - ROWS, rows + sub)
    global_row = at.px * rows + outer_row
    row_ok = (global_row >= 0) & (global_row < rows * at.npx)

    ys = at.ycoord(lane)
    cx = [factors(SPIN * ys, LAP, scale) for scale in (0.5, 1.0)]
    has_next = jnp.where(lane < cols - 1, 1.0, 0.0)
    has_prev = jnp.where(lane > 0, 1.0, 0.0)
    for j in range(tiles + 1):
        xs = at.xcoord(outer_row if j == 0 else sub + (j - 1) * ROWS)
        here = slice(j * ROWS, (j + 1) * ROWS)
        for which, scale in enumerate((0.5, 1.0)):
            for i, factor in enumerate(factors(SPIN * xs, LAP, scale)):
                coef[4 * which + i, here] = factor * has_next
                coef[4 * which + 2 + i, here] = factor * has_prev

    zero = jnp.zeros((ROWS, LANES), F32)
    xs = at.xcoord(outer_row)
    dist = (0.5 * STEP) * (xs * xs + ys * ys)
    for p in range(1, slots - 1):
        a, b, level = unpack_rows(sub, even, first[p - 1], second[p - 1])
        put_field(w, (p,), (a, b), 0, True, end)
        zs = at.zcoord(p)
        outer_pot[p - 1] = look_up(table + (0.5 * STEP) * (zs * zs), to_level(level)) + dist
    for p in (0, slots - 1):
        put_field(w, (p,), (zero, zero), 0, True, end)

    def field_linear(ref, q, base, outer, lap_z, which=0):
        c = tile_of(ref, (q,), base)
        xp, xm = x_pair(ref, (q,), base, outer, end)
        zp = tile_of(ref, (q + 1,), base)
        zm = tile_of(ref, (q - 1,), base)
        yp = [roll(c[i], -1, 1) for i in range(2)]
        ym = [roll(c[i], 1, 1) for i in range(2)]
        cyp = [get(coef, (4 * which + i,), base) for i in (0, 1)]
        cym = [get(coef, (4 * which + i,), base) for i in (2, 3)]
        lap = (0.5, 1.0)[which] * LAP
        return c, linear(c, xp, xm, yp, ym, zp, zm, cyp, cym, cx[which], lap, lap if lap_z is None else lap_z)

    for p in (*range(DEEP), *range(slots - DEEP, slots)):
        @pl.when(jnp.logical_not(at.valid(p)))
        def _():
            w[:, p, ROWS:end] = jnp.zeros((2, rows, LANES), F32)

    def fill(p, j):
        to = jnp.where(at.valid(p), p, slots)
        for i in range(2):
            put(w, (i, to), psi[i, at.plane(p), (j - 1) * ROWS : j * ROWS, :], j * ROWS)

    for p in range(2):
        for j in range(1, tiles + 1):
            fill(p, j)

    def potential(p, j):
        return get(pot, (p - 1,), (j - 1) * ROWS) if j else outer_pot[p - 1]

    def one_tile(p, j, lap_z):
        base, outer = j * ROWS, j == 0
        c, lin = field_linear(w, p, base, outer, lap_z)
        slope = first_slope(c, lin, potential(p, j))
        if outer:
            slope = [jnp.where(row_ok, s, 0.0) for s in slope]
        put_field(k, (p - 1,), slope, base, outer, end)
        put_field(lw, (p - 1,), lin, base, False, end)

    def two_tile(p, j, full, lap_z):
        base, outer = j * ROWS, j == 0
        c, lin = field_linear(k, p - 1, base, outer, lap_z)
        z, rest = second_stage(
            tile_of(w, (p,), base), c, tile_of(lw, (p - 1,), base), lin, potential(p, j), full and not outer
        )
        if outer:
            z = [jnp.where(row_ok, s, 0.0) for s in z]
        put_field(zf, (p - 2,), z, base, outer, end)
        if rest is not None:
            for i in range(2):
                put(part, (i, p - DEEP), rest[i], base - ROWS)

    def three_tile(p, j):
        base = j * ROWS
        _, lin = field_linear(zf, p - 2, base, False, None, 1)
        for i in range(2):
            lead = (i, p - DEEP)
            put(part, lead, get(part, lead, base - ROWS) + lin[i], base - ROWS)

    def planes(p, two, three):
        lap_p = jnp.where(at.valid(p), 0.5 * LAP, 0.0)
        lap_before = None if two else jnp.where(at.valid(p - 1), 0.5 * LAP, 0.0)
        for j in range(1, tiles + 1):
            fill(p + 1, j)
        for j in range(tiles + 1):
            one_tile(p, j, lap_p)
            if two is not None:
                two_tile(p - 1, j, two, lap_before)
            if three and j:
                three_tile(p - 2, j)

    last = slots - 2
    for p in range(1, last + 1):
        planes(p, None if p < DEEP else p not in (DEEP, last), p > DEEP + 1)


def strip_kernel(dims, part, *refs):
    at = Place(dims)
    own, outer_own, got = (refs[i * at.sides : (i + 1) * at.sides] for i in range(3))
    out, result, sw, sk, sl, sp, sz, coef, osem = refs[3 * at.sides :]
    tiles, rows, cols = at.tiles, at.rows, at.cols
    end = ROWS + rows
    sub = iota(0)
    lane = iota(1)
    slot, off = strip_lanes()
    table = level_table()
    outer_row = jnp.where(sub >= 4, sub - ROWS, rows + sub)
    inside = lambda index, count: (index >= 0) & (index < count)
    row_ok = inside(at.px * rows + outer_row, rows * at.npx)
    zs = at.zcoord(slot)

    for j in range(tiles + 1):
        xs = at.xcoord(outer_row if j == 0 else sub + (j - 1) * ROWS)
        here = slice(j * ROWS, (j + 1) * ROWS)
        coef[0, here], coef[1, here] = factors(SPIN * xs, LAP, 0.5)
        coef[2, here], coef[3, here] = factors(SPIN * xs, LAP, 1.0)
        coef[4, here] = (0.5 * STEP) * (xs * xs)

    for side in range(at.sides):
        col = off + at.pick(side, -DEEP, cols - 2 * DEEP)
        ok = inside(at.z0 + slot, at.planes) & inside(at.py * cols + col, cols * at.npy)
        ys = at.ycoord(col)
        cx = factors(SPIN * ys, LAP, 0.5)
        far = (0.5 * STEP) * (zs * zs + ys * ys)
        halo = at.pick(side, off, 8 - off) < DEEP
        back_b = at.pick(side, LANES - DEEP, DEEP)
        back_d = at.pick(side, LANES - 2 * DEEP, 2 * DEEP)

        def strip_load(base, outer):
            if outer:
                new = got[side][rows:, :]
                mine = [outer_own[side][i] for i in range(3)]
            else:
                here = pl.ds(base - ROWS, ROWS)
                new = got[side][here, :]
                mine = [own[side][i, here, :] for i in range(3)]
            a = jnp.where(halo, new, mine[0])
            b = jnp.where(halo, roll(new, back_b, 1), mine[1])
            level = to_level(jnp.where(halo, roll(new, back_d, 1), mine[2]))
            put_field(sw, (side,), (a, b), base, outer, end)
            put(sp, (side,), look_up(table, level) + (far + get(coef, (4,), base)), base)

        def strip_linear(ref, base, outer):
            c = tile_of(ref, (side,), base)
            xp, xm = x_pair(ref, (side,), base, outer, end)
            yp, ym, zp, zm = [[roll(c[i], s, 1) for i in range(2)] for s in (-1, 1, -WIDE, WIDE)]
            cy = [get(coef, (i,), base) for i in (0, 1)]
            return c, linear(c, xp, xm, yp, ym, zp, zm, cy, cy, cx, 0.5 * LAP, 0.5 * LAP)

        def keep(values, outer):
            good = (ok & row_ok) if outer else ok
            return [jnp.where(good, s, 0.0) for s in values]

        def strip_one(base, outer):
            c, lin = strip_linear(sw, base, outer)
            slope = first_slope(c, lin, get(sp, (side,), base))
            put_field(sk, (side,), keep(slope, outer), base, outer, end)
            put_field(sl, (side,), lin, base, False, end)

        def strip_two(base, outer):
            c, lin = strip_linear(sk, base, outer)
            z, rest = second_stage(
                tile_of(sw, (side,), base), c, tile_of(sl, (side,), base), lin, get(sp, (side,), base), not outer
            )
            put_field(sz, (side,), keep(z, outer), base, outer, end)
            if rest is not None:
                put_field(sl, (side,), rest, base, False, end)

        for stage in (strip_load, strip_one, strip_two):
            for j in range(tiles + 1):
                stage(j * ROWS, j == 0)

    def out_copy(p):
        return pltpu.make_async_copy(result.at[:, p], out.at[:, p], osem.at[p])

    for side in range(at.sides):
        ys = at.ycoord(off + at.pick(side, -DEEP, cols - 2 * DEEP))
        cx = factors(SPIN * ys, LAP, 1.0)
        for j in range(1, tiles + 1):
            base = j * ROWS
            c = tile_of(sz, (side,), base)
            xp, xm = x_pair(sz, (side,), base, False, end)
            yp, ym, zp, zm = [[roll(c[i], s, 1) for i in range(2)] for s in (-1, 1, -WIDE, WIDE)]
            cy = [get(coef, (i,), base) for i in (2, 3)]
            lin = linear(c, xp, xm, yp, ym, zp, zm, cy, cy, cx, LAP, LAP)
            put_field(sk, (side,), [get(sl, (i, side), base) + lin[i] for i in range(2)], base, False, end)

    for p in range(at.share):
        from_lane = DEEP + WIDE * (p + DEEP)
        for j in range(tiles):
            for i in range(2):
                value = get(part, (i, p), j * ROWS)
                for side in range(at.sides):
                    shift = (at.pick(side, 0, cols - DEEP) + 2 * LANES - from_lane) % LANES
                    face = at.pick(side, lane, cols - 1 - lane) < DEEP
                    value = jnp.where(face, roll(get(sk, (i, side), (j + 1) * ROWS), shift, 1), value)
                put(result, (i, p), value, j * ROWS)
        out_copy(p).start()
    for p in range(at.share):
        out_copy(p).wait()


def local(npx, npy, psi, disorder):
    planes, rows, cols = psi.shape[1:]
    share = planes // lax.axis_size("section")
    two = npy == 2
    sides = 1 if two else 2
    slots = share + 2 * DEEP
    tall = rows + ROWS
    dims = (planes, share, rows, cols, npx, npy)
    hbm = pl.BlockSpec(memory_space=pltpu.HBM)
    vmem = pl.BlockSpec(memory_space=pltpu.VMEM)
    f32 = lambda *shape: jax.ShapeDtypeStruct(shape, F32)
    scratch = lambda *shape: pltpu.VMEM(shape, F32)
    levels = lambda *shape: pltpu.VMEM(shape, jnp.int32)
    dma = lambda *shape: pltpu.SemaphoreType.DMA(shape)

    def call(kernel, name, room, ins, outs, out_specs, scratches, flops, moved, *args):
        return pl.pallas_call(
            functools.partial(kernel, dims),
            out_shape=outs,
            in_specs=ins,
            out_specs=out_specs,
            scratch_shapes=scratches,
            compiler_params=pltpu.CompilerParams(vmem_limit_bytes=room * 1024 * 1024),
            cost_estimate=pl.CostEstimate(flops=flops, bytes_accessed=moved, transcendentals=0),
            name=name,
        )(*args)

    def send(value, pairs):
        return lax.ppermute(value, ("px", "py"), pairs)

    def row_pairs(start):
        found = []
        for i in range(start, npx - 1, 2):
            for j in range(npy):
                found += [(i * npy + j, (i + 1) * npy + j), ((i + 1) * npy + j, i * npy + j)]
        return found

    cells = share * rows * cols
    block = 4 * slots * rows * cols
    first, second = call(
        rows_kernel, "pack_rows", 52, [hbm] * 2, [f32(slots - 2, ROWS, LANES)] * 2, [vmem] * 2,
        [scratch(2, 2, slots - 2, ROWS, LANES), levels(2, slots - 2, ROWS, LANES), dma(2), dma(2)],
        cells // 16, block // 8, psi, disorder,
    )
    first = send(first, row_pairs(0))
    second = send(second, row_pairs(1))

    packed = call(
        columns_kernel, "pack_columns", 24, [vmem] * 2,
        [f32(slots - 2, rows, cols)] + [f32(3, rows, LANES)] * sides + [f32(rows, LANES)] * sides,
        [vmem] * (1 + 2 * sides), [], 12 * cells, 3 * block, psi, disorder,
    )
    pot = packed[0]
    own, message = packed[1 : 1 + sides], packed[1 + sides :]

    made = call(
        corner_kernel, "pack_corners", 24, [vmem] * (2 + sides), [f32(3, ROWS, LANES)] * sides + [f32(tall, LANES)] * sides,
        [vmem] * (2 * sides), [], cells // 8, block // 16, first, second, *message,
    )
    outer, message = made[:sides], made[sides:]
    right = [(i * npy + j, i * npy + j + 1) for i in range(npx) for j in range(npy - 1)]
    left = [(b, a) for a, b in right]
    if two:
        got = [send(message[0], right + left)]
    else:
        got = [send(message[1], right), send(message[0], left)]

    field = lambda depth: scratch(2, depth, tall + ROWS, LANES)
    part = call(
        step_kernel, "step", 24, [vmem] * 4, f32(2, share, rows, cols), vmem,
        [
            field(slots + 1),
            field(slots - 2),
            field(slots - 2),
            scratch(slots - 2, ROWS, LANES),
            field(slots - 4),
            scratch(8, tall, LANES),
        ],
        300 * cells, 4 * block, psi, pot, first, second,
    )
    return call(
        strip_kernel, "strips", 24, [vmem] * (1 + 3 * sides), f32(2, share, rows, cols), hbm,
        [
            scratch(2, share, rows, cols),
            field(sides),
            field(sides),
            field(sides),
            scratch(sides, tall, LANES),
            field(sides),
            scratch(5, tall, LANES),
            dma(share),
        ],
        30 * cells, 2 * block, part, *own, *outer, *got,
    )


def solution(mesh):
    in_specs = (P(None, None, "px", "py"), P(None, "px", "py"))
    out_specs = P(None, "section", "px", "py")
    run = functools.partial(local, mesh.shape["px"], mesh.shape["py"])
    return jax.shard_map(run, mesh=mesh, in_specs=in_specs, out_specs=out_specs, check_vma=False)
```

```python
import functools
import math

import jax
import jax.numpy as jnp
from jax import lax
from jax.experimental import pallas as pl
from jax.experimental.pallas import tpu as pltpu
from jax.sharding import PartitionSpec as P

LEVELS = 16
STEP = 0.05
ROTATION = 0.8
COUPLING = 0.25

ROOT_OUT = math.sqrt((3.0 + 2.0 * math.sqrt(1.2)) / 7.0)
ROOT_IN = math.sqrt((3.0 - 2.0 * math.sqrt(1.2)) / 7.0)
WEIGHT_OUT = (18.0 - math.sqrt(30.0)) / 36.0
WEIGHT_IN = 1.0 - WEIGHT_OUT

LAP = 0.5 * STEP
SPIN = 0.5 * STEP * ROTATION
KAPPA = 0.5 * STEP * COUPLING

DEEP = 3
WIDE = 3 * DEEP
LANES = 128
ROWS = 8
F32 = jnp.float32


def iota(dim):
    return lax.broadcasted_iota(jnp.int32, (ROWS, LANES), dim)


def roll(value, shift, axis):
    return pltpu.roll(value, shift % value.shape[axis] if isinstance(shift, int) else shift, axis)


def strip_lanes():
    lane = iota(1)
    slot = (lane * 57) >> 9
    return slot, lane - WIDE * slot


def level_table():
    lane = iota(1)
    table = jnp.zeros((ROWS, LANES), F32)
    for level in range(LEVELS):
        table = jnp.where(lane == level, F32(0.75 * STEP * math.sin(2.3 * level + 0.4)), table)
    return table


def look_up(table, level):
    return jnp.take_along_axis(table, level, axis=1, mode="promise_in_bounds")


def to_level(value):
    return jnp.clip(value, 0.0, LEVELS - 1.0).astype(jnp.int32)


def factors(spin, lap, scale):
    return scale * (spin + lap), scale * (spin - lap)


def linear(c, xp, xm, yp, ym, zp, zm, cyp, cym, cx, lap, lap_z):
    diag = [lap_z * (zp[i] + zm[i]) - (6.0 * lap) * c[i] for i in range(2)]
    real = cyp[1] * yp[0] - cym[0] * ym[0] - cx[0] * xp[0] + cx[1] * xm[0] - diag[0]
    imag = cyp[0] * yp[1] - cym[1] * ym[1] - cx[1] * xp[1] + cx[0] * xm[1] + diag[1]
    return real, imag


def first_slope(w, lin, pot):
    g = pot + KAPPA * (w[0] * w[0] + w[1] * w[1])
    return lin[0] + g * w[1], lin[1] - g * w[0]


def second_stage(w, k, lin_w, lin_k, pot, full):
    m = [w[i] + k[i] for i in range(2)]
    p0 = pot + KAPPA * (m[0] * m[0] + m[1] * m[1])
    p1 = (2.0 * KAPPA) * (m[0] * k[0] + m[1] * k[1])
    p2 = KAPPA * (k[0] * k[0] + k[1] * k[1])
    f0 = lin_w[0] + lin_k[0] + p0 * m[1], lin_w[1] + lin_k[1] - p0 * m[0]
    f1 = lin_k[0] + (p0 * k[1] + p1 * m[1]), lin_k[1] - (p0 * k[0] + p1 * m[0])
    f2 = p1 * k[1] + p2 * m[1], p1 * k[0] + p2 * m[0]
    f3 = p2 * k[1], p2 * k[0]
    sign = 1.0, -1.0
    base = [w[i] + f0[i] + (sign[i] / 3.0) * f2[i] for i in range(2)]
    z = [base[i] - (1.0 / 3.0) * f1[i] - (sign[i] / 5.0) * f3[i] for i in range(2)]
    if not full:
        return z, None
    square = ROOT_OUT * ROOT_OUT
    even_out = [
        base[i] + (0.5 * (square - 1.0)) * f1[i] + (sign[i] * 0.25 * (square * square - 1.0)) * f3[i] for i in range(2)
    ]
    even_in = [z[i] + (WEIGHT_OUT / WEIGHT_IN) * (z[i] - even_out[i]) for i in range(2)]
    total = [(pot + pot) * z[i] for i in range(2)]
    for even, square, weight in (
        (even_out, ROOT_OUT * ROOT_OUT, WEIGHT_OUT),
        (even_in, ROOT_IN * ROOT_IN, WEIGHT_IN),
    ):
        odd = [f0[i] + (sign[i] * square / 3.0) * f2[i] for i in range(2)]
        scale = 2.0 * KAPPA * weight
        p = scale * (even[0] * even[0] + even[1] * even[1]) + (scale * square) * (odd[0] * odd[0] + odd[1] * odd[1])
        q = (2.0 * scale * square) * (even[0] * odd[0] + even[1] * odd[1])
        total = [total[i] + p * even[i] + q * odd[i] for i in range(2)]
    return z, (w[0] + total[1], w[1] - total[0])


class Place:
    def __init__(self, dims):
        self.planes, self.share, self.rows, self.cols, self.npx, self.npy = dims
        self.slots = self.share + 2 * DEEP
        self.tiles = self.rows // ROWS
        self.two = self.npy == 2
        self.sides = 1 if self.two else 2
        self.z0 = lax.axis_index("section") * self.share - DEEP
        self.px = lax.axis_index("px")
        self.py = lax.axis_index("py")
        self.core = lax.axis_index("section") % 2
        self.sends_up = (self.px + self.core) % 2 == 0
        self.pair_planes = 2 * self.share + 2 * DEEP - 2

    def valid(self, p):
        return (self.z0 + p >= 0) & (self.z0 + p < self.planes)

    def outer_row(self, sub):
        return jnp.where(sub >= 4, sub - ROWS, self.rows + sub)

    def on_grid(self, row):
        row = self.px * self.rows + row
        return (row >= 0) & (row < self.rows * self.npx)

    def plane(self, p):
        return jnp.clip(self.z0 + p, 0, self.planes - 1)

    def is_left(self, side):
        return self.py == 1 if self.two else side == 0

    def pick(self, side, left, right):
        if self.two:
            return jnp.where(self.py == 1, left, right)
        return left if side == 0 else right

    def coordinate(self, index, count):
        return (index.astype(F32) - (count - 1) / 2.0) / (count / 2.0)

    def xcoord(self, row):
        return self.coordinate(self.px * self.rows + row, self.rows * self.npx)

    def ycoord(self, col):
        return self.coordinate(self.py * self.cols + col, self.cols * self.npy)

    def zcoord(self, slot):
        return self.coordinate(self.z0 + slot, self.planes)


def unpack_rows(at, p, got, other):
    sub = iota(0)
    index = p - 1 + at.core * at.share
    got, other = got[index], other[index]
    up = jnp.where(at.sends_up, other, got)
    dn = jnp.where(at.sends_up, got, other)
    upper = sub >= 4
    ok = at.on_grid(at.outer_row(sub))
    a = jnp.where(ok, jnp.where(upper, up, dn), 0.0)
    b = jnp.where(ok, jnp.where(upper, roll(up, 3, 0), roll(dn, -3, 0)), 0.0)
    level = jnp.where(upper, roll(up, -2, 0), roll(dn, 2, 0))
    return a, b, level


def rows_kernel(dims, psi, dis, message, vpsi, vdis, psem, dsem):
    at = Place(dims)
    start = at.z0 - at.core * at.share + 1
    window = jnp.clip(start, 0, at.planes - at.pair_planes)
    edge = pl.ds(pl.multiple_of(jnp.where(at.sends_up, at.rows - ROWS, 0), ROWS), ROWS)
    span = pl.ds(window, at.pair_planes)
    copies = [
        pltpu.make_async_copy(psi.at[:, span, edge], vpsi, psem),
        pltpu.make_async_copy(dis.at[span, edge], vdis, dsem),
    ]
    for copy in copies:
        copy.start()
    sub = iota(0)
    place = jnp.where(at.sends_up, ROWS - 1 - sub, sub)
    shift_b = jnp.where(at.sends_up, ROWS - 3, 3)
    shift_d = jnp.where(at.sends_up, 2, ROWS - 2)
    for copy in copies:
        copy.wait()
    for t in range(at.pair_planes):
        z = start + t
        index = jnp.clip(z - window, 0, at.pair_planes - 1)
        a, b, level = vpsi[0, index], vpsi[1, index], vdis[index].astype(F32)
        value = jnp.where(place < 3, a, jnp.where(place < 6, roll(b, shift_b, 0), roll(level, shift_d, 0)))
        message[t] = jnp.where((z >= 0) & (z < at.planes), value, 0.0)


def columns_kernel(dims, psi, dis, pot, *refs):
    at = Place(dims)
    own, message = refs[: at.sides], refs[at.sides :]
    slot, off = strip_lanes()
    sub = iota(0)
    table = level_table()
    ys = at.ycoord(iota(1))
    here = [slot == jnp.where(at.valid(p), p, -1) for p in range(at.slots)]
    level_at = [table + (0.5 * STEP) * (at.zcoord(p) * at.zcoord(p)) for p in range(at.slots)]
    for j in range(at.tiles):
        rows = slice(j * ROWS, (j + 1) * ROWS)
        xs = at.xcoord(sub + j * ROWS)
        dist = (0.5 * STEP) * (xs * xs + ys * ys)
        for p in range(1, at.slots - 1):
            pot[p - 1, rows, :] = look_up(level_at[p], dis[at.plane(p), rows, :]) + dist
        for side in range(at.sides):
            shift = at.pick(side, DEEP, LANES - at.cols + 2 * DEEP)
            back = at.pick(side, DEEP, LANES - DEEP)
            strips = []
            for i in range(3):
                acc = jnp.zeros((ROWS, LANES), F32)
                for p in range(at.slots):
                    if i == 2 and p in (0, at.slots - 1):
                        continue
                    z = at.plane(p)
                    value = psi[i, z, rows, :] if i < 2 else dis[z, rows, :].astype(F32)
                    acc = jnp.where(here[p], roll(value, shift + WIDE * p, 1), acc)
                own[side][i, rows, :] = acc
                strips.append(acc)
            message[side][rows, :] = strip_message(at, side, off, back, *strips)


def strip_message(at, side, off, back, a, b, level):
    a, level = roll(a, back, 1), roll(level, LANES - back, 1)
    place = at.pick(side, 8 - off, off)
    return jnp.where(place < DEEP, a, jnp.where(place < 2 * DEEP, b, level))


def corner_kernel(dims, got, other, *refs):
    at = Place(dims)
    message = refs[: at.sides]
    outer, whole = refs[at.sides : 2 * at.sides], refs[2 * at.sides :]
    slot, off = strip_lanes()
    tiles = [unpack_rows(at, p, got, other) for p in range(1, at.slots - 1)]
    for side in range(at.sides):
        shift = at.pick(side, DEEP, LANES - at.cols + 2 * DEEP)
        back = at.pick(side, DEEP, LANES - DEEP)
        strips = []
        for i in range(3):
            acc = jnp.zeros((ROWS, LANES), F32)
            for p in range(1, at.slots - 1):
                acc = jnp.where(slot == p, roll(tiles[p - 1][i], shift + WIDE * p, 1), acc)
            strips.append(acc)
            outer[side][i] = acc
        whole[side][: at.rows] = message[side][...]
        whole[side][at.rows :] = strip_message(at, side, off, back, *strips)


def put(ref, lead, value, base):
    ref[lead + (pl.ds(base, ROWS), slice(None))] = value


def get(ref, lead, base):
    return ref[lead + (pl.ds(base, ROWS), slice(None))]


def tile_of(ref, lead, base):
    return [get(ref, (i,) + lead, base) for i in range(2)]


def x_pair(ref, lead, base, outer, end):
    if outer:
        return tile_of(ref, lead, 1), tile_of(ref, lead, end - 1)
    return tile_of(ref, lead, base + 1), tile_of(ref, lead, base - 1)


def put_field(ref, lead, values, base, outer, end):
    for i in range(2):
        put(ref, (i,) + lead, values[i], base)
        if outer:
            put(ref, (i,) + lead, values[i], end)


class Stages:
    def __init__(self, at, w, k, lw, coef, scales):
        self.at, self.w, self.k, self.lw, self.coef = at, w, k, lw, coef
        self.end = ROWS + at.rows
        sub, lane = iota(0), iota(1)
        self.outer_row = at.outer_row(sub)
        self.row_ok = at.on_grid(self.outer_row)
        self.ys = at.ycoord(lane)
        self.cx = [factors(SPIN * self.ys, LAP, scale) for scale in scales]
        self.scales = scales
        has_next = jnp.where(lane < at.cols - 1, 1.0, 0.0)
        has_prev = jnp.where(lane > 0, 1.0, 0.0)
        for j in range(at.tiles + 1):
            xs = at.xcoord(self.outer_row if j == 0 else sub + (j - 1) * ROWS)
            here = slice(j * ROWS, (j + 1) * ROWS)
            for which, scale in enumerate(scales):
                for i, factor in enumerate(factors(SPIN * xs, LAP, scale)):
                    coef[4 * which + i, here] = factor * has_next
                    coef[4 * which + 2 + i, here] = factor * has_prev

    def linear(self, ref, q, base, outer, lap_z, which=0):
        c = tile_of(ref, (q,), base)
        xp, xm = x_pair(ref, (q,), base, outer, self.end)
        zp = tile_of(ref, (q + 1,), base)
        zm = tile_of(ref, (q - 1,), base)
        yp = [roll(c[i], -1, 1) for i in range(2)]
        ym = [roll(c[i], 1, 1) for i in range(2)]
        cyp = [get(self.coef, (4 * which + i,), base) for i in (0, 1)]
        cym = [get(self.coef, (4 * which + i,), base) for i in (2, 3)]
        lap = self.scales[which] * LAP
        return c, linear(c, xp, xm, yp, ym, zp, zm, cyp, cym, self.cx[which], lap, lap if lap_z is None else lap_z)

    def one(self, p, j, pot, lap_z):
        base, outer = j * ROWS, j == 0
        c, lin = self.linear(self.w, p, base, outer, lap_z)
        slope = first_slope(c, lin, pot)
        if outer:
            slope = [jnp.where(self.row_ok, s, 0.0) for s in slope]
        put_field(self.k, (p - 1,), slope, base, outer, self.end)
        put_field(self.lw, (p - 1,), lin, base, False, self.end)

    def lap_of(self, p):
        return jnp.where(self.at.valid(p), self.scales[0] * LAP, 0.0)


def slopes_kernel(dims, psi, pot, w, k, lw, coef):
    at = Place(dims)
    stages = Stages(at, w, k, lw, coef, (0.5,))

    for p in (*range(DEEP), *range(at.slots - DEEP, at.slots)):
        @pl.when(jnp.logical_not(at.valid(p)))
        def _():
            w[:, p, ROWS : stages.end] = jnp.zeros((2, at.rows, LANES), F32)

    def fill(p):
        to = jnp.where(at.valid(p), p, at.slots)
        for j in range(1, at.tiles + 1):
            for i in range(2):
                put(w, (i, to), psi[i, at.plane(p), (j - 1) * ROWS : j * ROWS, :], j * ROWS)

    fill(0)
    fill(1)
    for p in range(1, at.slots - 1):
        fill(p + 1)
        lap_p = stages.lap_of(p)
        for j in range(2, at.tiles):
            stages.one(p, j, get(pot, (p - 1,), (j - 1) * ROWS), lap_p)


def step_kernel(dims, pot, got, other, w_in, k_in, lw_in, part, w, k, lw, outer_pot, zf, coef):
    at = Place(dims)
    slots, tiles, rows = at.slots, at.tiles, at.rows
    stages = Stages(at, w, k, lw, coef, (0.5, 1.0))
    end, ys = stages.end, stages.ys
    table = level_table()

    zero = jnp.zeros((ROWS, LANES), F32)
    xs = at.xcoord(stages.outer_row)
    dist = (0.5 * STEP) * (xs * xs + ys * ys)
    for p in range(1, slots - 1):
        a, b, level = unpack_rows(at, p, got, other)
        put_field(w, (p,), (a, b), 0, True, end)
        zs = at.zcoord(p)
        outer_pot[p - 1] = look_up(table + (0.5 * STEP) * (zs * zs), to_level(level)) + dist
    for p in (0, slots - 1):
        put_field(w, (p,), (zero, zero), 0, True, end)

    def potential(p, j):
        return get(pot, (p - 1,), (j - 1) * ROWS) if j else outer_pot[p - 1]

    def two_tile(p, j, full, lap_z):
        base, outer = j * ROWS, j == 0
        c, lin = stages.linear(k, p - 1, base, outer, lap_z)
        z, rest = second_stage(
            tile_of(w, (p,), base), c, tile_of(lw, (p - 1,), base), lin, potential(p, j), full and not outer
        )
        if outer:
            z = [jnp.where(stages.row_ok, s, 0.0) for s in z]
        put_field(zf, (p - 2,), z, base, outer, end)
        if rest is not None:
            for i in range(2):
                put(part, (i, p - DEEP), rest[i], base - ROWS)

    def three_tile(p, j):
        base = j * ROWS
        _, lin = stages.linear(zf, p - 2, base, False, None, 1)
        for i in range(2):
            lead = (i, p - DEEP)
            put(part, lead, get(part, lead, base - ROWS) + lin[i], base - ROWS)

    last = slots - 2
    for p in range(1, last + 1):
        two = None if p < DEEP else p not in (DEEP, last)
        lap_p = stages.lap_of(p)
        lap_before = None if two else stages.lap_of(p - 1)
        for j in range(tiles + 1):
            if j < 2 or j == tiles:
                stages.one(p, j, potential(p, j), lap_p)
            if two is not None:
                two_tile(p - 1, j, two, lap_before)
            if p > DEEP + 1 and j:
                three_tile(p - 2, j)


def strip_kernel(dims, part, *refs):
    at = Place(dims)
    own, outer_own, got = (refs[i * at.sides : (i + 1) * at.sides] for i in range(3))
    out, result, sw, sk, sl, sp, sz, coef, osem = refs[3 * at.sides :]
    tiles, rows, cols = at.tiles, at.rows, at.cols
    end = ROWS + rows
    sub = iota(0)
    lane = iota(1)
    slot, off = strip_lanes()
    table = level_table()
    outer_row = at.outer_row(sub)
    inside = lambda index, count: (index >= 0) & (index < count)
    row_ok = at.on_grid(outer_row)
    zs = at.zcoord(slot)

    for j in range(tiles + 1):
        xs = at.xcoord(outer_row if j == 0 else sub + (j - 1) * ROWS)
        here = slice(j * ROWS, (j + 1) * ROWS)
        coef[0, here], coef[1, here] = factors(SPIN * xs, LAP, 0.5)
        coef[2, here], coef[3, here] = factors(SPIN * xs, LAP, 1.0)
        coef[4, here] = (0.5 * STEP) * (xs * xs)

    for side in range(at.sides):
        col = off + at.pick(side, -DEEP, cols - 2 * DEEP)
        ok = inside(at.z0 + slot, at.planes) & inside(at.py * cols + col, cols * at.npy)
        ys = at.ycoord(col)
        cx = factors(SPIN * ys, LAP, 0.5)
        far = (0.5 * STEP) * (zs * zs + ys * ys)
        halo = at.pick(side, off, 8 - off) < DEEP
        back_b = at.pick(side, LANES - DEEP, DEEP)
        back_d = at.pick(side, LANES - 2 * DEEP, 2 * DEEP)

        def strip_load(base, outer):
            if outer:
                new = got[side][rows:, :]
                mine = [outer_own[side][i] for i in range(3)]
            else:
                here = pl.ds(base - ROWS, ROWS)
                new = got[side][here, :]
                mine = [own[side][i, here, :] for i in range(3)]
            a = jnp.where(halo, new, mine[0])
            b = jnp.where(halo, roll(new, back_b, 1), mine[1])
            level = to_level(jnp.where(halo, roll(new, back_d, 1), mine[2]))
            put_field(sw, (side,), (a, b), base, outer, end)
            put(sp, (side,), look_up(table, level) + (far + get(coef, (4,), base)), base)

        def strip_linear(ref, base, outer):
            c = tile_of(ref, (side,), base)
            xp, xm = x_pair(ref, (side,), base, outer, end)
            yp, ym, zp, zm = [[roll(c[i], s, 1) for i in range(2)] for s in (-1, 1, -WIDE, WIDE)]
            cy = [get(coef, (i,), base) for i in (0, 1)]
            return c, linear(c, xp, xm, yp, ym, zp, zm, cy, cy, cx, 0.5 * LAP, 0.5 * LAP)

        def keep(values, outer):
            good = (ok & row_ok) if outer else ok
            return [jnp.where(good, s, 0.0) for s in values]

        def strip_one(base, outer):
            c, lin = strip_linear(sw, base, outer)
            slope = first_slope(c, lin, get(sp, (side,), base))
            put_field(sk, (side,), keep(slope, outer), base, outer, end)
            put_field(sl, (side,), lin, base, False, end)

        def strip_two(base, outer):
            c, lin = strip_linear(sk, base, outer)
            z, rest = second_stage(
                tile_of(sw, (side,), base), c, tile_of(sl, (side,), base), lin, get(sp, (side,), base), not outer
            )
            put_field(sz, (side,), keep(z, outer), base, outer, end)
            if rest is not None:
                put_field(sl, (side,), rest, base, False, end)

        for stage in (strip_load, strip_one, strip_two):
            for j in range(tiles + 1):
                stage(j * ROWS, j == 0)

    def out_copy(p):
        return pltpu.make_async_copy(result.at[:, p], out.at[:, p], osem.at[p])

    for side in range(at.sides):
        ys = at.ycoord(off + at.pick(side, -DEEP, cols - 2 * DEEP))
        cx = factors(SPIN * ys, LAP, 1.0)
        for j in range(1, tiles + 1):
            base = j * ROWS
            c = tile_of(sz, (side,), base)
            xp, xm = x_pair(sz, (side,), base, False, end)
            yp, ym, zp, zm = [[roll(c[i], s, 1) for i in range(2)] for s in (-1, 1, -WIDE, WIDE)]
            cy = [get(coef, (i,), base) for i in (2, 3)]
            lin = linear(c, xp, xm, yp, ym, zp, zm, cy, cy, cx, LAP, LAP)
            put_field(sk, (side,), [get(sl, (i, side), base) + lin[i] for i in range(2)], base, False, end)

    for p in range(at.share):
        from_lane = DEEP + WIDE * (p + DEEP)
        for j in range(tiles):
            for i in range(2):
                value = get(part, (i, p), j * ROWS)
                for side in range(at.sides):
                    shift = (at.pick(side, 0, cols - DEEP) + 2 * LANES - from_lane) % LANES
                    face = at.pick(side, lane, cols - 1 - lane) < DEEP
                    value = jnp.where(face, roll(get(sk, (i, side), (j + 1) * ROWS), shift, 1), value)
                put(result, (i, p), value, j * ROWS)
        out_copy(p).start()
    for p in range(at.share):
        out_copy(p).wait()


def local(npx, npy, psi, disorder):
    planes, rows, cols = psi.shape[1:]
    share = planes // lax.axis_size("section")
    two = npy == 2
    sides = 1 if two else 2
    slots = share + 2 * DEEP
    tall = rows + ROWS
    dims = (planes, share, rows, cols, npx, npy)
    hbm = pl.BlockSpec(memory_space=pltpu.HBM)
    vmem = pl.BlockSpec(memory_space=pltpu.VMEM)
    f32 = lambda *shape: jax.ShapeDtypeStruct(shape, F32)
    scratch = lambda *shape: pltpu.VMEM(shape, F32)
    levels = lambda *shape: pltpu.VMEM(shape, jnp.int32)
    dma = lambda *shape: pltpu.SemaphoreType.DMA(shape)

    def call(kernel, name, room, ins, outs, out_specs, scratches, flops, moved, *args, aliases={}):
        return pl.pallas_call(
            functools.partial(kernel, dims),
            out_shape=outs,
            in_specs=ins,
            out_specs=out_specs,
            scratch_shapes=scratches,
            input_output_aliases=aliases,
            compiler_params=pltpu.CompilerParams(vmem_limit_bytes=room * 1024 * 1024),
            cost_estimate=pl.CostEstimate(flops=flops, bytes_accessed=moved, transcendentals=0),
            name=name,
        )(*args)

    def send(value, pairs):
        return lax.ppermute(value, ("px", "py"), pairs)

    sections = lax.axis_size("section")
    place = lambda s, i, j: (s * npx + i) * npy + j
    row_pairs = []
    for s in range(sections):
        for i in range(npx):
            partner = i ^ 1 if s % 2 == 0 else ((i + 1) ^ 1) - 1
            for j in range(npy):
                to = (partner, j) if 0 <= partner < npx else (i, j ^ 1)
                if to[1] < npy:
                    row_pairs.append((place(s, i, j), place(s, *to)))
    core_pairs = [(s, s ^ 1) for s in range(sections)]

    cells = share * rows * cols
    block = 4 * slots * rows * cols
    pair_planes = 2 * share + 2 * DEEP - 2
    edges = call(
        rows_kernel, "pack_rows", 52, [hbm] * 2, f32(pair_planes, ROWS, LANES), vmem,
        [scratch(2, pair_planes, ROWS, LANES), levels(pair_planes, ROWS, LANES), dma(), dma()],
        cells // 16, block // 8, psi, disorder,
    )
    edges = lax.ppermute(edges, ("section", "px", "py"), row_pairs)

    packed = call(
        columns_kernel, "pack_columns", 24, [vmem] * 2,
        [f32(slots - 2, rows, cols)] + [f32(3, rows, LANES)] * sides + [f32(rows, LANES)] * sides,
        [vmem] * (1 + 2 * sides), [], 12 * cells, 3 * block, psi, disorder,
    )
    edges, packed = lax.optimization_barrier((edges, packed))
    pot = packed[0]
    own, message = packed[1 : 1 + sides], packed[1 + sides :]
    others = lax.ppermute(edges, "section", core_pairs)
    field = lambda depth: (2, depth, tall + ROWS, LANES)
    begun = call(
        slopes_kernel, "slopes", 24, [vmem] * 2, [f32(*field(n)) for n in (slots + 1, slots - 2, slots - 2)], [vmem] * 3,
        [scratch(4, tall, LANES)], 60 * cells, 4 * block, psi, pot,
    )
    others, begun = lax.optimization_barrier((others, begun))

    made = call(
        corner_kernel, "pack_corners", 24, [vmem] * (2 + sides), [f32(3, ROWS, LANES)] * sides + [f32(tall, LANES)] * sides,
        [vmem] * (2 * sides), [], cells // 8, block // 16, edges, others, *message,
    )
    outer, message = made[:sides], made[sides:]
    right = [(i * npy + j, i * npy + j + 1) for i in range(npx) for j in range(npy - 1)]
    left = [(b, a) for a, b in right]
    if two:
        got = [send(message[0], right + left)]
    else:
        got = [send(message[1], right), send(message[0], left)]

    part = call(
        step_kernel, "step", 24, [vmem] * 6,
        [f32(2, share, rows, cols)] + [f32(*field(n)) for n in (slots + 1, slots - 2, slots - 2)], [vmem] * 4,
        [scratch(slots - 2, ROWS, LANES), scratch(*field(slots - 4)), scratch(8, tall, LANES)],
        240 * cells, 4 * block, pot, edges, others, *begun, aliases={3: 1, 4: 2, 5: 3},
    )[0]
    return call(
        strip_kernel, "strips", 24, [vmem] * (1 + 3 * sides), f32(2, share, rows, cols), hbm,
        [
            scratch(2, share, rows, cols),
            scratch(*field(sides)),
            scratch(*field(sides)),
            scratch(*field(sides)),
            scratch(sides, tall, LANES),
            scratch(*field(sides)),
            scratch(5, tall, LANES),
            dma(share),
        ],
        30 * cells, 2 * block, part, *own, *outer, *got,
    )


def solution(mesh):
    in_specs = (P(None, None, "px", "py"), P(None, "px", "py"))
    out_specs = P(None, "section", "px", "py")
    run = functools.partial(local, mesh.shape["px"], mesh.shape["py"])
    return jax.shard_map(run, mesh=mesh, in_specs=in_specs, out_specs=out_specs, check_vma=False)
```

```python
import functools
import math

import jax
import jax.numpy as jnp
from jax import lax
from jax.experimental import pallas as pl
from jax.experimental.pallas import tpu as pltpu
from jax.sharding import PartitionSpec as P

LEVELS = 16
STEP = 0.05
ROTATION = 0.8
COUPLING = 0.25

ROOT_OUT = math.sqrt((3.0 + 2.0 * math.sqrt(1.2)) / 7.0)
ROOT_IN = math.sqrt((3.0 - 2.0 * math.sqrt(1.2)) / 7.0)
WEIGHT_OUT = (18.0 - math.sqrt(30.0)) / 36.0
WEIGHT_IN = 1.0 - WEIGHT_OUT

LAP = 0.5 * STEP
SPIN = 0.5 * STEP * ROTATION
KAPPA = 0.5 * STEP * COUPLING

DEEP = 3
WIDE = 3 * DEEP
LANES = 128
ROWS = 8
AHEAD = 6
F32 = jnp.float32


def iota(dim):
    return lax.broadcasted_iota(jnp.int32, (ROWS, LANES), dim)


def roll(value, shift, axis):
    return pltpu.roll(value, shift % value.shape[axis] if isinstance(shift, int) else shift, axis)


def strip_lanes():
    lane = iota(1)
    slot = (lane * 57) >> 9
    return slot, lane - WIDE * slot


def level_table():
    lane = iota(1)
    table = jnp.zeros((ROWS, LANES), F32)
    for level in range(LEVELS):
        table = jnp.where(lane == level, F32(0.75 * STEP * math.sin(2.3 * level + 0.4)), table)
    return table


def look_up(table, level):
    return jnp.take_along_axis(table, level, axis=1, mode="promise_in_bounds")


def to_level(value):
    return jnp.clip(value, 0.0, LEVELS - 1.0).astype(jnp.int32)


def factors(spin, lap, scale):
    return scale * (spin + lap), scale * (spin - lap)


def linear(c, xp, xm, yp, ym, zp, zm, cyp, cym, cx, lap, lap_z):
    diag = [lap_z * (zp[i] + zm[i]) - (6.0 * lap) * c[i] for i in range(2)]
    real = cyp[1] * yp[0] - cym[0] * ym[0] - cx[0] * xp[0] + cx[1] * xm[0] - diag[0]
    imag = cyp[0] * yp[1] - cym[1] * ym[1] - cx[1] * xp[1] + cx[0] * xm[1] + diag[1]
    return real, imag


def first_slope(w, lin, pot):
    g = pot + KAPPA * (w[0] * w[0] + w[1] * w[1])
    return lin[0] + g * w[1], lin[1] - g * w[0]


def powers(w, k, lin_w, pot):
    m = [w[i] + k[i] for i in range(2)]
    p0 = pot + KAPPA * (m[0] * m[0] + m[1] * m[1])
    p1 = (2.0 * KAPPA) * (m[0] * k[0] + m[1] * k[1])
    p2 = KAPPA * (k[0] * k[0] + k[1] * k[1])
    return (
        lin_w[0] + p0 * m[1],
        lin_w[1] - p0 * m[0],
        p0 * k[1] + p1 * m[1],
        -(p0 * k[0] + p1 * m[0]),
        p1 * k[1] + p2 * m[1],
        p1 * k[0] + p2 * m[0],
        p2 * k[1],
        p2 * k[0],
    )


def second_stage(w, parts, lin_k, pot, full):
    f0 = parts[0] + lin_k[0], parts[1] + lin_k[1]
    f1 = parts[2] + lin_k[0], parts[3] + lin_k[1]
    f2, f3 = parts[4:6], parts[6:8]
    sign = 1.0, -1.0
    base = [w[i] + f0[i] + (sign[i] / 3.0) * f2[i] for i in range(2)]
    z = [base[i] - (1.0 / 3.0) * f1[i] - (sign[i] / 5.0) * f3[i] for i in range(2)]
    if not full:
        return z, None
    square = ROOT_OUT * ROOT_OUT
    even_out = [
        base[i] + (0.5 * (square - 1.0)) * f1[i] + (sign[i] * 0.25 * (square * square - 1.0)) * f3[i] for i in range(2)
    ]
    even_in = [z[i] + (WEIGHT_OUT / WEIGHT_IN) * (z[i] - even_out[i]) for i in range(2)]
    total = [(pot + pot) * z[i] for i in range(2)]
    for even, square, weight in (
        (even_out, ROOT_OUT * ROOT_OUT, WEIGHT_OUT),
        (even_in, ROOT_IN * ROOT_IN, WEIGHT_IN),
    ):
        odd = [f0[i] + (sign[i] * square / 3.0) * f2[i] for i in range(2)]
        scale = 2.0 * KAPPA * weight
        p = scale * (even[0] * even[0] + even[1] * even[1]) + (scale * square) * (odd[0] * odd[0] + odd[1] * odd[1])
        q = (2.0 * scale * square) * (even[0] * odd[0] + even[1] * odd[1])
        total = [total[i] + p * even[i] + q * odd[i] for i in range(2)]
    return z, (w[0] + total[1], w[1] - total[0])


class Place:
    def __init__(self, dims):
        self.planes, self.share, self.rows, self.cols, self.npx, self.npy = dims
        self.slots = self.share + 2 * DEEP
        self.tiles = self.rows // ROWS
        self.two = self.npy == 2
        self.sides = 1 if self.two else 2
        self.z0 = lax.axis_index("section") * self.share - DEEP
        self.px = lax.axis_index("px")
        self.py = lax.axis_index("py")
        self.core = lax.axis_index("section") % 2
        self.sends_up = (self.px + self.core) % 2 == 0
        self.pair_planes = 2 * self.share + 2 * DEEP - 2

    def valid(self, p):
        return (self.z0 + p >= 0) & (self.z0 + p < self.planes)

    def outer_row(self, sub):
        return jnp.where(sub >= 4, sub - ROWS, self.rows + sub)

    def on_grid(self, row):
        row = self.px * self.rows + row
        return (row >= 0) & (row < self.rows * self.npx)

    def plane(self, p):
        return jnp.clip(self.z0 + p, 0, self.planes - 1)

    def is_left(self, side):
        return self.py == 1 if self.two else side == 0

    def pick(self, side, left, right):
        if self.two:
            return jnp.where(self.py == 1, left, right)
        return left if side == 0 else right

    def coordinate(self, index, count):
        return (index.astype(F32) - (count - 1) / 2.0) / (count / 2.0)

    def xcoord(self, row):
        return self.coordinate(self.px * self.rows + row, self.rows * self.npx)

    def ycoord(self, col):
        return self.coordinate(self.py * self.cols + col, self.cols * self.npy)

    def zcoord(self, slot):
        return self.coordinate(self.z0 + slot, self.planes)


def unpack_rows(at, p, got, other):
    sub = iota(0)
    index = p - 1 + at.core * at.share
    got, other = got[index], other[index]
    up = jnp.where(at.sends_up, other, got)
    dn = jnp.where(at.sends_up, got, other)
    upper = sub >= 4
    ok = at.on_grid(at.outer_row(sub))
    a = jnp.where(ok, jnp.where(upper, up, dn), 0.0)
    b = jnp.where(ok, jnp.where(upper, roll(up, 3, 0), roll(dn, -3, 0)), 0.0)
    level = jnp.where(upper, roll(up, -2, 0), roll(dn, 2, 0))
    return a, b, level


def rows_kernel(dims, psi, dis, message, vpsi, vdis, psem, dsem):
    at = Place(dims)
    start = at.z0 - at.core * at.share + 1
    window = jnp.clip(start, 0, at.planes - at.pair_planes)
    edge = pl.ds(pl.multiple_of(jnp.where(at.sends_up, at.rows - ROWS, 0), ROWS), ROWS)
    span = pl.ds(window, at.pair_planes)
    copies = [
        pltpu.make_async_copy(psi.at[:, span, edge], vpsi, psem),
        pltpu.make_async_copy(dis.at[span, edge], vdis, dsem),
    ]
    for copy in copies:
        copy.start()
    sub = iota(0)
    place = jnp.where(at.sends_up, ROWS - 1 - sub, sub)
    shift_b = jnp.where(at.sends_up, ROWS - 3, 3)
    shift_d = jnp.where(at.sends_up, 2, ROWS - 2)
    for copy in copies:
        copy.wait()
    for t in range(at.pair_planes):
        z = start + t
        index = jnp.clip(z - window, 0, at.pair_planes - 1)
        a, b, level = vpsi[0, index], vpsi[1, index], vdis[index].astype(F32)
        value = jnp.where(place < 3, a, jnp.where(place < 6, roll(b, shift_b, 0), roll(level, shift_d, 0)))
        message[t] = jnp.where((z >= 0) & (z < at.planes), value, 0.0)


def columns_kernel(dims, psi, dis, pot, *refs):
    at = Place(dims)
    own, message = refs[: at.sides], refs[at.sides :]
    slot, off = strip_lanes()
    sub = iota(0)
    table = level_table()
    ys = at.ycoord(iota(1))
    here = [slot == jnp.where(at.valid(p), p, -1) for p in range(at.slots)]
    level_at = [table + (0.5 * STEP) * (at.zcoord(p) * at.zcoord(p)) for p in range(at.slots)]
    for j in range(at.tiles):
        rows = slice(j * ROWS, (j + 1) * ROWS)
        xs = at.xcoord(sub + j * ROWS)
        dist = (0.5 * STEP) * (xs * xs + ys * ys)
        for p in range(1, at.slots - 1):
            pot[p - 1, rows, :] = look_up(level_at[p], dis[at.plane(p), rows, :]) + dist
        for side in range(at.sides):
            shift = at.pick(side, DEEP, LANES - at.cols + 2 * DEEP)
            back = at.pick(side, DEEP, LANES - DEEP)
            strips = []
            for i in range(3):
                acc = jnp.zeros((ROWS, LANES), F32)
                for p in range(at.slots):
                    if i == 2 and p in (0, at.slots - 1):
                        continue
                    z = at.plane(p)
                    value = psi[i, z, rows, :] if i < 2 else dis[z, rows, :].astype(F32)
                    acc = jnp.where(here[p], roll(value, shift + WIDE * p, 1), acc)
                own[side][i, rows, :] = acc
                strips.append(acc)
            message[side][rows, :] = strip_message(at, side, off, back, *strips)


def strip_message(at, side, off, back, a, b, level):
    a, level = roll(a, back, 1), roll(level, LANES - back, 1)
    place = at.pick(side, 8 - off, off)
    return jnp.where(place < DEEP, a, jnp.where(place < 2 * DEEP, b, level))


def corner_kernel(dims, got, other, *refs):
    at = Place(dims)
    message = refs[: at.sides]
    outer, whole = refs[at.sides : 2 * at.sides], refs[2 * at.sides :]
    slot, off = strip_lanes()
    tiles = [unpack_rows(at, p, got, other) for p in range(1, at.slots - 1)]
    for side in range(at.sides):
        shift = at.pick(side, DEEP, LANES - at.cols + 2 * DEEP)
        back = at.pick(side, DEEP, LANES - DEEP)
        strips = []
        for i in range(3):
            acc = jnp.zeros((ROWS, LANES), F32)
            for p in range(1, at.slots - 1):
                acc = jnp.where(slot == p, roll(tiles[p - 1][i], shift + WIDE * p, 1), acc)
            strips.append(acc)
            outer[side][i] = acc
        whole[side][: at.rows] = message[side][...]
        whole[side][at.rows :] = strip_message(at, side, off, back, *strips)


def put(ref, lead, value, base):
    ref[lead + (pl.ds(base, ROWS), slice(None))] = value


def get(ref, lead, base):
    return ref[lead + (pl.ds(base, ROWS), slice(None))]


def tile_of(ref, lead, base):
    return [get(ref, (i,) + lead, base) for i in range(2)]


def x_pair(ref, lead, base, outer, end):
    if outer:
        return tile_of(ref, lead, 1), tile_of(ref, lead, end - 1)
    return tile_of(ref, lead, base + 1), tile_of(ref, lead, base - 1)


def put_field(ref, lead, values, base, outer, end):
    for i in range(2):
        put(ref, (i,) + lead, values[i], base)
        if outer:
            put(ref, (i,) + lead, values[i], end)


class Stages:
    def __init__(self, at, w, k, lw, coef, scales):
        self.at, self.w, self.k, self.lw, self.coef = at, w, k, lw, coef
        self.end = ROWS + at.rows
        sub, lane = iota(0), iota(1)
        self.outer_row = at.outer_row(sub)
        self.row_ok = at.on_grid(self.outer_row)
        self.ys = at.ycoord(lane)
        self.cx = [factors(SPIN * self.ys, LAP, scale) for scale in scales]
        self.scales = scales
        has_next = jnp.where(lane < at.cols - 1, 1.0, 0.0)
        has_prev = jnp.where(lane > 0, 1.0, 0.0)
        for j in range(at.tiles + 1):
            xs = at.xcoord(self.outer_row if j == 0 else sub + (j - 1) * ROWS)
            here = slice(j * ROWS, (j + 1) * ROWS)
            for which, scale in enumerate(scales):
                for i, factor in enumerate(factors(SPIN * xs, LAP, scale)):
                    coef[4 * which + i, here] = factor * has_next
                    coef[4 * which + 2 + i, here] = factor * has_prev

    def linear(self, ref, q, base, outer, lap_z, which=0):
        c = tile_of(ref, (q,), base)
        xp, xm = x_pair(ref, (q,), base, outer, self.end)
        zp = tile_of(ref, (q + 1,), base)
        zm = tile_of(ref, (q - 1,), base)
        yp = [roll(c[i], -1, 1) for i in range(2)]
        ym = [roll(c[i], 1, 1) for i in range(2)]
        cyp = [get(self.coef, (4 * which + i,), base) for i in (0, 1)]
        cym = [get(self.coef, (4 * which + i,), base) for i in (2, 3)]
        lap = self.scales[which] * LAP
        return c, linear(c, xp, xm, yp, ym, zp, zm, cyp, cym, self.cx[which], lap, lap if lap_z is None else lap_z)

    def one(self, p, j, pot, lap_z):
        base, outer = j * ROWS, j == 0
        c, lin = self.linear(self.w, p, base, outer, lap_z)
        slope = first_slope(c, lin, pot)
        if outer:
            slope = [jnp.where(self.row_ok, s, 0.0) for s in slope]
        put_field(self.k, (p - 1,), slope, base, outer, self.end)
        put_field(self.lw, (p - 1,), lin, base, False, self.end)
        return c, slope, lin

    def lap_of(self, p):
        return jnp.where(self.at.valid(p), self.scales[0] * LAP, 0.0)


def slopes_kernel(dims, psi, pot, w, k, lw, ready, coef):
    at = Place(dims)
    stages = Stages(at, w, k, lw, coef, (0.5,))

    def fill(p):
        sure = DEEP <= p < at.slots - DEEP
        for j in range(1, at.tiles + 1):
            for i in range(2):
                value = psi[i, at.plane(p), (j - 1) * ROWS : j * ROWS, :]
                put(w, (i, p), value if sure else jnp.where(at.valid(p), value, 0.0), j * ROWS)

    fill(0)
    fill(1)
    for p in range(1, at.slots - 1):
        fill(p + 1)
        lap_p = stages.lap_of(p)
        for j in range(2, at.tiles):
            here = get(pot, (p - 1,), (j - 1) * ROWS)
            values = stages.one(p, j, here, lap_p)
            if DEEP <= p < DEEP + AHEAD:
                for i, part in enumerate(powers(*values, here)):
                    put(ready, (i, p - DEEP), part, (j - 2) * ROWS)


def step_kernel(dims, pot, got, other, ready, w_in, k_in, lw_in, part, w, k, lw, outer_pot, zf, coef):
    at = Place(dims)
    slots, tiles, rows = at.slots, at.tiles, at.rows
    stages = Stages(at, w, k, lw, coef, (0.5, 1.0))
    end, ys = stages.end, stages.ys
    table = level_table()

    zero = jnp.zeros((ROWS, LANES), F32)
    xs = at.xcoord(stages.outer_row)
    dist = (0.5 * STEP) * (xs * xs + ys * ys)
    for p in range(1, slots - 1):
        a, b, level = unpack_rows(at, p, got, other)
        put_field(w, (p,), (a, b), 0, True, end)
        zs = at.zcoord(p)
        outer_pot[p - 1] = look_up(table + (0.5 * STEP) * (zs * zs), to_level(level)) + dist
    for p in (0, slots - 1):
        put_field(w, (p,), (zero, zero), 0, True, end)

    def potential(p, j):
        return get(pot, (p - 1,), (j - 1) * ROWS) if j else outer_pot[p - 1]

    def two_tile(p, j, full, lap_z):
        base, outer = j * ROWS, j == 0
        c, lin = stages.linear(k, p - 1, base, outer, lap_z)
        here, field = potential(p, j), tile_of(w, (p,), base)
        if DEEP <= p < DEEP + AHEAD and 2 <= j < tiles:
            parts = [get(ready, (i, p - DEEP), (j - 2) * ROWS) for i in range(8)]
        else:
            parts = powers(field, c, tile_of(lw, (p - 1,), base), here)
        z, rest = second_stage(field, parts, lin, here, full and not outer)
        if outer:
            z = [jnp.where(stages.row_ok, s, 0.0) for s in z]
        put_field(zf, (p - 2,), z, base, outer, end)
        if rest is not None:
            for i in range(2):
                put(part, (i, p - DEEP), rest[i], base - ROWS)

    def three_tile(p, j):
        base = j * ROWS
        _, lin = stages.linear(zf, p - 2, base, False, None, 1)
        for i in range(2):
            lead = (i, p - DEEP)
            put(part, lead, get(part, lead, base - ROWS) + lin[i], base - ROWS)

    last = slots - 2
    for p in range(1, last + 1):
        two = None if p < DEEP else p not in (DEEP, last)
        lap_p = stages.lap_of(p)
        lap_before = None if two else stages.lap_of(p - 1)
        for j in range(tiles + 1):
            if j < 2 or j == tiles:
                stages.one(p, j, potential(p, j), lap_p)
            if two is not None:
                two_tile(p - 1, j, two, lap_before)
            if p > DEEP + 1 and j:
                three_tile(p - 2, j)


def strip_kernel(dims, part, *refs):
    at = Place(dims)
    own, outer_own, got = (refs[i * at.sides : (i + 1) * at.sides] for i in range(3))
    out, result, sw, sk, sl, sp, sz, coef, osem = refs[3 * at.sides :]
    tiles, rows, cols = at.tiles, at.rows, at.cols
    end = ROWS + rows
    sub = iota(0)
    lane = iota(1)
    slot, off = strip_lanes()
    table = level_table()
    outer_row = at.outer_row(sub)
    inside = lambda index, count: (index >= 0) & (index < count)
    row_ok = at.on_grid(outer_row)
    zs = at.zcoord(slot)

    for j in range(tiles + 1):
        xs = at.xcoord(outer_row if j == 0 else sub + (j - 1) * ROWS)
        here = slice(j * ROWS, (j + 1) * ROWS)
        coef[0, here], coef[1, here] = factors(SPIN * xs, LAP, 0.5)
        coef[2, here], coef[3, here] = factors(SPIN * xs, LAP, 1.0)
        coef[4, here] = (0.5 * STEP) * (xs * xs)

    for side in range(at.sides):
        col = off + at.pick(side, -DEEP, cols - 2 * DEEP)
        ok = inside(at.z0 + slot, at.planes) & inside(at.py * cols + col, cols * at.npy)
        ys = at.ycoord(col)
        cx = factors(SPIN * ys, LAP, 0.5)
        far = (0.5 * STEP) * (zs * zs + ys * ys)
        halo = at.pick(side, off, 8 - off) < DEEP
        back_b = at.pick(side, LANES - DEEP, DEEP)
        back_d = at.pick(side, LANES - 2 * DEEP, 2 * DEEP)

        def strip_load(base, outer):
            if outer:
                new = got[side][rows:, :]
                mine = [outer_own[side][i] for i in range(3)]
            else:
                here = pl.ds(base - ROWS, ROWS)
                new = got[side][here, :]
                mine = [own[side][i, here, :] for i in range(3)]
            a = jnp.where(halo, new, mine[0])
            b = jnp.where(halo, roll(new, back_b, 1), mine[1])
            level = to_level(jnp.where(halo, roll(new, back_d, 1), mine[2]))
            put_field(sw, (side,), (a, b), base, outer, end)
            put(sp, (side,), look_up(table, level) + (far + get(coef, (4,), base)), base)

        def strip_linear(ref, base, outer):
            c = tile_of(ref, (side,), base)
            xp, xm = x_pair(ref, (side,), base, outer, end)
            yp, ym, zp, zm = [[roll(c[i], s, 1) for i in range(2)] for s in (-1, 1, -WIDE, WIDE)]
            cy = [get(coef, (i,), base) for i in (0, 1)]
            return c, linear(c, xp, xm, yp, ym, zp, zm, cy, cy, cx, 0.5 * LAP, 0.5 * LAP)

        def keep(values, outer):
            good = (ok & row_ok) if outer else ok
            return [jnp.where(good, s, 0.0) for s in values]

        def strip_one(base, outer):
            c, lin = strip_linear(sw, base, outer)
            slope = first_slope(c, lin, get(sp, (side,), base))
            put_field(sk, (side,), keep(slope, outer), base, outer, end)
            put_field(sl, (side,), lin, base, False, end)

        def strip_two(base, outer):
            c, lin = strip_linear(sk, base, outer)
            field, here = tile_of(sw, (side,), base), get(sp, (side,), base)
            parts = powers(field, c, tile_of(sl, (side,), base), here)
            z, rest = second_stage(field, parts, lin, here, not outer)
            put_field(sz, (side,), keep(z, outer), base, outer, end)
            if rest is not None:
                put_field(sl, (side,), rest, base, False, end)

        for stage in (strip_load, strip_one, strip_two):
            for j in range(tiles + 1):
                stage(j * ROWS, j == 0)

    def out_copy(p):
        return pltpu.make_async_copy(result.at[:, p], out.at[:, p], osem.at[p])

    for side in range(at.sides):
        ys = at.ycoord(off + at.pick(side, -DEEP, cols - 2 * DEEP))
        cx = factors(SPIN * ys, LAP, 1.0)
        for j in range(1, tiles + 1):
            base = j * ROWS
            c = tile_of(sz, (side,), base)
            xp, xm = x_pair(sz, (side,), base, False, end)
            yp, ym, zp, zm = [[roll(c[i], s, 1) for i in range(2)] for s in (-1, 1, -WIDE, WIDE)]
            cy = [get(coef, (i,), base) for i in (2, 3)]
            lin = linear(c, xp, xm, yp, ym, zp, zm, cy, cy, cx, LAP, LAP)
            put_field(sk, (side,), [get(sl, (i, side), base) + lin[i] for i in range(2)], base, False, end)

    for p in range(at.share):
        from_lane = DEEP + WIDE * (p + DEEP)
        for j in range(tiles):
            for i in range(2):
                value = get(part, (i, p), j * ROWS)
                for side in range(at.sides):
                    shift = (at.pick(side, 0, cols - DEEP) + 2 * LANES - from_lane) % LANES
                    face = at.pick(side, lane, cols - 1 - lane) < DEEP
                    value = jnp.where(face, roll(get(sk, (i, side), (j + 1) * ROWS), shift, 1), value)
                put(result, (i, p), value, j * ROWS)
        out_copy(p).start()
    for p in range(at.share):
        out_copy(p).wait()


def local(npx, npy, psi, disorder):
    planes, rows, cols = psi.shape[1:]
    share = planes // lax.axis_size("section")
    two = npy == 2
    sides = 1 if two else 2
    slots = share + 2 * DEEP
    tall = rows + ROWS
    dims = (planes, share, rows, cols, npx, npy)
    hbm = pl.BlockSpec(memory_space=pltpu.HBM)
    vmem = pl.BlockSpec(memory_space=pltpu.VMEM)
    f32 = lambda *shape: jax.ShapeDtypeStruct(shape, F32)
    scratch = lambda *shape: pltpu.VMEM(shape, F32)
    levels = lambda *shape: pltpu.VMEM(shape, jnp.int32)
    dma = lambda *shape: pltpu.SemaphoreType.DMA(shape)

    def call(kernel, name, room, ins, outs, out_specs, scratches, flops, moved, *args, aliases={}):
        return pl.pallas_call(
            functools.partial(kernel, dims),
            out_shape=outs,
            in_specs=ins,
            out_specs=out_specs,
            scratch_shapes=scratches,
            input_output_aliases=aliases,
            compiler_params=pltpu.CompilerParams(vmem_limit_bytes=room * 1024 * 1024),
            cost_estimate=pl.CostEstimate(flops=flops, bytes_accessed=moved, transcendentals=0),
            name=name,
        )(*args)

    def send(value, pairs):
        return lax.ppermute(value, ("px", "py"), pairs)

    sections = lax.axis_size("section")
    place = lambda s, i, j: (s * npx + i) * npy + j
    row_pairs = []
    for s in range(sections):
        for i in range(npx):
            partner = i ^ 1 if s % 2 == 0 else ((i + 1) ^ 1) - 1
            for j in range(npy):
                to = (partner, j) if 0 <= partner < npx else (i, j ^ 1)
                if to[1] < npy:
                    row_pairs.append((place(s, i, j), place(s, *to)))
    core_pairs = [(s, s ^ 1) for s in range(sections)]

    cells = share * rows * cols
    block = 4 * slots * rows * cols
    pair_planes = 2 * share + 2 * DEEP - 2
    edges = call(
        rows_kernel, "pack_rows", 52, [hbm] * 2, f32(pair_planes, ROWS, LANES), vmem,
        [scratch(2, pair_planes, ROWS, LANES), levels(pair_planes, ROWS, LANES), dma(), dma()],
        cells // 16, block // 8, psi, disorder,
    )
    edges = lax.ppermute(edges, ("section", "px", "py"), row_pairs)

    packed = call(
        columns_kernel, "pack_columns", 24, [vmem] * 2,
        [f32(slots - 2, rows, cols)] + [f32(3, rows, LANES)] * sides + [f32(rows, LANES)] * sides,
        [vmem] * (1 + 2 * sides), [], 12 * cells, 3 * block, psi, disorder,
    )
    edges, packed = lax.optimization_barrier((edges, packed))
    pot = packed[0]
    own, message = packed[1 : 1 + sides], packed[1 + sides :]
    others = lax.ppermute(edges, "section", core_pairs)
    field = lambda depth: (2, depth, tall + ROWS, LANES)
    begun = call(
        slopes_kernel, "slopes", 24, [vmem] * 2,
        [f32(*field(n)) for n in (slots, slots - 2, slots - 2)] + [f32(8, AHEAD, rows - 2 * ROWS, LANES)], [vmem] * 4,
        [scratch(4, tall, LANES)], 60 * cells, 4 * block, psi, pot,
    )
    others, begun = lax.optimization_barrier((others, begun))

    made = call(
        corner_kernel, "pack_corners", 24, [vmem] * (2 + sides), [f32(3, ROWS, LANES)] * sides + [f32(tall, LANES)] * sides,
        [vmem] * (2 * sides), [], cells // 8, block // 16, edges, others, *message,
    )
    outer, message = made[:sides], made[sides:]
    right = [(i * npy + j, i * npy + j + 1) for i in range(npx) for j in range(npy - 1)]
    left = [(b, a) for a, b in right]
    if two:
        got = [send(message[0], right + left)]
    else:
        got = [send(message[1], right), send(message[0], left)]

    part = call(
        step_kernel, "step", 24, [vmem] * 7,
        [f32(2, share, rows, cols)] + [f32(*field(n)) for n in (slots, slots - 2, slots - 2)], [vmem] * 4,
        [scratch(slots - 2, ROWS, LANES), scratch(*field(slots - 4)), scratch(8, tall, LANES)],
        240 * cells, 4 * block, pot, edges, others, begun[3], *begun[:3], aliases={4: 1, 5: 2, 6: 3},
    )[0]
    return call(
        strip_kernel, "strips", 24, [vmem] * (1 + 3 * sides), f32(2, share, rows, cols), hbm,
        [
            scratch(2, share, rows, cols),
            scratch(*field(sides)),
            scratch(*field(sides)),
            scratch(*field(sides)),
            scratch(sides, tall, LANES),
            scratch(*field(sides)),
            scratch(5, tall, LANES),
            dma(share),
        ],
        30 * cells, 2 * block, part, *own, *outer, *got,
    )


def solution(mesh):
    in_specs = (P(None, None, "px", "py"), P(None, "px", "py"))
    out_specs = P(None, "section", "px", "py")
    run = functools.partial(local, mesh.shape["px"], mesh.shape["py"])
    return jax.shard_map(run, mesh=mesh, in_specs=in_specs, out_specs=out_specs, check_vma=False)
```

```python
import functools
import math

import jax
import jax.numpy as jnp
from jax import lax
from jax.experimental import pallas as pl
from jax.experimental.pallas import tpu as pltpu
from jax.sharding import PartitionSpec as P

LEVELS = 16
STEP = 0.05
ROTATION = 0.8
COUPLING = 0.25

ROOT_OUT = math.sqrt((3.0 + 2.0 * math.sqrt(1.2)) / 7.0)
ROOT_IN = math.sqrt((3.0 - 2.0 * math.sqrt(1.2)) / 7.0)
WEIGHT_OUT = (18.0 - math.sqrt(30.0)) / 36.0
WEIGHT_IN = 1.0 - WEIGHT_OUT

LAP = 0.5 * STEP
SPIN = 0.5 * STEP * ROTATION
KAPPA = 0.5 * STEP * COUPLING

DEEP = 3
WIDE = 3 * DEEP
LANES = 128
ROWS = 8
AHEAD = 6
F32 = jnp.float32


def iota(dim):
    return lax.broadcasted_iota(jnp.int32, (ROWS, LANES), dim)


def roll(value, shift, axis):
    return pltpu.roll(value, shift % value.shape[axis] if isinstance(shift, int) else shift, axis)


def strip_lanes():
    lane = iota(1)
    slot = (lane * 57) >> 9
    return slot, lane - WIDE * slot


def level_table():
    lane = iota(1)
    table = jnp.zeros((ROWS, LANES), F32)
    for level in range(LEVELS):
        table = jnp.where(lane == level, F32(0.75 * STEP * math.sin(2.3 * level + 0.4)), table)
    return table


def look_up(table, level):
    return jnp.take_along_axis(table, level, axis=1, mode="promise_in_bounds")


def to_level(value):
    return jnp.clip(value, 0.0, LEVELS - 1.0).astype(jnp.int32)


def factors(spin, lap, scale):
    return scale * (spin + lap), scale * (spin - lap)


def linear(c, xp, xm, yp, ym, zp, zm, cyp, cym, cx, lap, lap_z):
    diag = [lap_z * (zp[i] + zm[i]) - (6.0 * lap) * c[i] for i in range(2)]
    real = cyp[1] * yp[0] - cym[0] * ym[0] - cx[0] * xp[0] + cx[1] * xm[0] - diag[0]
    imag = cyp[0] * yp[1] - cym[1] * ym[1] - cx[1] * xp[1] + cx[0] * xm[1] + diag[1]
    return real, imag


def first_slope(w, lin, pot):
    g = pot + KAPPA * (w[0] * w[0] + w[1] * w[1])
    return lin[0] + g * w[1], lin[1] - g * w[0]


def powers(w, k, lin_w, pot):
    m = [w[i] + k[i] for i in range(2)]
    p0 = pot + KAPPA * (m[0] * m[0] + m[1] * m[1])
    p1 = (2.0 * KAPPA) * (m[0] * k[0] + m[1] * k[1])
    p2 = KAPPA * (k[0] * k[0] + k[1] * k[1])
    return (
        lin_w[0] + p0 * m[1],
        lin_w[1] - p0 * m[0],
        p0 * k[1] + p1 * m[1],
        -(p0 * k[0] + p1 * m[0]),
        p1 * k[1] + p2 * m[1],
        p1 * k[0] + p2 * m[0],
        p2 * k[1],
        p2 * k[0],
    )


def second_stage(w, parts, lin_k, pot, full):
    f0 = parts[0] + lin_k[0], parts[1] + lin_k[1]
    f1 = parts[2] + lin_k[0], parts[3] + lin_k[1]
    f2, f3 = parts[4:6], parts[6:8]
    sign = 1.0, -1.0
    base = [w[i] + f0[i] + (sign[i] / 3.0) * f2[i] for i in range(2)]
    z = [base[i] - (1.0 / 3.0) * f1[i] - (sign[i] / 5.0) * f3[i] for i in range(2)]
    if not full:
        return z, None
    square = ROOT_OUT * ROOT_OUT
    even_out = [
        base[i] + (0.5 * (square - 1.0)) * f1[i] + (sign[i] * 0.25 * (square * square - 1.0)) * f3[i] for i in range(2)
    ]
    even_in = [z[i] + (WEIGHT_OUT / WEIGHT_IN) * (z[i] - even_out[i]) for i in range(2)]
    total = [(pot + pot) * z[i] for i in range(2)]
    for even, square, weight in (
        (even_out, ROOT_OUT * ROOT_OUT, WEIGHT_OUT),
        (even_in, ROOT_IN * ROOT_IN, WEIGHT_IN),
    ):
        odd = [f0[i] + (sign[i] * square / 3.0) * f2[i] for i in range(2)]
        scale = 2.0 * KAPPA * weight
        p = scale * (even[0] * even[0] + even[1] * even[1]) + (scale * square) * (odd[0] * odd[0] + odd[1] * odd[1])
        q = (2.0 * scale * square) * (even[0] * odd[0] + even[1] * odd[1])
        total = [total[i] + p * even[i] + q * odd[i] for i in range(2)]
    return z, (w[0] + total[1], w[1] - total[0])


class Place:
    def __init__(self, dims):
        self.planes, self.share, self.rows, self.cols, self.npx, self.npy = dims
        self.slots = self.share + 2 * DEEP
        self.tiles = self.rows // ROWS
        self.two = self.npy == 2
        self.sides = 1 if self.two else 2
        self.z0 = lax.axis_index("section") * self.share - DEEP
        self.px = lax.axis_index("px")
        self.py = lax.axis_index("py")
        self.core = lax.axis_index("section") % 2
        self.sends_up = (self.px + self.core) % 2 == 0
        self.pair_planes = 2 * self.share + 2 * DEEP - 2

    def valid(self, p):
        return (self.z0 + p >= 0) & (self.z0 + p < self.planes)

    def outer_row(self, sub):
        return jnp.where(sub >= 4, sub - ROWS, self.rows + sub)

    def on_grid(self, row):
        row = self.px * self.rows + row
        return (row >= 0) & (row < self.rows * self.npx)

    def plane(self, p):
        return jnp.clip(self.z0 + p, 0, self.planes - 1)

    def is_left(self, side):
        return self.py == 1 if self.two else side == 0

    def pick(self, side, left, right):
        if self.two:
            return jnp.where(self.py == 1, left, right)
        return left if side == 0 else right

    def coordinate(self, index, count):
        return (index.astype(F32) - (count - 1) / 2.0) / (count / 2.0)

    def xcoord(self, row):
        return self.coordinate(self.px * self.rows + row, self.rows * self.npx)

    def ycoord(self, col):
        return self.coordinate(self.py * self.cols + col, self.cols * self.npy)

    def zcoord(self, slot):
        return self.coordinate(self.z0 + slot, self.planes)


def unpack_rows(at, p, got, other):
    sub = iota(0)
    index = p - 1 + at.core * at.share
    got, other = got[index], other[index]
    up = jnp.where(at.sends_up, other, got)
    dn = jnp.where(at.sends_up, got, other)
    upper = sub >= 4
    ok = at.on_grid(at.outer_row(sub))
    a = jnp.where(ok, jnp.where(upper, up, dn), 0.0)
    b = jnp.where(ok, jnp.where(upper, roll(up, 3, 0), roll(dn, -3, 0)), 0.0)
    level = jnp.where(upper, roll(up, -2, 0), roll(dn, 2, 0))
    return a, b, level


def rows_kernel(dims, psi, dis, message, vpsi, vdis, psem, dsem):
    at = Place(dims)
    start = at.z0 - at.core * at.share + 1
    window = jnp.clip(start, 0, at.planes - at.pair_planes)
    edge = pl.ds(pl.multiple_of(jnp.where(at.sends_up, at.rows - ROWS, 0), ROWS), ROWS)
    span = pl.ds(window, at.pair_planes)
    copies = []
    half = at.pair_planes // 2
    for h in range(2):
        span, to = pl.ds(window + h * half, half), pl.ds(h * half, half)
        for i in range(2):
            copies.append(pltpu.make_async_copy(psi.at[i, span, edge], vpsi.at[i, to], psem.at[h, i]))
        copies.append(pltpu.make_async_copy(dis.at[span, edge], vdis.at[to], dsem.at[h]))
    for copy in copies:
        copy.start()
    sub = iota(0)
    place = jnp.where(at.sends_up, ROWS - 1 - sub, sub)
    shift_b = jnp.where(at.sends_up, ROWS - 3, 3)
    shift_d = jnp.where(at.sends_up, 2, ROWS - 2)
    for copy in copies:
        copy.wait()
    for t in range(at.pair_planes):
        z = start + t
        index = jnp.clip(z - window, 0, at.pair_planes - 1)
        a, b, level = vpsi[0, index], vpsi[1, index], vdis[index].astype(F32)
        value = jnp.where(place < 3, a, jnp.where(place < 6, roll(b, shift_b, 0), roll(level, shift_d, 0)))
        message[t] = jnp.where((z >= 0) & (z < at.planes), value, 0.0)


def columns_kernel(dims, psi, dis, pot, *refs):
    at = Place(dims)
    own, message = refs[: at.sides], refs[at.sides :]
    slot, off = strip_lanes()
    sub = iota(0)
    table = level_table()
    ys = at.ycoord(iota(1))
    here = [slot == jnp.where(at.valid(p), p, -1) for p in range(at.slots)]
    level_at = [table + (0.5 * STEP) * (at.zcoord(p) * at.zcoord(p)) for p in range(at.slots)]
    for j in range(at.tiles):
        rows = slice(j * ROWS, (j + 1) * ROWS)
        xs = at.xcoord(sub + j * ROWS)
        dist = (0.5 * STEP) * (xs * xs + ys * ys)
        for p in range(1, at.slots - 1):
            pot[p - 1, rows, :] = look_up(level_at[p], dis[at.plane(p), rows, :]) + dist
        for side in range(at.sides):
            shift = at.pick(side, DEEP, LANES - at.cols + 2 * DEEP)
            back = at.pick(side, DEEP, LANES - DEEP)
            strips = []
            for i in range(3):
                acc = jnp.zeros((ROWS, LANES), F32)
                for p in range(at.slots):
                    if i == 2 and p in (0, at.slots - 1):
                        continue
                    z = at.plane(p)
                    value = psi[i, z, rows, :] if i < 2 else dis[z, rows, :].astype(F32)
                    acc = jnp.where(here[p], roll(value, shift + WIDE * p, 1), acc)
                own[side][i, rows, :] = acc
                strips.append(acc)
            message[side][rows, :] = strip_message(at, side, off, back, *strips)


def strip_message(at, side, off, back, a, b, level):
    a, level = roll(a, back, 1), roll(level, LANES - back, 1)
    place = at.pick(side, 8 - off, off)
    return jnp.where(place < DEEP, a, jnp.where(place < 2 * DEEP, b, level))


def corner_kernel(dims, got, other, *refs):
    at = Place(dims)
    message = refs[: at.sides]
    outer, whole = refs[at.sides : 2 * at.sides], refs[2 * at.sides :]
    slot, off = strip_lanes()
    tiles = [unpack_rows(at, p, got, other) for p in range(1, at.slots - 1)]
    for side in range(at.sides):
        shift = at.pick(side, DEEP, LANES - at.cols + 2 * DEEP)
        back = at.pick(side, DEEP, LANES - DEEP)
        strips = []
        for i in range(3):
            acc = jnp.zeros((ROWS, LANES), F32)
            for p in range(1, at.slots - 1):
                acc = jnp.where(slot == p, roll(tiles[p - 1][i], shift + WIDE * p, 1), acc)
            strips.append(acc)
            outer[side][i] = acc
        whole[side][: at.rows] = message[side][...]
        whole[side][at.rows :] = strip_message(at, side, off, back, *strips)


def put(ref, lead, value, base):
    ref[lead + (pl.ds(base, ROWS), slice(None))] = value


def get(ref, lead, base):
    return ref[lead + (pl.ds(base, ROWS), slice(None))]


def tile_of(ref, lead, base):
    return [get(ref, (i,) + lead, base) for i in range(2)]


def x_pair(ref, lead, base, outer, end):
    if outer:
        return tile_of(ref, lead, 1), tile_of(ref, lead, end - 1)
    return tile_of(ref, lead, base + 1), tile_of(ref, lead, base - 1)


def put_field(ref, lead, values, base, outer, end):
    for i in range(2):
        put(ref, (i,) + lead, values[i], base)
        if outer:
            put(ref, (i,) + lead, values[i], end)


class Stages:
    def __init__(self, at, w, k, lw, coef, scales):
        self.at, self.w, self.k, self.lw, self.coef = at, w, k, lw, coef
        self.end = ROWS + at.rows
        sub, lane = iota(0), iota(1)
        self.outer_row = at.outer_row(sub)
        self.row_ok = at.on_grid(self.outer_row)
        self.ys = at.ycoord(lane)
        self.cx = [factors(SPIN * self.ys, LAP, scale) for scale in scales]
        self.scales = scales
        has_next = jnp.where(lane < at.cols - 1, 1.0, 0.0)
        has_prev = jnp.where(lane > 0, 1.0, 0.0)
        for j in range(at.tiles + 1):
            xs = at.xcoord(self.outer_row if j == 0 else sub + (j - 1) * ROWS)
            here = slice(j * ROWS, (j + 1) * ROWS)
            for which, scale in enumerate(scales):
                for i, factor in enumerate(factors(SPIN * xs, LAP, scale)):
                    coef[4 * which + i, here] = factor * has_next
                    coef[4 * which + 2 + i, here] = factor * has_prev

    def linear(self, ref, q, base, outer, lap_z, which=0):
        c = tile_of(ref, (q,), base)
        xp, xm = x_pair(ref, (q,), base, outer, self.end)
        zp = tile_of(ref, (q + 1,), base)
        zm = tile_of(ref, (q - 1,), base)
        yp = [roll(c[i], -1, 1) for i in range(2)]
        ym = [roll(c[i], 1, 1) for i in range(2)]
        cyp = [get(self.coef, (4 * which + i,), base) for i in (0, 1)]
        cym = [get(self.coef, (4 * which + i,), base) for i in (2, 3)]
        lap = self.scales[which] * LAP
        return c, linear(c, xp, xm, yp, ym, zp, zm, cyp, cym, self.cx[which], lap, lap if lap_z is None else lap_z)

    def one(self, p, j, pot, lap_z):
        base, outer = j * ROWS, j == 0
        c, lin = self.linear(self.w, p, base, outer, lap_z)
        slope = first_slope(c, lin, pot)
        if outer:
            slope = [jnp.where(self.row_ok, s, 0.0) for s in slope]
        put_field(self.k, (p - 1,), slope, base, outer, self.end)
        put_field(self.lw, (p - 1,), lin, base, False, self.end)
        return c, slope, lin

    def lap_of(self, p):
        return jnp.where(self.at.valid(p), self.scales[0] * LAP, 0.0)


def slopes_kernel(dims, psi, pot, w, k, lw, ready, coef):
    at = Place(dims)
    stages = Stages(at, w, k, lw, coef, (0.5,))

    def fill(p):
        sure = DEEP <= p < at.slots - DEEP
        for j in range(1, at.tiles + 1):
            for i in range(2):
                value = psi[i, at.plane(p), (j - 1) * ROWS : j * ROWS, :]
                put(w, (i, p), value if sure else jnp.where(at.valid(p), value, 0.0), j * ROWS)

    fill(0)
    fill(1)
    for p in range(1, at.slots - 1):
        fill(p + 1)
        lap_p = stages.lap_of(p)
        for j in range(2, at.tiles):
            here = get(pot, (p - 1,), (j - 1) * ROWS)
            values = stages.one(p, j, here, lap_p)
            if DEEP <= p < DEEP + AHEAD:
                for i, part in enumerate(powers(*values, here)):
                    put(ready, (i, p - DEEP), part, (j - 2) * ROWS)


def step_kernel(dims, pot, got, other, ready, w_in, k_in, lw_in, part, w, k, lw, outer_pot, zf, coef):
    at = Place(dims)
    slots, tiles, rows = at.slots, at.tiles, at.rows
    stages = Stages(at, w, k, lw, coef, (0.5, 1.0))
    end, ys = stages.end, stages.ys
    table = level_table()

    zero = jnp.zeros((ROWS, LANES), F32)
    xs = at.xcoord(stages.outer_row)
    dist = (0.5 * STEP) * (xs * xs + ys * ys)
    for p in range(1, slots - 1):
        a, b, level = unpack_rows(at, p, got, other)
        put_field(w, (p,), (a, b), 0, True, end)
        zs = at.zcoord(p)
        outer_pot[p - 1] = look_up(table + (0.5 * STEP) * (zs * zs), to_level(level)) + dist
    for p in (0, slots - 1):
        put_field(w, (p,), (zero, zero), 0, True, end)

    def potential(p, j):
        return get(pot, (p - 1,), (j - 1) * ROWS) if j else outer_pot[p - 1]

    def two_tile(p, j, full, lap_z):
        base, outer = j * ROWS, j == 0
        c, lin = stages.linear(k, p - 1, base, outer, lap_z)
        here, field = potential(p, j), tile_of(w, (p,), base)
        if DEEP <= p < DEEP + AHEAD and 2 <= j < tiles:
            parts = [get(ready, (i, p - DEEP), (j - 2) * ROWS) for i in range(8)]
        else:
            parts = powers(field, c, tile_of(lw, (p - 1,), base), here)
        z, rest = second_stage(field, parts, lin, here, full and not outer)
        if outer:
            z = [jnp.where(stages.row_ok, s, 0.0) for s in z]
        put_field(zf, (p - 2,), z, base, outer, end)
        if rest is not None:
            for i in range(2):
                put(part, (i, p - DEEP), rest[i], base - ROWS)

    def three_tile(p, j):
        base = j * ROWS
        _, lin = stages.linear(zf, p - 2, base, False, None, 1)
        for i in range(2):
            lead = (i, p - DEEP)
            put(part, lead, get(part, lead, base - ROWS) + lin[i], base - ROWS)

    last = slots - 2
    for p in range(1, last + 1):
        two = None if p < DEEP else p not in (DEEP, last)
        lap_p = stages.lap_of(p)
        lap_before = None if two else stages.lap_of(p - 1)
        for j in range(tiles + 1):
            if j < 2 or j == tiles:
                stages.one(p, j, potential(p, j), lap_p)
            if two is not None:
                two_tile(p - 1, j, two, lap_before)
            if p > DEEP + 1 and j:
                three_tile(p - 2, j)


def strip_kernel(dims, part, *refs):
    at = Place(dims)
    own, outer_own, got = (refs[i * at.sides : (i + 1) * at.sides] for i in range(3))
    out, result, sw, sk, sl, sp, sz, coef, osem = refs[3 * at.sides :]
    tiles, rows, cols = at.tiles, at.rows, at.cols
    end = ROWS + rows
    sub = iota(0)
    lane = iota(1)
    slot, off = strip_lanes()
    table = level_table()
    outer_row = at.outer_row(sub)
    inside = lambda index, count: (index >= 0) & (index < count)
    row_ok = at.on_grid(outer_row)
    zs = at.zcoord(slot)

    for j in range(tiles + 1):
        xs = at.xcoord(outer_row if j == 0 else sub + (j - 1) * ROWS)
        here = slice(j * ROWS, (j + 1) * ROWS)
        coef[0, here], coef[1, here] = factors(SPIN * xs, LAP, 0.5)
        coef[2, here], coef[3, here] = factors(SPIN * xs, LAP, 1.0)
        coef[4, here] = (0.5 * STEP) * (xs * xs)

    for side in range(at.sides):
        col = off + at.pick(side, -DEEP, cols - 2 * DEEP)
        ok = inside(at.z0 + slot, at.planes) & inside(at.py * cols + col, cols * at.npy)
        ys = at.ycoord(col)
        cx = factors(SPIN * ys, LAP, 0.5)
        far = (0.5 * STEP) * (zs * zs + ys * ys)
        halo = at.pick(side, off, 8 - off) < DEEP
        back_b = at.pick(side, LANES - DEEP, DEEP)
        back_d = at.pick(side, LANES - 2 * DEEP, 2 * DEEP)

        def strip_load(base, outer):
            if outer:
                new = got[side][rows:, :]
                mine = [outer_own[side][i] for i in range(3)]
            else:
                here = pl.ds(base - ROWS, ROWS)
                new = got[side][here, :]
                mine = [own[side][i, here, :] for i in range(3)]
            a = jnp.where(halo, new, mine[0])
            b = jnp.where(halo, roll(new, back_b, 1), mine[1])
            level = to_level(jnp.where(halo, roll(new, back_d, 1), mine[2]))
            put_field(sw, (side,), (a, b), base, outer, end)
            put(sp, (side,), look_up(table, level) + (far + get(coef, (4,), base)), base)

        def strip_linear(ref, base, outer):
            c = tile_of(ref, (side,), base)
            xp, xm = x_pair(ref, (side,), base, outer, end)
            yp, ym, zp, zm = [[roll(c[i], s, 1) for i in range(2)] for s in (-1, 1, -WIDE, WIDE)]
            cy = [get(coef, (i,), base) for i in (0, 1)]
            return c, linear(c, xp, xm, yp, ym, zp, zm, cy, cy, cx, 0.5 * LAP, 0.5 * LAP)

        def keep(values, outer):
            good = (ok & row_ok) if outer else ok
            return [jnp.where(good, s, 0.0) for s in values]

        def strip_one(base, outer):
            c, lin = strip_linear(sw, base, outer)
            slope = first_slope(c, lin, get(sp, (side,), base))
            put_field(sk, (side,), keep(slope, outer), base, outer, end)
            put_field(sl, (side,), lin, base, False, end)

        def strip_two(base, outer):
            c, lin = strip_linear(sk, base, outer)
            field, here = tile_of(sw, (side,), base), get(sp, (side,), base)
            parts = powers(field, c, tile_of(sl, (side,), base), here)
            z, rest = second_stage(field, parts, lin, here, not outer)
            put_field(sz, (side,), keep(z, outer), base, outer, end)
            if rest is not None:
                put_field(sl, (side,), rest, base, False, end)

        for stage in (strip_load, strip_one, strip_two):
            for j in range(tiles + 1):
                stage(j * ROWS, j == 0)

    def out_copy(p):
        return pltpu.make_async_copy(result.at[:, p], out.at[:, p], osem.at[p])

    for side in range(at.sides):
        ys = at.ycoord(off + at.pick(side, -DEEP, cols - 2 * DEEP))
        cx = factors(SPIN * ys, LAP, 1.0)
        for j in range(1, tiles + 1):
            base = j * ROWS
            c = tile_of(sz, (side,), base)
            xp, xm = x_pair(sz, (side,), base, False, end)
            yp, ym, zp, zm = [[roll(c[i], s, 1) for i in range(2)] for s in (-1, 1, -WIDE, WIDE)]
            cy = [get(coef, (i,), base) for i in (2, 3)]
            lin = linear(c, xp, xm, yp, ym, zp, zm, cy, cy, cx, LAP, LAP)
            put_field(sk, (side,), [get(sl, (i, side), base) + lin[i] for i in range(2)], base, False, end)

    for p in range(at.share):
        from_lane = DEEP + WIDE * (p + DEEP)
        for j in range(tiles):
            for i in range(2):
                value = get(part, (i, p), j * ROWS)
                for side in range(at.sides):
                    shift = (at.pick(side, 0, cols - DEEP) + 2 * LANES - from_lane) % LANES
                    face = at.pick(side, lane, cols - 1 - lane) < DEEP
                    value = jnp.where(face, roll(get(sk, (i, side), (j + 1) * ROWS), shift, 1), value)
                put(result, (i, p), value, j * ROWS)
        out_copy(p).start()
    for p in range(at.share):
        out_copy(p).wait()


def local(npx, npy, psi, disorder):
    planes, rows, cols = psi.shape[1:]
    share = planes // lax.axis_size("section")
    two = npy == 2
    sides = 1 if two else 2
    slots = share + 2 * DEEP
    tall = rows + ROWS
    dims = (planes, share, rows, cols, npx, npy)
    hbm = pl.BlockSpec(memory_space=pltpu.HBM)
    vmem = pl.BlockSpec(memory_space=pltpu.VMEM)
    f32 = lambda *shape: jax.ShapeDtypeStruct(shape, F32)
    scratch = lambda *shape: pltpu.VMEM(shape, F32)
    levels = lambda *shape: pltpu.VMEM(shape, jnp.int32)
    dma = lambda *shape: pltpu.SemaphoreType.DMA(shape)

    def call(kernel, name, room, ins, outs, out_specs, scratches, flops, moved, *args, aliases={}):
        return pl.pallas_call(
            functools.partial(kernel, dims),
            out_shape=outs,
            in_specs=ins,
            out_specs=out_specs,
            scratch_shapes=scratches,
            input_output_aliases=aliases,
            compiler_params=pltpu.CompilerParams(vmem_limit_bytes=room * 1024 * 1024),
            cost_estimate=pl.CostEstimate(flops=flops, bytes_accessed=moved, transcendentals=0),
            name=name,
        )(*args)

    def send(value, pairs):
        return lax.ppermute(value, ("px", "py"), pairs)

    sections = lax.axis_size("section")
    place = lambda s, i, j: (s * npx + i) * npy + j
    row_pairs = []
    for s in range(sections):
        for i in range(npx):
            partner = i ^ 1 if s % 2 == 0 else ((i + 1) ^ 1) - 1
            for j in range(npy):
                to = (partner, j) if 0 <= partner < npx else (i, j ^ 1)
                if to[1] < npy:
                    row_pairs.append((place(s, i, j), place(s, *to)))
    core_pairs = [(s, s ^ 1) for s in range(sections)]

    cells = share * rows * cols
    block = 4 * slots * rows * cols
    pair_planes = 2 * share + 2 * DEEP - 2
    edges = call(
        rows_kernel, "pack_rows", 52, [hbm] * 2, f32(pair_planes, ROWS, LANES), vmem,
        [scratch(2, pair_planes, ROWS, LANES), levels(pair_planes, ROWS, LANES), dma(2, 2), dma(2)],
        cells // 16, block // 8, psi, disorder,
    )
    edges = lax.ppermute(edges, ("section", "px", "py"), row_pairs)

    packed = call(
        columns_kernel, "pack_columns", 24, [vmem] * 2,
        [f32(slots - 2, rows, cols)] + [f32(3, rows, LANES)] * sides + [f32(rows, LANES)] * sides,
        [vmem] * (1 + 2 * sides), [], 12 * cells, 3 * block, psi, disorder,
    )
    edges, packed = lax.optimization_barrier((edges, packed))
    pot = packed[0]
    own, message = packed[1 : 1 + sides], packed[1 + sides :]
    others = lax.ppermute(edges, "section", core_pairs)
    field = lambda depth: (2, depth, tall + ROWS, LANES)
    begun = call(
        slopes_kernel, "slopes", 24, [vmem] * 2,
        [f32(*field(n)) for n in (slots, slots - 2, slots - 2)] + [f32(8, AHEAD, rows - 2 * ROWS, LANES)], [vmem] * 4,
        [scratch(4, tall, LANES)], 60 * cells, 4 * block, psi, pot,
    )
    others, begun = lax.optimization_barrier((others, begun))

    made = call(
        corner_kernel, "pack_corners", 24, [vmem] * (2 + sides), [f32(3, ROWS, LANES)] * sides + [f32(tall, LANES)] * sides,
        [vmem] * (2 * sides), [], cells // 8, block // 16, edges, others, *message,
    )
    outer, message = made[:sides], made[sides:]
    right = [(i * npy + j, i * npy + j + 1) for i in range(npx) for j in range(npy - 1)]
    left = [(b, a) for a, b in right]
    if two:
        got = [send(message[0], right + left)]
    else:
        got = [send(message[1], right), send(message[0], left)]

    part = call(
        step_kernel, "step", 24, [vmem] * 7,
        [f32(2, share, rows, cols)] + [f32(*field(n)) for n in (slots, slots - 2, slots - 2)], [vmem] * 4,
        [scratch(slots - 2, ROWS, LANES), scratch(*field(slots - 4)), scratch(8, tall, LANES)],
        240 * cells, 4 * block, pot, edges, others, begun[3], *begun[:3], aliases={4: 1, 5: 2, 6: 3},
    )[0]
    return call(
        strip_kernel, "strips", 24, [vmem] * (1 + 3 * sides), f32(2, share, rows, cols), hbm,
        [
            scratch(2, share, rows, cols),
            scratch(*field(sides)),
            scratch(*field(sides)),
            scratch(*field(sides)),
            scratch(sides, tall, LANES),
            scratch(*field(sides)),
            scratch(5, tall, LANES),
            dma(share),
        ],
        30 * cells, 2 * block, part, *own, *outer, *got,
    )


def solution(mesh):
    in_specs = (P(None, None, "px", "py"), P(None, "px", "py"))
    out_specs = P(None, "section", "px", "py")
    run = functools.partial(local, mesh.shape["px"], mesh.shape["py"])
    return jax.shard_map(run, mesh=mesh, in_specs=in_specs, out_specs=out_specs, check_vma=False)
```

```python
import functools
import math

import jax
import jax.numpy as jnp
from jax import lax
from jax.experimental import pallas as pl
from jax.experimental.pallas import tpu as pltpu
from jax.sharding import PartitionSpec as P

LEVELS = 16
STEP = 0.05
ROTATION = 0.8
COUPLING = 0.25

ROOT_OUT = math.sqrt((3.0 + 2.0 * math.sqrt(1.2)) / 7.0)
ROOT_IN = math.sqrt((3.0 - 2.0 * math.sqrt(1.2)) / 7.0)
WEIGHT_OUT = (18.0 - math.sqrt(30.0)) / 36.0
WEIGHT_IN = 1.0 - WEIGHT_OUT

LAP = 0.5 * STEP
SPIN = 0.5 * STEP * ROTATION
KAPPA = 0.5 * STEP * COUPLING

DEEP = 3
WIDE = 3 * DEEP
LANES = 128
ROWS = 8
AHEAD = 6
F32 = jnp.float32


def iota(dim):
    return lax.broadcasted_iota(jnp.int32, (ROWS, LANES), dim)


def roll(value, shift, axis):
    return pltpu.roll(value, shift % value.shape[axis] if isinstance(shift, int) else shift, axis)


def strip_lanes():
    lane = iota(1)
    slot = (lane * 57) >> 9
    return slot, lane - WIDE * slot


def level_table():
    lane = iota(1)
    table = jnp.zeros((ROWS, LANES), F32)
    for level in range(LEVELS):
        table = jnp.where(lane == level, F32(0.75 * STEP * math.sin(2.3 * level + 0.4)), table)
    return table


def look_up(table, level):
    return jnp.take_along_axis(table, level, axis=1, mode="promise_in_bounds")


def to_level(value):
    return jnp.clip(value, 0.0, LEVELS - 1.0).astype(jnp.int32)


def factors(spin, lap, scale):
    return scale * (spin + lap), scale * (spin - lap)


def linear(c, xp, xm, yp, ym, zp, zm, cyp, cym, cx, lap, lap_z):
    diag = [lap_z * (zp[i] + zm[i]) - (6.0 * lap) * c[i] for i in range(2)]
    real = cyp[1] * yp[0] - cym[0] * ym[0] - cx[0] * xp[0] + cx[1] * xm[0] - diag[0]
    imag = cyp[0] * yp[1] - cym[1] * ym[1] - cx[1] * xp[1] + cx[0] * xm[1] + diag[1]
    return real, imag


def first_slope(w, lin, pot):
    g = pot + KAPPA * (w[0] * w[0] + w[1] * w[1])
    return lin[0] + g * w[1], lin[1] - g * w[0]


def powers(w, k, lin_w, pot):
    m = [w[i] + k[i] for i in range(2)]
    p0 = pot + KAPPA * (m[0] * m[0] + m[1] * m[1])
    p1 = (2.0 * KAPPA) * (m[0] * k[0] + m[1] * k[1])
    p2 = KAPPA * (k[0] * k[0] + k[1] * k[1])
    return (
        lin_w[0] + p0 * m[1],
        lin_w[1] - p0 * m[0],
        p0 * k[1] + p1 * m[1],
        p0 * k[0] + p1 * m[0],
        p1 * k[1] + p2 * m[1],
        p1 * k[0] + p2 * m[0],
        p2 * k[1],
        p2 * k[0],
    )


def second_stage(w, parts, lin_k, pot, full):
    f0 = parts[0] + lin_k[0], parts[1] + lin_k[1]
    f1 = lin_k[0] + parts[2], lin_k[1] - parts[3]
    f2, f3 = parts[4:6], parts[6:8]
    sign = 1.0, -1.0
    base = [w[i] + f0[i] + (sign[i] / 3.0) * f2[i] for i in range(2)]
    z = [base[i] - (1.0 / 3.0) * f1[i] - (sign[i] / 5.0) * f3[i] for i in range(2)]
    if not full:
        return z, None
    square = ROOT_OUT * ROOT_OUT
    even_out = [
        base[i] + (0.5 * (square - 1.0)) * f1[i] + (sign[i] * 0.25 * (square * square - 1.0)) * f3[i] for i in range(2)
    ]
    even_in = [z[i] + (WEIGHT_OUT / WEIGHT_IN) * (z[i] - even_out[i]) for i in range(2)]
    total = [(pot + pot) * z[i] for i in range(2)]
    for even, square, weight in (
        (even_out, ROOT_OUT * ROOT_OUT, WEIGHT_OUT),
        (even_in, ROOT_IN * ROOT_IN, WEIGHT_IN),
    ):
        odd = [f0[i] + (sign[i] * square / 3.0) * f2[i] for i in range(2)]
        scale = 2.0 * KAPPA * weight
        p = scale * (even[0] * even[0] + even[1] * even[1]) + (scale * square) * (odd[0] * odd[0] + odd[1] * odd[1])
        q = (2.0 * scale * square) * (even[0] * odd[0] + even[1] * odd[1])
        total = [total[i] + p * even[i] + q * odd[i] for i in range(2)]
    return z, (w[0] + total[1], w[1] - total[0])


class Place:
    def __init__(self, dims):
        self.planes, self.share, self.rows, self.cols, self.npx, self.npy = dims
        self.slots = self.share + 2 * DEEP
        self.tiles = self.rows // ROWS
        self.two = self.npy == 2
        self.sides = 1 if self.two else 2
        self.z0 = lax.axis_index("section") * self.share - DEEP
        self.px = lax.axis_index("px")
        self.py = lax.axis_index("py")
        self.core = lax.axis_index("section") % 2
        self.sends_up = (self.px + self.core) % 2 == 0
        self.pair_planes = 2 * self.share + 2 * DEEP - 2

    def valid(self, p):
        return (self.z0 + p >= 0) & (self.z0 + p < self.planes)

    def outer_row(self, sub):
        return jnp.where(sub >= 4, sub - ROWS, self.rows + sub)

    def on_grid(self, row):
        row = self.px * self.rows + row
        return (row >= 0) & (row < self.rows * self.npx)

    def plane(self, p):
        return jnp.clip(self.z0 + p, 0, self.planes - 1)

    def is_left(self, side):
        return self.py == 1 if self.two else side == 0

    def pick(self, side, left, right):
        if self.two:
            return jnp.where(self.py == 1, left, right)
        return left if side == 0 else right

    def coordinate(self, index, count):
        return (index.astype(F32) - (count - 1) / 2.0) / (count / 2.0)

    def xcoord(self, row):
        return self.coordinate(self.px * self.rows + row, self.rows * self.npx)

    def ycoord(self, col):
        return self.coordinate(self.py * self.cols + col, self.cols * self.npy)

    def zcoord(self, slot):
        return self.coordinate(self.z0 + slot, self.planes)


def unpack_rows(at, p, got, other):
    sub = iota(0)
    index = p - 1 + at.core * at.share
    got, other = got[index], other[index]
    up = jnp.where(at.sends_up, other, got)
    dn = jnp.where(at.sends_up, got, other)
    upper = sub >= 4
    ok = at.on_grid(at.outer_row(sub))
    a = jnp.where(ok, jnp.where(upper, up, dn), 0.0)
    b = jnp.where(ok, jnp.where(upper, roll(up, 3, 0), roll(dn, -3, 0)), 0.0)
    level = jnp.where(upper, roll(up, -2, 0), roll(dn, 2, 0))
    return a, b, level


def rows_kernel(dims, psi, dis, message, vpsi, vdis, psem, dsem):
    at = Place(dims)
    start = at.z0 - at.core * at.share + 1
    window = jnp.clip(start, 0, at.planes - at.pair_planes)
    edge = pl.ds(pl.multiple_of(jnp.where(at.sends_up, at.rows - ROWS, 0), ROWS), ROWS)
    span = pl.ds(window, at.pair_planes)
    copies = []
    half = at.pair_planes // 2
    for h in range(2):
        span, to = pl.ds(window + h * half, half), pl.ds(h * half, half)
        for i in range(2):
            copies.append(pltpu.make_async_copy(psi.at[i, span, edge], vpsi.at[i, to], psem.at[h, i]))
        copies.append(pltpu.make_async_copy(dis.at[span, edge], vdis.at[to], dsem.at[h]))
    for copy in copies:
        copy.start()
    sub = iota(0)
    place = jnp.where(at.sends_up, ROWS - 1 - sub, sub)
    shift_b = jnp.where(at.sends_up, ROWS - 3, 3)
    shift_d = jnp.where(at.sends_up, 2, ROWS - 2)
    for copy in copies:
        copy.wait()
    for t in range(at.pair_planes):
        z = start + t
        index = jnp.clip(z - window, 0, at.pair_planes - 1)
        a, b, level = vpsi[0, index], vpsi[1, index], vdis[index].astype(F32)
        value = jnp.where(place < 3, a, jnp.where(place < 6, roll(b, shift_b, 0), roll(level, shift_d, 0)))
        message[t] = jnp.where((z >= 0) & (z < at.planes), value, 0.0)


def columns_kernel(dims, psi, dis, pot, *refs):
    at = Place(dims)
    own, message = refs[: at.sides], refs[at.sides :]
    slot, off = strip_lanes()
    sub = iota(0)
    table = level_table()
    ys = at.ycoord(iota(1))
    here = [slot == jnp.where(at.valid(p), p, -1) for p in range(at.slots)]
    level_at = [table + (0.5 * STEP) * (at.zcoord(p) * at.zcoord(p)) for p in range(at.slots)]
    for j in range(at.tiles):
        rows = slice(j * ROWS, (j + 1) * ROWS)
        xs = at.xcoord(sub + j * ROWS)
        dist = (0.5 * STEP) * (xs * xs + ys * ys)
        for p in range(1, at.slots - 1):
            pot[p - 1, rows, :] = look_up(level_at[p], dis[at.plane(p), rows, :]) + dist
        for side in range(at.sides):
            shift = at.pick(side, DEEP, LANES - at.cols + 2 * DEEP)
            back = at.pick(side, DEEP, LANES - DEEP)
            strips = []
            for i in range(3):
                acc = jnp.zeros((ROWS, LANES), F32)
                for p in range(at.slots):
                    if i == 2 and p in (0, at.slots - 1):
                        continue
                    z = at.plane(p)
                    value = psi[i, z, rows, :] if i < 2 else dis[z, rows, :].astype(F32)
                    acc = jnp.where(here[p], roll(value, shift + WIDE * p, 1), acc)
                own[side][i, rows, :] = acc
                strips.append(acc)
            message[side][rows, :] = strip_message(at, side, off, back, *strips)


def strip_message(at, side, off, back, a, b, level):
    a, level = roll(a, back, 1), roll(level, LANES - back, 1)
    place = at.pick(side, 8 - off, off)
    return jnp.where(place < DEEP, a, jnp.where(place < 2 * DEEP, b, level))


def corner_kernel(dims, got, other, *refs):
    at = Place(dims)
    message = refs[: at.sides]
    outer, whole = refs[at.sides : 2 * at.sides], refs[2 * at.sides :]
    slot, off = strip_lanes()
    tiles = [unpack_rows(at, p, got, other) for p in range(1, at.slots - 1)]
    for side in range(at.sides):
        shift = at.pick(side, DEEP, LANES - at.cols + 2 * DEEP)
        back = at.pick(side, DEEP, LANES - DEEP)
        strips = []
        for i in range(3):
            acc = jnp.zeros((ROWS, LANES), F32)
            for p in range(1, at.slots - 1):
                acc = jnp.where(slot == p, roll(tiles[p - 1][i], shift + WIDE * p, 1), acc)
            strips.append(acc)
            outer[side][i] = acc
        whole[side][: at.rows] = message[side][...]
        whole[side][at.rows :] = strip_message(at, side, off, back, *strips)


def put(ref, lead, value, base):
    ref[lead + (pl.ds(base, ROWS), slice(None))] = value


def get(ref, lead, base):
    return ref[lead + (pl.ds(base, ROWS), slice(None))]


def tile_of(ref, lead, base):
    return [get(ref, (i,) + lead, base) for i in range(2)]


def x_pair(ref, lead, base, outer, end):
    if outer:
        return tile_of(ref, lead, 1), tile_of(ref, lead, end - 1)
    return tile_of(ref, lead, base + 1), tile_of(ref, lead, base - 1)


def put_field(ref, lead, values, base, outer, end):
    for i in range(2):
        put(ref, (i,) + lead, values[i], base)
        if outer:
            put(ref, (i,) + lead, values[i], end)


class Stages:
    def __init__(self, at, w, k, lw, coef, scales):
        self.at, self.w, self.k, self.lw, self.coef = at, w, k, lw, coef
        self.end = ROWS + at.rows
        sub, lane = iota(0), iota(1)
        self.outer_row = at.outer_row(sub)
        self.row_ok = at.on_grid(self.outer_row)
        self.ys = at.ycoord(lane)
        self.cx = [factors(SPIN * self.ys, LAP, scale) for scale in scales]
        self.scales = scales
        has_next = jnp.where(lane < at.cols - 1, 1.0, 0.0)
        has_prev = jnp.where(lane > 0, 1.0, 0.0)
        for j in range(at.tiles + 1):
            xs = at.xcoord(self.outer_row if j == 0 else sub + (j - 1) * ROWS)
            here = slice(j * ROWS, (j + 1) * ROWS)
            for which, scale in enumerate(scales):
                for i, factor in enumerate(factors(SPIN * xs, LAP, scale)):
                    coef[4 * which + i, here] = factor * has_next
                    coef[4 * which + 2 + i, here] = factor * has_prev

    def linear(self, ref, q, base, outer, lap_z, which=0):
        c = tile_of(ref, (q,), base)
        xp, xm = x_pair(ref, (q,), base, outer, self.end)
        zp = tile_of(ref, (q + 1,), base)
        zm = tile_of(ref, (q - 1,), base)
        yp = [roll(c[i], -1, 1) for i in range(2)]
        ym = [roll(c[i], 1, 1) for i in range(2)]
        cyp = [get(self.coef, (4 * which + i,), base) for i in (0, 1)]
        cym = [get(self.coef, (4 * which + i,), base) for i in (2, 3)]
        lap = self.scales[which] * LAP
        return c, linear(c, xp, xm, yp, ym, zp, zm, cyp, cym, self.cx[which], lap, lap if lap_z is None else lap_z)

    def one(self, p, j, pot, lap_z):
        base, outer = j * ROWS, j == 0
        c, lin = self.linear(self.w, p, base, outer, lap_z)
        slope = first_slope(c, lin, pot)
        if outer:
            slope = [jnp.where(self.row_ok, s, 0.0) for s in slope]
        put_field(self.k, (p - 1,), slope, base, outer, self.end)
        put_field(self.lw, (p - 1,), lin, base, False, self.end)
        return c, slope, lin

    def lap_of(self, p):
        return jnp.where(self.at.valid(p), self.scales[0] * LAP, 0.0)


def slopes_kernel(dims, psi, pot, w, k, lw, ready, coef):
    at = Place(dims)
    stages = Stages(at, w, k, lw, coef, (0.5,))

    def fill(p):
        sure = DEEP <= p < at.slots - DEEP
        for j in range(1, at.tiles + 1):
            for i in range(2):
                value = psi[i, at.plane(p), (j - 1) * ROWS : j * ROWS, :]
                put(w, (i, p), value if sure else jnp.where(at.valid(p), value, 0.0), j * ROWS)

    fill(0)
    fill(1)
    for p in range(1, at.slots - 1):
        fill(p + 1)
        lap_p = stages.lap_of(p)
        for j in range(2, at.tiles):
            here = get(pot, (p - 1,), (j - 1) * ROWS)
            values = stages.one(p, j, here, lap_p)
            if DEEP <= p < DEEP + AHEAD:
                for i, part in enumerate(powers(*values, here)):
                    put(ready, (i, p - DEEP), part, (j - 2) * ROWS)


def step_kernel(dims, pot, got, other, ready, w_in, k_in, lw_in, part, w, k, lw, outer_pot, zf, coef):
    at = Place(dims)
    slots, tiles, rows = at.slots, at.tiles, at.rows
    stages = Stages(at, w, k, lw, coef, (0.5, 1.0))
    end, ys = stages.end, stages.ys
    table = level_table()

    zero = jnp.zeros((ROWS, LANES), F32)
    xs = at.xcoord(stages.outer_row)
    dist = (0.5 * STEP) * (xs * xs + ys * ys)
    for p in range(1, slots - 1):
        a, b, level = unpack_rows(at, p, got, other)
        put_field(w, (p,), (a, b), 0, True, end)
        zs = at.zcoord(p)
        outer_pot[p - 1] = look_up(table + (0.5 * STEP) * (zs * zs), to_level(level)) + dist
    for p in (0, slots - 1):
        put_field(w, (p,), (zero, zero), 0, True, end)

    def potential(p, j):
        return get(pot, (p - 1,), (j - 1) * ROWS) if j else outer_pot[p - 1]

    def two_tile(p, j, full, lap_z):
        base, outer = j * ROWS, j == 0
        c, lin = stages.linear(k, p - 1, base, outer, lap_z)
        here, field = potential(p, j), tile_of(w, (p,), base)
        if DEEP <= p < DEEP + AHEAD and 2 <= j < tiles:
            parts = [get(ready, (i, p - DEEP), (j - 2) * ROWS) for i in range(8)]
        else:
            parts = powers(field, c, tile_of(lw, (p - 1,), base), here)
        z, rest = second_stage(field, parts, lin, here, full and not outer)
        if outer:
            z = [jnp.where(stages.row_ok, s, 0.0) for s in z]
        put_field(zf, (p - 2,), z, base, outer, end)
        if rest is not None:
            for i in range(2):
                put(part, (i, p - DEEP), rest[i], base - ROWS)

    def three_tile(p, j):
        base = j * ROWS
        _, lin = stages.linear(zf, p - 2, base, False, None, 1)
        for i in range(2):
            lead = (i, p - DEEP)
            put(part, lead, get(part, lead, base - ROWS) + lin[i], base - ROWS)

    last = slots - 2
    for p in range(1, last + 1):
        two = None if p < DEEP else p not in (DEEP, last)
        lap_p = stages.lap_of(p)
        lap_before = None if two else stages.lap_of(p - 1)
        for j in range(tiles + 1):
            if j < 2 or j == tiles:
                stages.one(p, j, potential(p, j), lap_p)
            if two is not None:
                two_tile(p - 1, j, two, lap_before)
            if p > DEEP + 1 and j:
                three_tile(p - 2, j)


def strip_kernel(dims, part, *refs):
    at = Place(dims)
    own, outer_own, got = (refs[i * at.sides : (i + 1) * at.sides] for i in range(3))
    out, result, sw, sk, sl, sp, sz, coef, osem = refs[3 * at.sides :]
    tiles, rows, cols = at.tiles, at.rows, at.cols
    end = ROWS + rows
    sub = iota(0)
    lane = iota(1)
    slot, off = strip_lanes()
    table = level_table()
    outer_row = at.outer_row(sub)
    inside = lambda index, count: (index >= 0) & (index < count)
    row_ok = at.on_grid(outer_row)
    zs = at.zcoord(slot)

    for j in range(tiles + 1):
        xs = at.xcoord(outer_row if j == 0 else sub + (j - 1) * ROWS)
        here = slice(j * ROWS, (j + 1) * ROWS)
        coef[0, here], coef[1, here] = factors(SPIN * xs, LAP, 0.5)
        coef[2, here], coef[3, here] = factors(SPIN * xs, LAP, 1.0)
        coef[4, here] = (0.5 * STEP) * (xs * xs)

    for side in range(at.sides):
        col = off + at.pick(side, -DEEP, cols - 2 * DEEP)
        ok = inside(at.z0 + slot, at.planes) & inside(at.py * cols + col, cols * at.npy)
        ys = at.ycoord(col)
        cx = factors(SPIN * ys, LAP, 0.5)
        far = (0.5 * STEP) * (zs * zs + ys * ys)
        halo = at.pick(side, off, 8 - off) < DEEP
        back_b = at.pick(side, LANES - DEEP, DEEP)
        back_d = at.pick(side, LANES - 2 * DEEP, 2 * DEEP)

        def strip_load(base, outer):
            if outer:
                new = got[side][rows:, :]
                mine = [outer_own[side][i] for i in range(3)]
            else:
                here = pl.ds(base - ROWS, ROWS)
                new = got[side][here, :]
                mine = [own[side][i, here, :] for i in range(3)]
            a = jnp.where(halo, new, mine[0])
            b = jnp.where(halo, roll(new, back_b, 1), mine[1])
            level = to_level(jnp.where(halo, roll(new, back_d, 1), mine[2]))
            put_field(sw, (side,), (a, b), base, outer, end)
            put(sp, (side,), look_up(table, level) + (far + get(coef, (4,), base)), base)

        def strip_linear(ref, base, outer):
            c = tile_of(ref, (side,), base)
            xp, xm = x_pair(ref, (side,), base, outer, end)
            yp, ym, zp, zm = [[roll(c[i], s, 1) for i in range(2)] for s in (-1, 1, -WIDE, WIDE)]
            cy = [get(coef, (i,), base) for i in (0, 1)]
            return c, linear(c, xp, xm, yp, ym, zp, zm, cy, cy, cx, 0.5 * LAP, 0.5 * LAP)

        def keep(values, outer):
            good = (ok & row_ok) if outer else ok
            return [jnp.where(good, s, 0.0) for s in values]

        def strip_one(base, outer):
            c, lin = strip_linear(sw, base, outer)
            slope = first_slope(c, lin, get(sp, (side,), base))
            put_field(sk, (side,), keep(slope, outer), base, outer, end)
            put_field(sl, (side,), lin, base, False, end)

        def strip_two(base, outer):
            c, lin = strip_linear(sk, base, outer)
            field, here = tile_of(sw, (side,), base), get(sp, (side,), base)
            parts = powers(field, c, tile_of(sl, (side,), base), here)
            z, rest = second_stage(field, parts, lin, here, not outer)
            put_field(sz, (side,), keep(z, outer), base, outer, end)
            if rest is not None:
                put_field(sl, (side,), rest, base, False, end)

        for stage in (strip_load, strip_one, strip_two):
            for j in range(tiles + 1):
                stage(j * ROWS, j == 0)

    def out_copy(p):
        return pltpu.make_async_copy(result.at[:, p], out.at[:, p], osem.at[p])

    for side in range(at.sides):
        ys = at.ycoord(off + at.pick(side, -DEEP, cols - 2 * DEEP))
        cx = factors(SPIN * ys, LAP, 1.0)
        for j in range(1, tiles + 1):
            base = j * ROWS
            c = tile_of(sz, (side,), base)
            xp, xm = x_pair(sz, (side,), base, False, end)
            yp, ym, zp, zm = [[roll(c[i], s, 1) for i in range(2)] for s in (-1, 1, -WIDE, WIDE)]
            cy = [get(coef, (i,), base) for i in (2, 3)]
            lin = linear(c, xp, xm, yp, ym, zp, zm, cy, cy, cx, LAP, LAP)
            put_field(sk, (side,), [get(sl, (i, side), base) + lin[i] for i in range(2)], base, False, end)

    for p in range(at.share):
        from_lane = DEEP + WIDE * (p + DEEP)
        for j in range(tiles):
            for i in range(2):
                value = get(part, (i, p), j * ROWS)
                for side in range(at.sides):
                    shift = (at.pick(side, 0, cols - DEEP) + 2 * LANES - from_lane) % LANES
                    face = at.pick(side, lane, cols - 1 - lane) < DEEP
                    value = jnp.where(face, roll(get(sk, (i, side), (j + 1) * ROWS), shift, 1), value)
                put(result, (i, p), value, j * ROWS)
        out_copy(p).start()
    for p in range(at.share):
        out_copy(p).wait()


def local(npx, npy, psi, disorder):
    planes, rows, cols = psi.shape[1:]
    share = planes // lax.axis_size("section")
    two = npy == 2
    sides = 1 if two else 2
    slots = share + 2 * DEEP
    tall = rows + ROWS
    dims = (planes, share, rows, cols, npx, npy)
    hbm = pl.BlockSpec(memory_space=pltpu.HBM)
    vmem = pl.BlockSpec(memory_space=pltpu.VMEM)
    f32 = lambda *shape: jax.ShapeDtypeStruct(shape, F32)
    scratch = lambda *shape: pltpu.VMEM(shape, F32)
    levels = lambda *shape: pltpu.VMEM(shape, jnp.int32)
    dma = lambda *shape: pltpu.SemaphoreType.DMA(shape)

    def call(kernel, name, room, ins, outs, out_specs, scratches, flops, moved, *args, aliases={}):
        return pl.pallas_call(
            functools.partial(kernel, dims),
            out_shape=outs,
            in_specs=ins,
            out_specs=out_specs,
            scratch_shapes=scratches,
            input_output_aliases=aliases,
            compiler_params=pltpu.CompilerParams(vmem_limit_bytes=room * 1024 * 1024),
            cost_estimate=pl.CostEstimate(flops=flops, bytes_accessed=moved, transcendentals=0),
            name=name,
        )(*args)

    def send(value, pairs):
        return lax.ppermute(value, ("px", "py"), pairs)

    sections = lax.axis_size("section")
    place = lambda s, i, j: (s * npx + i) * npy + j
    row_pairs = []
    for s in range(sections):
        for i in range(npx):
            partner = i ^ 1 if s % 2 == 0 else ((i + 1) ^ 1) - 1
            for j in range(npy):
                to = (partner, j) if 0 <= partner < npx else (i, j ^ 1)
                if to[1] < npy:
                    row_pairs.append((place(s, i, j), place(s, *to)))
    core_pairs = [(s, s ^ 1) for s in range(sections)]

    cells = share * rows * cols
    block = 4 * slots * rows * cols
    pair_planes = 2 * share + 2 * DEEP - 2
    edges = call(
        rows_kernel, "pack_rows", 52, [hbm] * 2, f32(pair_planes, ROWS, LANES), vmem,
        [scratch(2, pair_planes, ROWS, LANES), levels(pair_planes, ROWS, LANES), dma(2, 2), dma(2)],
        cells // 16, block // 8, psi, disorder,
    )
    edges = lax.ppermute(edges, ("section", "px", "py"), row_pairs)

    packed = call(
        columns_kernel, "pack_columns", 24, [vmem] * 2,
        [f32(slots - 2, rows, cols)] + [f32(3, rows, LANES)] * sides + [f32(rows, LANES)] * sides,
        [vmem] * (1 + 2 * sides), [], 12 * cells, 3 * block, psi, disorder,
    )
    edges, packed = lax.optimization_barrier((edges, packed))
    pot = packed[0]
    own, message = packed[1 : 1 + sides], packed[1 + sides :]
    others = lax.ppermute(edges, "section", core_pairs)
    field = lambda depth: (2, depth, tall + ROWS, LANES)
    begun = call(
        slopes_kernel, "slopes", 24, [vmem] * 2,
        [f32(*field(n)) for n in (slots, slots - 2, slots - 2)] + [f32(8, AHEAD, rows - 2 * ROWS, LANES)], [vmem] * 4,
        [scratch(4, tall, LANES)], 60 * cells, 4 * block, psi, pot,
    )
    others, begun = lax.optimization_barrier((others, begun))

    made = call(
        corner_kernel, "pack_corners", 24, [vmem] * (2 + sides), [f32(3, ROWS, LANES)] * sides + [f32(tall, LANES)] * sides,
        [vmem] * (2 * sides), [], cells // 8, block // 16, edges, others, *message,
    )
    outer, message = made[:sides], made[sides:]
    right = [(i * npy + j, i * npy + j + 1) for i in range(npx) for j in range(npy - 1)]
    left = [(b, a) for a, b in right]
    if two:
        got = [send(message[0], right + left)]
    else:
        got = [send(message[1], right), send(message[0], left)]

    part = call(
        step_kernel, "step", 24, [vmem] * 7,
        [f32(2, share, rows, cols)] + [f32(*field(n)) for n in (slots, slots - 2, slots - 2)], [vmem] * 4,
        [scratch(slots - 2, ROWS, LANES), scratch(*field(slots - 4)), scratch(8, tall, LANES)],
        240 * cells, 4 * block, pot, edges, others, begun[3], *begun[:3], aliases={4: 1, 5: 2, 6: 3},
    )[0]
    return call(
        strip_kernel, "strips", 24, [vmem] * (1 + 3 * sides), f32(2, share, rows, cols), hbm,
        [
            scratch(2, share, rows, cols),
            scratch(*field(sides)),
            scratch(*field(sides)),
            scratch(*field(sides)),
            scratch(sides, tall, LANES),
            scratch(*field(sides)),
            scratch(5, tall, LANES),
            dma(share),
        ],
        30 * cells, 2 * block, part, *own, *outer, *got,
    )


def solution(mesh):
    in_specs = (P(None, None, "px", "py"), P(None, "px", "py"))
    out_specs = P(None, "section", "px", "py")
    run = functools.partial(local, mesh.shape["px"], mesh.shape["py"])
    return jax.shard_map(run, mesh=mesh, in_specs=in_specs, out_specs=out_specs, check_vma=False)
```
